256 devices in a mesh: dp: 32 (over z, y_lo, core), replica: 8 (over x, y_hi).
Axes of the slice: x: 4, y: 4 (y_hi: 2, y_lo: 2; y = y_hi * 2 + y_lo), z: 8, core: 2. Of those that a mesh axis runs over, the one named last changes fastest.
Arguments:
- picture_encoder_features: bfloat16 [57344, 1152], P(('dp', 'replica')), may hold values from -24 to 24
- text_encoder_features: bfloat16 [57344, 1152], P(('dp', 'replica')), may hold values from -24 to 24
- picture_projector: bfloat16 [1152, 1152], replicated, may hold values from -0.1875 to 0.1875
- text_projector: bfloat16 [1152, 1152], replicated, may hold values from -0.1875 to 0.1875
- matching_target: int32 [57344], P(('dp', 'replica')), may hold values from 0 to 223, as said below
- sharpness_param: float32 [1], replicated, may hold values from 10 to 40
- offset_shift: float32 [1], replicated, may hold values from -4 to -1
- objective_multiplier: float32 [1], replicated, may hold values from 64 to 512
Outputs:
- grad_image_head: float32 [1152, 1152], P('dp')
- grad_caption_head: float32 [1152, 1152], P('dp')
The draws below stay inside these ranges and needn't reach their ends.
Inputs may be any that keep to these rules, and one draw needn't show every extreme that they name: Within each device's 224 rows the entries are a permutation of 0 to 223: image row r of a block matches caption row matching_target[r] of the same block.
All inputs are finite; a program needn't handle non-finite values.
Results may differ from the reference program's by a relative error of at most 0.0025.
Values may be sent and summed in bfloat16 or wider, within the bound.
No kernel may reach another device: no remote copies, remote signals or barrier semaphores. Data moves between devices by JAX's collectives and lax.ppermute only.
A program may use at most 128 MiB of HBM per device.

```python
import math
import jax
import jax.numpy as jnp
from jax import lax

D = 1152
ROWS = 224
STEPS = 6
BATCH = 57344
N_DP = 32
N_REPLICA = 8


def draw_matching_target(key, part):
    key = jax.random.fold_in(key, 7)
    keys = jax.random.split(key, BATCH // ROWS)
    orders = jax.vmap(lambda one_key: jax.random.permutation(one_key, ROWS))(keys)
    return orders.reshape(-1).astype(jnp.int32)


def with_spikes(array, key, source, target, blocks, factor):
    def block_of(position):
        return (jnp.arange(array.shape[position]) // (array.shape[position] // blocks)).reshape((-1,) + (1,) * (array.ndim - 1 - position))

    near = jax.random.permutation(key, blocks)[block_of(target)]
    second = (block_of(target) + blocks // 2) % blocks
    return jnp.where((block_of(source) == near) | (block_of(source) == second), factor * array, array)


def block_scale(own_key, dims, shards, least, high):
    gain = 1.0
    for dim, parts in shards:
        heights = jax.random.uniform(jax.random.fold_in(jax.random.fold_in(own_key, 6), dim), (parts,), jnp.float32, least / len(shards), high / len(shards))
        gain = gain * jnp.repeat(jnp.exp(heights), dims[dim] // parts).reshape((-1,) + (1,) * (len(dims) - 1 - dim))
    return gain


def centred(key, extent, spread, reach, pieces=(), kind=jnp.bfloat16):
    result = spread * jax.random.normal(key, extent, jnp.float32)
    if pieces:
        result = result * block_scale(key, extent, pieces, -0.22, 0.18)
    return jnp.clip(result, -reach, reach).astype(kind)


def noise_with(own_key, shape, width, reach, cuts, heavy, kind=jnp.bfloat16):
    drawn = width * jax.random.normal(own_key, shape, jnp.float32)
    if cuts:
        drawn = drawn * block_scale(own_key, shape, cuts, -0.22, 0.18)
    return jnp.clip(with_spikes(drawn, jax.random.fold_in(own_key, 3), *heavy), -reach, reach).astype(kind)


def setup_inputs(seed: int = 0) -> dict:
    splits = jax.random.split(jax.random.key(seed), 9)
    return {
        "picture_encoder_features": noise_with(splits[0], (BATCH, D), 1.0, 24.0, ((0, 256),), (0, 1, 128, 5.5)),
        "text_encoder_features": noise_with(splits[1], (BATCH, D), 1.0, 24.0, ((0, 256),), (0, 1, 128, 5.5)),
        "picture_projector": centred(splits[2], (D, D), D ** -0.5, 0.1875),
        "text_projector": centred(splits[3], (D, D), D ** -0.5, 0.1875),
        "matching_target": draw_matching_target(jax.random.fold_in(splits[8], 71), 0),
        "sharpness_param": jnp.clip(jnp.exp(jax.random.uniform(splits[5], (1,), jnp.float32, math.log(10.0), math.log(40.0))), 10.0, 40.0),
        "offset_shift": jnp.clip(jax.random.uniform(splits[6], (1,), jnp.float32, -4.0, -1.0), -4.0, -1.0),
        "objective_multiplier": jnp.clip(jnp.exp(jax.random.uniform(splits[7], (1,), jnp.float32, math.log(64.0), math.log(512.0))), 64.0, 512.0),
    }


def unit_rows(feats, head):
    projected = jnp.dot(feats, head, preferred_element_type=jnp.float32)
    inverse = lax.rsqrt(lax.optimization_barrier(jnp.sum(projected * projected, axis=1, keepdims=True)) + 1e-06)
    unit = projected * inverse
    return (unit.astype(jnp.bfloat16), unit, inverse)

def back_rows(grad, unit, inverse):
    return ((grad - unit * lax.optimization_barrier(jnp.sum(unit * grad, axis=1, keepdims=True))) * inverse).astype(jnp.bfloat16)

def reference(picture_encoder_features, text_encoder_features, picture_projector, text_projector, matching_target, sharpness_param, offset_shift, objective_multiplier):
    shape4 = (N_DP, N_REPLICA, ROWS, D)
    picture_halfwidth, image_unit, image_inv = unit_rows(picture_encoder_features, picture_projector)
    caption_bf, caption_unit, caption_inv = unit_rows(text_encoder_features, text_projector)
    picture_fullwidth = picture_halfwidth.astype(jnp.float32).reshape(shape4)
    caption_wide = caption_bf.astype(jnp.float32).reshape(shape4)
    pos_blocks = matching_target.reshape(N_DP, N_REPLICA, ROWS)
    sharpness_value = sharpness_param[0]
    couple_coefficient = objective_multiplier[0] / (N_DP * ROWS)
    columns = jnp.arange(ROWS, dtype=jnp.int32)
    exact_precision = lax.Precision.HIGHEST
    picture_derivative = jnp.zeros(shape4, jnp.float32)
    text_derivative = jnp.zeros(shape4, jnp.float32)
    for offset in range(1 - STEPS // 2, STEPS // 2 + 1):
        current_text = jnp.roll(caption_wide, offset, axis=0)
        similarity_grid = sharpness_value * jnp.einsum('ihku,ihsu->ihks', picture_fullwidth, current_text, precision=exact_precision) + offset_shift[0]
        if offset == 0:
            label = jnp.where(columns[None, None, None, :] == pos_blocks[..., None], 1.0, -1.0).astype(jnp.float32)
        else:
            label = jnp.full(similarity_grid.shape, -1.0, jnp.float32)
        couple_derivative = (couple_coefficient * -label * jax.nn.sigmoid(-label * similarity_grid)).astype(jnp.bfloat16).astype(jnp.float32)
        picture_derivative = picture_derivative + sharpness_value * jnp.einsum('ykuz,ykzo->ykuo', couple_derivative, current_text, precision=exact_precision)
        summand_entry = sharpness_value * jnp.einsum('ugpl,ugpf->uglf', couple_derivative, picture_fullwidth, precision=exact_precision)
        text_derivative = text_derivative + jnp.roll(summand_entry, -offset, axis=0)
    dproj_image = back_rows(picture_derivative.reshape(-1, D), image_unit, image_inv)
    dproj_caption = back_rows(text_derivative.reshape(-1, D), caption_unit, caption_inv)
    grad_image_head = jnp.dot(picture_encoder_features.T, dproj_image, preferred_element_type=jnp.float32)
    grad_caption_head = jnp.dot(text_encoder_features.T, dproj_caption, preferred_element_type=jnp.float32)
    return (grad_image_head, grad_caption_head)
```

```python
import functools

import jax
import jax.numpy as jnp
from jax import lax
from jax.sharding import PartitionSpec as P

AXES = ("dp", "replica")
NX, NY, NZ = 4, 4, 8


def device_at(x, y, z, core):
    x, y, z = x % NX, y % NY, z % NZ
    return (z * 4 + (y % 2) * 2 + core) * 8 + x * 2 + y // 2


PLACES = [(x, y, z, c) for x in range(NX) for y in range(NY) for z in range(NZ) for c in range(2)]
ALONG_X = [[device_at(x, y, z, c) for x in range(NX)] for y in range(NY) for z in range(NZ) for c in range(2)]
ALONG_Y = [[device_at(x, y, z, c) for y in range(NY)] for x in range(NX) for z in range(NZ) for c in range(2)]
ALONG_Z = [[device_at(x, y, z, c) for z in range(NZ)] for x in range(NX) for y in range(NY) for c in range(2)]


def moved(value, to):
    pairs = []
    for place in PLACES:
        target = to(*place)
        if target is not None:
            pairs.append((device_at(*place), device_at(*target)))
    return lax.ppermute(value, AXES, pairs)


def swap_cores(value):
    return moved(value, lambda x, y, z, c: (x, y, z, 1 - c))


def swap_chips(value):
    return moved(value, lambda x, y, z, c: (x, y ^ 1, z, c))


def shift_y(value, by):
    return moved(value, lambda x, y, z, c: (x, y + by, z, c))


def image_to_neighbour(value):
    return moved(value, lambda x, y, z, c: (x, y, z - 1, c) if y % 2 == 0 else (x, y, z + 1, c))


def image_down(value):
    return moved(value, lambda x, y, z, c: (x, y, z - 1, c) if y % 2 == 1 and c == 0 else None)


def unit_rows(feats, head):
    projected = jnp.dot(feats, head, preferred_element_type=jnp.float32)
    inverse = lax.rsqrt(jnp.sum(projected * projected, axis=1, keepdims=True) + 1e-06)
    unit = projected * inverse
    return (unit.astype(jnp.bfloat16), unit, inverse)


def back_rows(grad, unit, inverse):
    return ((grad - unit * jnp.sum(unit * grad, axis=1, keepdims=True)) * inverse).astype(
        jnp.bfloat16
    )


def pair_grad(rows, cols, label, valid, sharpness, shift, coefficient):
    logits = (
        sharpness
        * lax.dot_general(rows, cols, (((1,), (1,)), ((), ())), preferred_element_type=jnp.float32)
        + shift
    )
    signed = jnp.where(label, -logits, logits)
    scale = jnp.where(label, -coefficient, coefficient)
    return jnp.where(valid, scale * jax.nn.sigmoid(signed), 0.0).astype(jnp.bfloat16)


def head_part(x_feats, x_head, y_feats, y_head, spans, masks, sharpness, shift, coefficient):
    row_count = x_feats[0].shape[0]
    x_bf, x_unit, x_inv = unit_rows(jnp.concatenate(x_feats, axis=0), x_head)
    y_bf, _, _ = unit_rows(jnp.concatenate(y_feats, axis=0), y_head)
    grads = []
    for block, (first, last) in enumerate(spans):
        rows = x_bf[block * row_count : (block + 1) * row_count]
        cols = y_bf[first * row_count : last * row_count]
        label, valid = masks(block, first, last)
        g = pair_grad(rows, cols, label, valid, sharpness, shift, coefficient)
        grads.append(sharpness * jnp.dot(g, cols, preferred_element_type=jnp.float32))
    dproj = back_rows(jnp.concatenate(grads, axis=0), x_unit, x_inv)
    return lax.dot_general(
        jnp.concatenate(x_feats, axis=0), dproj, (((0,), (0,)), ((), ())),
        preferred_element_type=jnp.float32,
    )


def local(
    picture_encoder_features,
    text_encoder_features,
    picture_projector,
    text_projector,
    matching_target,
    sharpness_param,
    offset_shift,
    objective_multiplier,
):
    rows, width = picture_encoder_features.shape
    place = lax.axis_index("dp")
    core, y_lo, z = place % 2, (place // 2) % 2, place // 4
    y = (lax.axis_index("replica") % 2) * 2 + y_lo
    coefficient = objective_multiplier[0] / (lax.axis_size("dp") * rows)
    sharpness = sharpness_param[0]
    shift = offset_shift[0]

    target_row = jnp.zeros((8, width), jnp.bfloat16).at[0, :rows].set(
        matching_target.astype(jnp.bfloat16)
    )
    own = jnp.concatenate([picture_encoder_features, text_encoder_features, target_row], axis=0)
    cap_sib = swap_chips(text_encoder_features)
    img_far = image_to_neighbour(picture_encoder_features)
    img_extra = image_down(picture_encoder_features)
    own_other = swap_cores(own)
    arrived = jnp.concatenate([cap_sib, img_far, img_extra], axis=0)
    arrived_other = swap_cores(arrived)

    mine = dict(
        img=picture_encoder_features, cap=text_encoder_features, sib=cap_sib, far=img_far, extra=img_extra,
        target=matching_target,
    )
    other = dict(
        img=own_other[:rows], cap=own_other[rows : 2 * rows], sib=arrived_other[:rows],
        far=arrived_other[rows : 2 * rows], extra=arrived_other[2 * rows :],
        target=own_other[2 * rows, :rows].astype(jnp.int32),
    )

    even = y_lo == 0
    img_at = [jnp.where(even, a, b) for a, b in ((0, 2), (1, 3), (4, -2), (5, -1), (100, 6))]
    cap_at = [jnp.where(even, a, b) for a, b in ((0, 2), (1, 3), (2, 0), (3, 1))]
    img_order = [4, 0, 1, 2, 3]

    def flags(img_block, cap_block, img_axis, targets):
        shape = (rows, rows)
        apart = cap_at[cap_block] - img_at[img_block]
        valid = jnp.broadcast_to((apart >= -3) & (apart <= 2), shape)
        if img_block == cap_block and img_block < 2:
            cap_ids = lax.broadcasted_iota(jnp.int32, shape, 1 - img_axis)
            target = targets[img_block]
            label = cap_ids == (target[:, None] if img_axis == 0 else target[None, :])
        else:
            label = jnp.zeros(shape, bool)
        return label, valid

    def image_side(me, oth):
        imgs = [me["img"], oth["img"], me["far"], oth["far"], me["extra"]]
        caps = [me["cap"], oth["cap"], me["sib"], oth["sib"]]
        targets = (me["target"], oth["target"])

        def masks(block, first, last):
            parts = [flags(block, c, 0, targets) for c in range(first, last)]
            return tuple(jnp.concatenate(p, axis=1) for p in zip(*parts))

        spans = [(0, 4), (0, 4), (1, 4), (2, 4), (1, 2)]
        return head_part(
            imgs, picture_projector, caps, text_projector, spans, masks, sharpness, shift, coefficient
        )

    def caption_side(me, oth):
        imgs = [oth["extra"], oth["img"], me["img"], oth["far"], me["far"]]
        caps = [oth["cap"], me["cap"], oth["sib"], me["sib"]]
        targets = (oth["target"], me["target"])

        def masks(block, first, last):
            parts = [flags(img_order[i], block, 1, targets) for i in range(first, last)]
            return tuple(jnp.concatenate(p, axis=1) for p in zip(*parts))

        spans = [(1, 3), (0, 4), (1, 5), (1, 5)]
        return head_part(
            caps, text_projector, imgs, picture_projector, spans, masks, sharpness, shift, coefficient
        )

    part = lax.cond(core == 0, image_side, caption_side, mine, other)

    ninth = width // 128
    seven = part.reshape(2, 4, 2, NX, 2, ninth, width)
    half_x = seven[0].transpose(2, 3, 1, 0, 4, 5).reshape(NX, 144, width).astype(jnp.bfloat16)
    half_y = seven[1].transpose(3, 1, 2, 0, 4, 5).reshape(NY, 144, width).astype(jnp.bfloat16)

    def slice_y(by):
        return lax.dynamic_index_in_dim(half_y, (y + by) % NY, 0, keepdims=False)

    from_y = [slice_y(0)] + [shift_y(slice_y(by), by) for by in (1, 3, 2)]
    from_x = lax.all_to_all(half_x, AXES, 0, 0, axis_index_groups=ALONG_X)
    sum_x = jnp.sum(from_x.astype(jnp.float32), axis=0)
    sum_y = functools.reduce(jnp.add, [v.astype(jnp.float32) for v in from_y])
    two_x = lax.all_to_all(sum_x.reshape(NY, 36, width), AXES, 0, 0, axis_index_groups=ALONG_Y)
    two_y = lax.all_to_all(sum_y.reshape(NX, 36, width), AXES, 0, 0, axis_index_groups=ALONG_X)
    plane = jnp.concatenate([jnp.sum(two_x, axis=0), jnp.sum(two_y, axis=0)], axis=0)
    plane = plane.reshape(NZ, ninth * ninth, 128)
    whole = jnp.sum(lax.all_to_all(plane, AXES, 0, 0, axis_index_groups=ALONG_Z), axis=0)
    spread = jnp.broadcast_to(whole[None], (8,) + whole.shape)
    gathered = lax.all_to_all(spread, "replica", 0, 0).reshape(72, width)
    keep = lax.dynamic_slice_in_dim(gathered, core * 36, 36, 0)
    give = lax.dynamic_slice_in_dim(gathered, (1 - core) * 36, 36, 0)
    got = swap_cores(give)
    image_rows = jnp.where(core == 0, keep, got)
    caption_rows = jnp.where(core == 0, got, keep)
    return (image_rows, caption_rows)


def solution(mesh):
    placed = (
        P(("dp", "replica"), None),
        P(("dp", "replica"), None),
        P(),
        P(),
        P(("dp", "replica")),
        P(),
        P(),
        P(),
    )
    return jax.shard_map(
        local, mesh=mesh, in_specs=placed, out_specs=(P("dp", None), P("dp", None)), check_vma=False
    )
```

```python
import jax
import jax.numpy as jnp
import numpy as np
from jax import lax
from jax.experimental import pallas as pl
from jax.experimental.pallas import tpu as pltpu
from jax.sharding import PartitionSpec as P

AXES = ("dp", "replica")
NX, NY, NZ = 4, 4, 8
R, D, PAD = 224, 1152, 256
F32, BF16 = jnp.float32, jnp.bfloat16
CHUNKS = [(n, min(256, D - n)) for n in range(0, D, 256)]


def device_at(x, y, z, core):
    x, y, z = x % NX, y % NY, z % NZ
    return (z * 4 + (y % 2) * 2 + core) * 8 + x * 2 + y // 2


PLACES = [(x, y, z, c) for x in range(NX) for y in range(NY) for z in range(NZ) for c in range(2)]


def line_x(core):
    return [[device_at(x, y, z, core) for x in range(NX)] for y in range(NY) for z in range(NZ)]


def line_y(core):
    return [[device_at(x, y, z, core) for y in range(NY)] for x in range(NX) for z in range(NZ)]


FIRST = line_x(0) + line_y(1)
SECOND = line_y(0) + line_x(1)
ALONG_Z = [[device_at(x, y, z, c) for z in range(NZ)] for x in range(NX) for y in range(NY) for c in range(2)]


def row_orders():
    rows = np.arange(D)
    ninth, z = rows % 9, rows // 9 % 8
    by_x = (rows // 288, rows // 144 % 2, rows // 72 % 2)
    by_y = (rows // 72 % 4, rows // 576, rows // 288 % 2)
    return [(z * 2 + y_lo) * 72 + x * 18 + y_hi * 9 + ninth for x, y_hi, y_lo in (by_x, by_y)]


def moved(value, to):
    pairs = []
    for place in PLACES:
        target = to(*place)
        if target is not None:
            pairs.append((device_at(*place), device_at(*target)))
    return lax.ppermute(value, AXES, pairs)


def swap_cores(value):
    return moved(value, lambda x, y, z, c: (x, y, z, 1 - c))


def swap_chips(value):
    return moved(value, lambda x, y, z, c: (x, y ^ 1, z, c))


def image_to_neighbour(value):
    return moved(value, lambda x, y, z, c: (x, y, z - 1, c) if y % 2 == 0 else (x, y, z + 1, c))


def image_down(value):
    return moved(value, lambda x, y, z, c: (x, y, z - 1, c) if y % 2 == 1 and c == 0 else None)


def pair_kernel(
    core_ref, scal_ref, lab_ref, im, io, cm, co, sm, so, fm, fo, em, eo, wi, wc, order, out,
    fx, fy, wx, wy, pv, zx, zy, ux, ix, gs, dz, dp, ft, lab, sems,
):
    sharpness = scal_ref[0]
    shift = scal_ref[1]

    def run(xs, ys, w_x, w_y, groups, own, cell):
        copies = []

        def fetch(src, dst):
            copy = pltpu.make_async_copy(src, dst, sems.at[len(copies)])
            copy.start()
            copies.append(copy)
            return copy

        for_x = [fetch(x, fx.at[pl.ds(i * R, R)]) for i, x in enumerate(xs)] + [fetch(w_x, wx)]
        for_y = [fetch(y, fy.at[pl.ds(i * R, R)]) for i, y in enumerate(ys)] + [fetch(w_y, wy)]
        for_rest = [fetch(order, pv), fetch(lab_ref, lab)]
        nx, ny = len(xs), len(ys)
        mx, my = nx * R, ny * R
        kx = -(-mx // PAD) * PAD

        def project(feats, head, m, buf):
            squares = jnp.zeros((m, 1), F32)
            for n, w in CHUNKS:
                p = jnp.dot(feats[0:m], head[:, n : n + w], preferred_element_type=F32)
                buf[0:m, n : n + w] = p
                squares = squares + jnp.sum(p * p, axis=1, keepdims=True)
            return lax.rsqrt(squares + 1e-6)

        for copy in for_x:
            copy.wait()
        inv = project(fx, wx, mx, ux)
        ix[0:mx] = jnp.broadcast_to(inv, (mx, 128))
        for n, w in CHUNKS:
            unit = ux[0:mx, n : n + w] * inv
            ux[0:mx, n : n + w] = unit
            zx[0:mx, n : n + w] = unit.astype(BF16)
        for copy in for_y:
            copy.wait()
        inv_y = project(fy, wy, my, dz)
        for b in range(ny):
            zy[b * PAD : b * PAD + R] = (dz[b * R : (b + 1) * R] * inv_y[b * R : (b + 1) * R]).astype(BF16)
            zy[b * PAD + R : (b + 1) * PAD] = jnp.zeros((PAD - R, D), BF16)
        for copy in for_rest:
            copy.wait()
        if kx > mx:
            ft[:, mx:kx] = jnp.zeros((D, kx - mx), BF16)
            dp[mx:kx] = jnp.zeros((kx - mx, D), BF16)
        ft[:, 0:mx] = lax.dot_general(
            pv[...], fx[0:mx], (((1,), (1,)), ((), ())), preferred_element_type=F32
        ).astype(BF16)
        for x0, x1, y0, y1 in groups:
            r0, r1, m = x0 * R, x1 * R, (x1 - x0) * R
            for yb in range(y0, y1):
                logits = (
                    lax.dot_general(
                        zx[r0:r1], zy[yb * PAD : (yb + 1) * PAD], (((1,), (1,)), ((), ())),
                        preferred_element_type=F32,
                    )
                    * sharpness
                    + shift
                )
                for xb in range(x0, x1):
                    part = logits[(xb - x0) * R : (xb - x0 + 1) * R]
                    scale = scal_ref[cell(xb, yb)]
                    if own(xb, yb):
                        sign = lab[xb]
                        g = (scale * sign) * jax.nn.sigmoid(sign * part)
                    else:
                        g = scale * jax.nn.sigmoid(part)
                    gs[xb * R : (xb + 1) * R, yb * PAD : (yb + 1) * PAD] = g.astype(BF16)
            along = jnp.zeros((m, 1), F32)
            for n, w in CHUNKS:
                d = sharpness * jnp.dot(
                    gs[r0:r1, y0 * PAD : y1 * PAD], zy[y0 * PAD : y1 * PAD, n : n + w],
                    preferred_element_type=F32,
                )
                dz[0:m, n : n + w] = d
                along = along + jnp.sum(d * ux[r0:r1, n : n + w], axis=1, keepdims=True)
            scale_rows = ix[r0:r1, 0:1]
            for n, w in CHUNKS:
                dp[r0:r1, n : n + w] = (
                    (dz[0:m, n : n + w] - ux[r0:r1, n : n + w] * along) * scale_rows
                ).astype(BF16)
        for n, w in CHUNKS:
            out[:, n : n + w] = jnp.dot(
                ft[:, 0:kx], dp[0:kx, n : n + w], preferred_element_type=F32
            ).astype(BF16)

    @pl.when(core_ref[0] == 0)
    def _():
        run(
            [im, io, fm, fo, em], [cm, co, sm, so], wi, wc,
            [(0, 2, 0, 4), (2, 4, 1, 4), (4, 5, 1, 2)],
            lambda x, y: x == y and x < 2,
            lambda x, y: 2 + x * 4 + y,
        )

    @pl.when(core_ref[0] == 1)
    def _():
        image = [4, 0, 1, 2, 3]
        run(
            [co, cm, so, sm], [eo, io, im, fo, fm], wc, wi,
            [(0, 2, 0, 4), (2, 4, 1, 5)],
            lambda x, y: x == image[y] and x < 2,
            lambda x, y: 2 + image[y] * 4 + x,
        )


def chip_part(*operands):
    smem = pl.BlockSpec(memory_space=pltpu.SMEM)
    return pl.pallas_call(
        pair_kernel,
        out_shape=jax.ShapeDtypeStruct((D, D), BF16),
        in_specs=[smem, smem] + [pl.BlockSpec(memory_space=pl.ANY)] * 14,
        out_specs=pl.BlockSpec(memory_space=pltpu.VMEM),
        scratch_shapes=[
            pltpu.VMEM((5 * R, D), BF16),
            pltpu.VMEM((5 * R, D), BF16),
            pltpu.VMEM((D, D), BF16),
            pltpu.VMEM((D, D), BF16),
            pltpu.VMEM((D, D), BF16),
            pltpu.VMEM((5 * R, D), BF16),
            pltpu.VMEM((5 * PAD, D), BF16),
            pltpu.VMEM((5 * R, D), F32),
            pltpu.VMEM((5 * R, 128), F32),
            pltpu.VMEM((5 * R, 5 * PAD), BF16),
            pltpu.VMEM((5 * R, D), F32),
            pltpu.VMEM((5 * PAD, D), BF16),
            pltpu.VMEM((D, 5 * PAD), BF16),
            pltpu.VMEM((2, R, PAD), F32),
            pltpu.SemaphoreType.DMA((13,)),
        ],
        compiler_params=pltpu.CompilerParams(vmem_limit_bytes=60 * 2**20),
        cost_estimate=pl.CostEstimate(flops=14 * 10**9, bytes_accessed=16 * 10**6, transcendentals=800000),
    )(*operands)


def local(
    picture_encoder_features,
    text_encoder_features,
    picture_projector,
    text_projector,
    matching_target,
    sharpness_param,
    offset_shift,
    objective_multiplier,
):
    place = lax.axis_index("dp")
    core, y_lo = place % 2, (place // 2) % 2
    coefficient = objective_multiplier[0] / (lax.axis_size("dp") * R)

    cap_sib = swap_chips(text_encoder_features)
    img_far = image_to_neighbour(picture_encoder_features)
    img_extra = image_down(picture_encoder_features)
    own_img = swap_cores(picture_encoder_features)
    own_cap = swap_cores(text_encoder_features)
    target_other = swap_cores(matching_target)
    cap_sib_other = swap_cores(cap_sib)
    img_far_other = swap_cores(img_far)
    img_extra_other = swap_cores(img_extra)

    even = y_lo == 0
    img_at = np.array([[0, 1, 4, 5, 100], [2, 3, -2, -1, 6]])
    cap_at = np.array([[0, 1, 2, 3], [2, 3, 0, 1]])
    apart = cap_at[:, None, :] - img_at[:, :, None]
    taken = ((apart >= -3) & (apart <= 2)).astype(np.float32).reshape(2, -1)
    scales = coefficient * jnp.where(even, taken[0], taken[1])
    scalars = jnp.concatenate([sharpness_param, offset_shift, scales])
    first = core == 0
    targets = jnp.stack(
        [jnp.where(first, matching_target, target_other), jnp.where(first, target_other, matching_target)]
    )
    column = lax.broadcasted_iota(jnp.int32, (2, R, PAD), 2)
    row = lax.broadcasted_iota(jnp.int32, (2, R, PAD), 1)
    wide = jnp.pad(targets, ((0, 0), (0, PAD - R)), constant_values=-1)
    match = jnp.where(first, column == targets[:, :, None], row == wide[:, None, :])
    signs = jnp.where(match, -1.0, 1.0).astype(F32)
    orders = row_orders()
    order = jnp.where(first, orders[0], orders[1]).astype(jnp.int32)
    one_hot = (lax.broadcasted_iota(jnp.int32, (D, D), 1) == order[:, None]).astype(BF16)

    part = chip_part(
        core[None].astype(jnp.int32), scalars, signs,
        picture_encoder_features, own_img, text_encoder_features, own_cap,
        cap_sib, cap_sib_other, img_far, img_far_other, img_extra, img_extra_other,
        picture_projector, text_projector, one_hot,
    )

    one = lax.all_to_all(part.reshape(4, D // 4, D), AXES, 0, 0, axis_index_groups=FIRST)
    one = jnp.sum(one.astype(F32), axis=0).astype(BF16)
    two = lax.all_to_all(one.reshape(4, D // 16, D), AXES, 0, 0, axis_index_groups=SECOND)
    two = jnp.sum(two.astype(F32), axis=0).reshape(NZ, 81, 128)
    whole = jnp.sum(lax.all_to_all(two, AXES, 0, 0, axis_index_groups=ALONG_Z), axis=0)
    spread = jnp.broadcast_to(whole[None], (8,) + whole.shape)
    gathered = lax.all_to_all(spread, "replica", 0, 0).reshape(72, D)
    keep = lax.dynamic_slice_in_dim(gathered, core * 36, 36, 0)
    give = lax.dynamic_slice_in_dim(gathered, (1 - core) * 36, 36, 0)
    got = swap_cores(give)
    return (jnp.where(first, keep, got), jnp.where(first, got, keep))


def solution(mesh):
    placed = (
        P(("dp", "replica"), None),
        P(("dp", "replica"), None),
        P(),
        P(),
        P(("dp", "replica")),
        P(),
        P(),
        P(),
    )
    return jax.shard_map(
        local, mesh=mesh, in_specs=placed, out_specs=(P("dp", None), P("dp", None)), check_vma=False
    )
```

```python
import jax
import jax.numpy as jnp
import numpy as np
from jax import lax
from jax.experimental import pallas as pl
from jax.experimental.pallas import tpu as pltpu
from jax.sharding import PartitionSpec as P

AXES = ("dp", "replica")
NX, NY, NZ = 4, 4, 8
R, D, PAD = 224, 1152, 256
F32, BF16 = jnp.float32, jnp.bfloat16
CHUNKS = [(n, min(256, D - n)) for n in range(0, D, 256)]


def device_at(x, y, z, core):
    x, y, z = x % NX, y % NY, z % NZ
    return (z * 4 + (y % 2) * 2 + core) * 8 + x * 2 + y // 2


PLACES = [(x, y, z, c) for x in range(NX) for y in range(NY) for z in range(NZ) for c in range(2)]


ALONG_Z = [[device_at(x, y, z, c) for z in range(NZ)] for x in range(NX) for y in range(NY) for c in range(2)]


def row_order(core, x, y):
    rows = np.arange(D)
    ninth, z = rows % 9, rows // 9 % 8
    one, two = rows // 288, rows // 72 % 4
    to_x = (x + jnp.where(core == 0, one, two)) % NX
    to_y = (y + jnp.where(core == 0, two, one)) % NY
    return (z * 2 + to_y % 2) * 72 + to_y // 2 * 36 + to_x * 9 + ninth


def moved(value, to):
    pairs = []
    for place in PLACES:
        target = to(*place)
        if target is not None:
            pairs.append((device_at(*place), device_at(*target)))
    return lax.ppermute(value, AXES, pairs)


def swap_cores(value):
    return moved(value, lambda x, y, z, c: (x, y, z, 1 - c))


def swap_chips(value):
    return moved(value, lambda x, y, z, c: (x, y ^ 1, z, c))


def image_to_neighbour(value):
    return moved(value, lambda x, y, z, c: (x, y, z - 1, c) if y % 2 == 0 else (x, y, z + 1, c))


def first_axis(value, by):
    return moved(value, lambda x, y, z, c: (x + by, y, z, c) if c == 0 else (x, y + by, z, c))


def second_axis(value, by):
    return moved(value, lambda x, y, z, c: (x, y + by, z, c) if c == 0 else (x + by, y, z, c))


def along_x(value, by):
    return moved(value, lambda x, y, z, c: (x + by, y, z, c))


def pass_on(value):
    def to(x, y, z, c):
        if c == y // 2:
            return (x, y ^ 2, z, c)
        return (x, y, z, 1 - c)

    return moved(value, to)


def pass_across(value):
    return moved(value, lambda x, y, z, c: (x, y ^ 2, z, 1 - c) if c != y // 2 else None)


def image_down(value):
    return moved(value, lambda x, y, z, c: (x, y, z - 1, c) if y % 2 == 1 and c == 0 else None)


def pair_kernel(
    core_ref, scal_ref, lab_ref, im, io, cm, co, sm, so, fm, fo, em, eo, wi, wc, order,
    out0, out1, out2, out3, fx, fy, wx, wy, pv, zx, zy, ux, ix, gs, dz, dp, ft, lab, sems,
):
    sharpness = scal_ref[0]
    shift = scal_ref[1]

    def run(xs, ys, w_x, w_y, groups, own, cell):
        copies = []

        def fetch(src, dst):
            copy = pltpu.make_async_copy(src, dst, sems.at[len(copies)])
            copy.start()
            copies.append(copy)
            return copy

        for_x = [fetch(x, fx.at[pl.ds(i * R, R)]) for i, x in enumerate(xs)] + [fetch(w_x, wx)]
        for_y = [fetch(y, fy.at[pl.ds(i * R, R)]) for i, y in enumerate(ys)] + [fetch(w_y, wy)]
        for_rest = [fetch(order, pv), fetch(lab_ref, lab)]
        nx, ny = len(xs), len(ys)
        mx, my = nx * R, ny * R
        kx = -(-mx // PAD) * PAD

        def project(feats, head, m, buf):
            squares = jnp.zeros((m, 1), F32)
            for n, w in CHUNKS:
                p = jnp.dot(feats[0:m], head[:, n : n + w], preferred_element_type=F32)
                buf[0:m, n : n + w] = p
                squares = squares + jnp.sum(p * p, axis=1, keepdims=True)
            return lax.rsqrt(squares + 1e-6)

        for copy in for_x:
            copy.wait()
        inv = project(fx, wx, mx, ux)
        ix[0:mx] = jnp.broadcast_to(inv, (mx, 128))
        for n, w in CHUNKS:
            unit = ux[0:mx, n : n + w] * inv
            ux[0:mx, n : n + w] = unit
            zx[0:mx, n : n + w] = unit.astype(BF16)
        for copy in for_y:
            copy.wait()
        inv_y = project(fy, wy, my, dz)
        for b in range(ny):
            zy[b * PAD : b * PAD + R] = (dz[b * R : (b + 1) * R] * inv_y[b * R : (b + 1) * R]).astype(BF16)
            zy[b * PAD + R : (b + 1) * PAD] = jnp.zeros((PAD - R, D), BF16)
        for copy in for_rest:
            copy.wait()
        if kx > mx:
            ft[:, mx:kx] = jnp.zeros((D, kx - mx), BF16)
            dp[mx:kx] = jnp.zeros((kx - mx, D), BF16)
        ft[:, 0:mx] = lax.dot_general(
            pv[...], fx[0:mx], (((1,), (1,)), ((), ())), preferred_element_type=F32
        ).astype(BF16)
        for x0, x1, y0, y1 in groups:
            r0, r1, m = x0 * R, x1 * R, (x1 - x0) * R
            for yb in range(y0, y1):
                logits = (
                    lax.dot_general(
                        zx[r0:r1], zy[yb * PAD : (yb + 1) * PAD], (((1,), (1,)), ((), ())),
                        preferred_element_type=F32,
                    )
                    * sharpness
                    + shift
                )
                for xb in range(x0, x1):
                    part = logits[(xb - x0) * R : (xb - x0 + 1) * R]
                    scale = scal_ref[cell(xb, yb)]
                    if own(xb, yb):
                        sign = lab[xb]
                        g = (scale * sign) * jax.nn.sigmoid(sign * part)
                    else:
                        g = scale * jax.nn.sigmoid(part)
                    gs[xb * R : (xb + 1) * R, yb * PAD : (yb + 1) * PAD] = g.astype(BF16)
            along = jnp.zeros((m, 1), F32)
            for n, w in CHUNKS:
                d = sharpness * jnp.dot(
                    gs[r0:r1, y0 * PAD : y1 * PAD], zy[y0 * PAD : y1 * PAD, n : n + w],
                    preferred_element_type=F32,
                )
                dz[0:m, n : n + w] = d
                along = along + jnp.sum(d * ux[r0:r1, n : n + w], axis=1, keepdims=True)
            scale_rows = ix[r0:r1, 0:1]
            for n, w in CHUNKS:
                dp[r0:r1, n : n + w] = (
                    (dz[0:m, n : n + w] - ux[r0:r1, n : n + w] * along) * scale_rows
                ).astype(BF16)
        for k, out in enumerate((out0, out1, out2, out3)):
            out[...] = jnp.dot(
                ft[k * 288 : (k + 1) * 288, 0:kx], dp[0:kx], preferred_element_type=F32
            ).astype(BF16)

    @pl.when(core_ref[0] == 0)
    def _():
        run(
            [im, io, fm, fo, em], [cm, co, sm, so], wi, wc,
            [(0, 2, 0, 4), (2, 4, 1, 4), (4, 5, 1, 2)],
            lambda x, y: x == y and x < 2,
            lambda x, y: 2 + x * 4 + y,
        )

    @pl.when(core_ref[0] == 1)
    def _():
        image = [4, 0, 1, 2, 3]
        run(
            [co, cm, so, sm], [eo, io, im, fo, fm], wc, wi,
            [(0, 2, 0, 4), (2, 4, 1, 5)],
            lambda x, y: x == image[y] and x < 2,
            lambda x, y: 2 + image[y] * 4 + x,
        )


def chip_part(*operands):
    smem = pl.BlockSpec(memory_space=pltpu.SMEM)
    return pl.pallas_call(
        pair_kernel,
        out_shape=[jax.ShapeDtypeStruct((D // 4, D), BF16)] * 4,
        in_specs=[smem, smem] + [pl.BlockSpec(memory_space=pl.ANY)] * 14,
        out_specs=[pl.BlockSpec(memory_space=pltpu.VMEM)] * 4,
        scratch_shapes=[
            pltpu.VMEM((5 * R, D), BF16),
            pltpu.VMEM((5 * R, D), BF16),
            pltpu.VMEM((D, D), BF16),
            pltpu.VMEM((D, D), BF16),
            pltpu.VMEM((D, D), BF16),
            pltpu.VMEM((5 * R, D), BF16),
            pltpu.VMEM((5 * PAD, D), BF16),
            pltpu.VMEM((5 * R, D), F32),
            pltpu.VMEM((5 * R, 128), F32),
            pltpu.VMEM((5 * R, 5 * PAD), BF16),
            pltpu.VMEM((5 * R, D), F32),
            pltpu.VMEM((5 * PAD, D), BF16),
            pltpu.VMEM((D, 5 * PAD), BF16),
            pltpu.VMEM((2, R, PAD), F32),
            pltpu.SemaphoreType.DMA((13,)),
        ],
        compiler_params=pltpu.CompilerParams(vmem_limit_bytes=60 * 2**20),
        cost_estimate=pl.CostEstimate(flops=14 * 10**9, bytes_accessed=16 * 10**6, transcendentals=800000),
    )(*operands)


def local(
    picture_encoder_features,
    text_encoder_features,
    picture_projector,
    text_projector,
    matching_target,
    sharpness_param,
    offset_shift,
    objective_multiplier,
):
    place = lax.axis_index("dp")
    core, y_lo = place % 2, (place // 2) % 2
    x, y_hi = lax.axis_index("replica") // 2, lax.axis_index("replica") % 2
    y = y_hi * 2 + y_lo
    coefficient = objective_multiplier[0] / (lax.axis_size("dp") * R)

    cap_sib = swap_chips(text_encoder_features)
    img_far = image_to_neighbour(picture_encoder_features)
    img_extra = image_down(picture_encoder_features)
    own_img = swap_cores(picture_encoder_features)
    own_cap = swap_cores(text_encoder_features)
    target_other = swap_cores(matching_target)
    cap_sib_other = swap_cores(cap_sib)
    img_far_other = swap_cores(img_far)
    img_extra_other = swap_cores(img_extra)

    even = y_lo == 0
    img_at = np.array([[0, 1, 4, 5, 100], [2, 3, -2, -1, 6]])
    cap_at = np.array([[0, 1, 2, 3], [2, 3, 0, 1]])
    apart = cap_at[:, None, :] - img_at[:, :, None]
    taken = ((apart >= -3) & (apart <= 2)).astype(np.float32).reshape(2, -1)
    scales = coefficient * jnp.where(even, taken[0], taken[1])
    scalars = jnp.concatenate([sharpness_param, offset_shift, scales])
    first = core == 0
    targets = jnp.stack(
        [jnp.where(first, matching_target, target_other), jnp.where(first, target_other, matching_target)]
    )
    column = lax.broadcasted_iota(jnp.int32, (2, R, PAD), 2)
    row = lax.broadcasted_iota(jnp.int32, (2, R, PAD), 1)
    wide = jnp.pad(targets, ((0, 0), (0, PAD - R)), constant_values=-1)
    match = jnp.where(first, column == targets[:, :, None], row == wide[:, None, :])
    signs = jnp.where(match, -1.0, 1.0).astype(F32)
    order = row_order(core, x, y).astype(jnp.int32)
    one_hot = (lax.broadcasted_iota(jnp.int32, (D, D), 1) == order[:, None]).astype(BF16)

    parts = chip_part(
        core[None].astype(jnp.int32), scalars, signs,
        picture_encoder_features, own_img, text_encoder_features, own_cap,
        cap_sib, cap_sib_other, img_far, img_far_other, img_extra, img_extra_other,
        picture_projector, text_projector, one_hot,
    )

    one = [parts[0]] + [first_axis(parts[by], by) for by in (1, 3, 2)]
    one = sum(v.astype(F32) for v in one).astype(BF16)
    pieces = [one[by * 72 : (by + 1) * 72] for by in range(4)]
    two = [pieces[0]] + [second_axis(pieces[by], by) for by in (1, 3, 2)]
    two = sum(v.astype(F32) for v in two).astype(BF16).reshape(NZ, 81, 128)
    three = lax.all_to_all(two, AXES, 0, 0, axis_index_groups=ALONG_Z)
    mine = jnp.sum(three.astype(F32), axis=0)

    ring, cross = pass_on(mine), pass_across(mine)
    home = core == y_hi
    image_piece = jnp.where(home & first, mine, jnp.where(home | first, ring, cross))
    caption_piece = jnp.where(home & first, ring, jnp.where(home, mine, jnp.where(first, cross, ring)))
    both = jnp.stack([image_piece, caption_piece])
    held = jnp.stack([both] + [along_x(both, by) for by in (1, 2, 3)])
    rows = jnp.take(held, (x - jnp.arange(NX)) % NX, axis=0).transpose(1, 0, 2, 3).reshape(2, 36, D)
    return (rows[0], rows[1])


def solution(mesh):
    placed = (
        P(("dp", "replica"), None),
        P(("dp", "replica"), None),
        P(),
        P(),
        P(("dp", "replica")),
        P(),
        P(),
        P(),
    )
    return jax.shard_map(
        local, mesh=mesh, in_specs=placed, out_specs=(P("dp", None), P("dp", None)), check_vma=False
    )
```

```python
import jax
import jax.numpy as jnp
import numpy as np
from jax import lax
from jax.experimental import pallas as pl
from jax.experimental.pallas import tpu as pltpu
from jax.sharding import PartitionSpec as P

AXES = ("dp", "replica")
NX, NY, NZ = 4, 4, 8
R, D, PAD = 224, 1152, 256
F32, BF16 = jnp.float32, jnp.bfloat16


def device_at(x, y, z, core):
    x, y, z = x % NX, y % NY, z % NZ
    return (z * 4 + (y % 2) * 2 + core) * 8 + x * 2 + y // 2


PLACES = [(x, y, z, c) for x in range(NX) for y in range(NY) for z in range(NZ) for c in range(2)]


ALONG_Z = [[device_at(x, y, z, c) for z in range(NZ)] for x in range(NX) for y in range(NY) for c in range(2)]


def row_order(core, x, y):
    rows = np.arange(D)
    ninth, z = rows % 9, rows // 9 % 8
    one, two = rows // 288, rows // 72 % 4
    to_x = (x + jnp.where(core == 0, one, two)) % NX
    to_y = (y + jnp.where(core == 0, two, one)) % NY
    return (z * 2 + to_y % 2) * 72 + to_y // 2 * 36 + to_x * 9 + ninth


def moved(value, to):
    pairs = []
    for place in PLACES:
        target = to(*place)
        if target is not None:
            pairs.append((device_at(*place), device_at(*target)))
    return lax.ppermute(value, AXES, pairs)


def swap_cores(value):
    return moved(value, lambda x, y, z, c: (x, y, z, 1 - c))


def swap_chips(value):
    return moved(value, lambda x, y, z, c: (x, y ^ 1, z, c))


def image_to_neighbour(value):
    return moved(value, lambda x, y, z, c: (x, y, z - 1, c) if y % 2 == 0 else (x, y, z + 1, c))


def first_axis(value, by):
    return moved(value, lambda x, y, z, c: (x + by, y, z, c) if c == 0 else (x, y + by, z, c))


def second_axis(value, by):
    return moved(value, lambda x, y, z, c: (x, y + by, z, c) if c == 0 else (x + by, y, z, c))


def along_x(value, by):
    return moved(value, lambda x, y, z, c: (x + by, y, z, c))


def pass_on(value):
    def to(x, y, z, c):
        if c == y // 2:
            return (x, y ^ 2, z, c)
        return (x, y, z, 1 - c)

    return moved(value, to)


def pass_across(value):
    return moved(value, lambda x, y, z, c: (x, y ^ 2, z, 1 - c) if c != y // 2 else None)


def image_down(value):
    return moved(value, lambda x, y, z, c: (x, y, z - 1, c) if y % 2 == 1 and c == 0 else None)


THIRDS = [(n, 384) for n in range(0, D, 384)]


def nt_dot(a, b):
    return lax.dot_general(a, b, (((1,), (1,)), ((), ())), preferred_element_type=F32)


def fetch(src, dst, sem):
    copy = pltpu.make_async_copy(src, dst, sem)
    copy.start()
    return copy


def by_role(core_ref, choices, sems):
    waits = []
    for k, (zero, one, dst) in enumerate(choices):

        @pl.when(core_ref[0] == 0)
        def _():
            fetch(zero, dst, sems.at[k])

        @pl.when(core_ref[0] == 1)
        def _():
            fetch(one, dst, sems.at[k])

        waits.append(pltpu.make_async_copy(zero, dst, sems.at[k]))
    return waits


def project(feats, head, tmp, rows):
    squares = jnp.zeros((rows, 1), F32)
    for n, w in THIRDS:
        p = jnp.dot(feats, head[:, n : n + w], preferred_element_type=F32)
        tmp[0:rows, n : n + w] = p
        squares = squares + jnp.sum(p * p, axis=1, keepdims=True)
    return lax.rsqrt(squares + 1e-6)


def pair_weights(scal_ref, rows, cols, xs, height, ys, gs, signs=None):
    logits = nt_dot(rows, cols) * scal_ref[0] + scal_ref[1]
    for i, x in enumerate(xs):
        for j, y in enumerate(ys):
            part = logits[i * height : (i + 1) * height, j * PAD : (j + 1) * PAD]
            scale = scal_ref[2 + x * 5 + y]
            if signs is not None and x == y:
                sign = signs[x]
                g = (scale * sign) * jax.nn.sigmoid(sign * part)
            else:
                g = scale * jax.nn.sigmoid(part)
            gs[i * height : (i + 1) * height, j * PAD : (j + 1) * PAD] = g.astype(BF16)


def own_kernel(
    core_ref, scal_ref, lab_ref, im, io, cm, co, wi, wc, order,
    zx, zy, ux, ix, ft, dz,
    f, w, pv, lab, tmp, gs, sems,
):
    waits = by_role(
        core_ref,
        [
            (im, co, f.at[0, pl.ds(0, R)]), (io, cm, f.at[0, pl.ds(R, R)]),
            (cm, io, f.at[1, pl.ds(0, R)]), (co, im, f.at[1, pl.ds(R, R)]),
            (wi, wc, w.at[0]), (wc, wi, w.at[1]),
        ],
        sems,
    )
    late = [fetch(order, pv, sems.at[6]), fetch(lab_ref, lab, sems.at[7])]
    for wait in waits:
        wait.wait()
    inv = project(f[0], w.at[0], tmp, 2 * R)
    ix[...] = jnp.broadcast_to(inv, (2 * R, 128))
    for n, wd in THIRDS:
        unit = tmp[:, n : n + wd] * inv
        ux[:, n : n + wd] = unit
        zx[:, n : n + wd] = unit.astype(BF16)
    inv = project(f[1], w.at[1], tmp, 2 * R)
    for b in range(2):
        zy[b * PAD : b * PAD + R] = (tmp[b * R : (b + 1) * R] * inv[b * R : (b + 1) * R]).astype(BF16)
        zy[b * PAD + R : (b + 1) * PAD] = jnp.zeros((PAD - R, D), BF16)
    for copy in late:
        copy.wait()

    @pl.loop(0, 3)
    def _(k):
        rows = pl.ds(pl.multiple_of(k * 384, 384), 384)
        ft[rows, 0 : 2 * R] = nt_dot(pv[rows], f[0]).astype(BF16)

    ft[:, 2 * R :] = jnp.zeros((D, 2 * PAD - 2 * R), BF16)
    pair_weights(scal_ref, zx[...], zy[...], (0, 1), R, (0, 1), gs, lab)

    @pl.loop(0, 3)
    def _(k):
        cols = pl.ds(pl.multiple_of(k * 384, 384), 384)
        dz[:, cols] = scal_ref[0] * jnp.dot(gs[...], zy[:, cols], preferred_element_type=F32)


def own_part(core, scal, lab, im, io, cm, co, wi, wc, order):
    smem = pl.BlockSpec(memory_space=pltpu.SMEM)
    vmem = pl.BlockSpec(memory_space=pltpu.VMEM)
    return pl.pallas_call(
        own_kernel,
        out_shape=[
            jax.ShapeDtypeStruct((2 * R, D), BF16),
            jax.ShapeDtypeStruct((2 * PAD, D), BF16),
            jax.ShapeDtypeStruct((2 * R, D), F32),
            jax.ShapeDtypeStruct((2 * R, 128), F32),
            jax.ShapeDtypeStruct((D, 2 * PAD), BF16),
            jax.ShapeDtypeStruct((2 * R, D), F32),
        ],
        in_specs=[smem, smem] + [pl.BlockSpec(memory_space=pl.ANY)] * 8,
        out_specs=[vmem] * 6,
        scratch_shapes=[
            pltpu.VMEM((2, 2 * R, D), BF16),
            pltpu.VMEM((2, D, D), BF16),
            pltpu.VMEM((D, D), BF16),
            pltpu.VMEM((2, R, PAD), F32),
            pltpu.VMEM((2 * R, D), F32),
            pltpu.VMEM((2 * R, 2 * PAD), BF16),
            pltpu.SemaphoreType.DMA((8,)),
        ],
        compiler_params=pltpu.CompilerParams(vmem_limit_bytes=60 * 2**20),
        cost_estimate=pl.CostEstimate(flops=6 * 10**9, bytes_accessed=16 * 10**6, transcendentals=230000),
    )(core, scal, lab, im, io, cm, co, wi, wc, order)


def arrived_kernel(
    core_ref, scal_ref, sm, so, fm, fo, em, eo, wi, wc, order, zx_in, zy_in, ux_in, ix_in, ft_in, dz_in,
    out0, out1, out2, out3,
    f, w, pv, zx, z, uo, ua, io_, ia, fto, fta, dz, da, gs, dp, tmp, sems,
):
    role = core_ref[0]
    gap = PAD - R
    rows_first = by_role(
        core_ref,
        [(fm, so, f.at[0, pl.ds(0, R)]), (fo, sm, f.at[1, pl.ds(0, R)]), (wi, wc, w.at[0])],
        sems.at[pl.ds(0, 3)],
    )
    cols_next = by_role(
        core_ref,
        [(sm, fo, f.at[3, pl.ds(0, R)]), (so, fm, f.at[4, pl.ds(0, R)]), (wc, wi, w.at[1])],
        sems.at[pl.ds(3, 3)],
    )

    @pl.when(role == 0)
    def _():
        fetch(em, f.at[2, pl.ds(0, R)], sems.at[6])
        f[5] = jnp.zeros((PAD, D), BF16)
        z[7 * PAD : 8 * PAD] = jnp.zeros((PAD, D), BF16)

    @pl.when(role == 1)
    def _():
        fetch(eo, f.at[5, pl.ds(0, R)], sems.at[6])
        f[2] = jnp.zeros((PAD, D), BF16)
        z[2 * PAD : 3 * PAD] = jnp.zeros((PAD, D), BF16)
        ua[2 * PAD : 3 * PAD] = jnp.zeros((PAD, D), F32)
        ia[2 * PAD : 3 * PAD] = jnp.zeros((PAD, 128), F32)

    for s in range(3):
        f[s, R:PAD] = jnp.zeros((gap, D), BF16)
        ua[s * PAD + R : (s + 1) * PAD] = jnp.zeros((gap, D), F32)
        ia[s * PAD + R : (s + 1) * PAD] = jnp.zeros((gap, 128), F32)
        z[s * PAD + R : (s + 1) * PAD] = jnp.zeros((gap, D), BF16)
        z[(s + 5) * PAD + R : (s + 6) * PAD] = jnp.zeros((gap, D), BF16)
    dp[2 * R : 2 * PAD] = jnp.zeros((2 * gap, D), BF16)
    extra = pltpu.make_async_copy(em, f.at[2, pl.ds(0, R)], sems.at[6])
    for wait in rows_first + [extra]:
        wait.wait()
    late = [
        fetch(order, pv, sems.at[7]),
        fetch(zx_in, zx, sems.at[8]),
        fetch(zy_in, z.at[pl.ds(3 * PAD, 2 * PAD)], sems.at[9]),
        fetch(ux_in, uo, sems.at[10]),
        fetch(ix_in, io_, sems.at[11]),
        fetch(dz_in, dz, sems.at[12]),
        fetch(ft_in, fto, sems.at[13]),
    ]

    @pl.loop(0, 3 - role)
    def _(k):
        inv = project(f[k, 0:R], w.at[0], tmp, R)
        rows = pl.ds(pl.multiple_of(k * PAD, PAD), R)
        unit = tmp[...] * inv
        z[rows] = unit.astype(BF16)
        ua[rows] = unit
        ia[rows] = jnp.broadcast_to(inv, (R, 128))

    for wait in cols_next:
        wait.wait()

    @pl.loop(0, 2 + role)
    def _(k):
        inv = project(f[k + 3, 0:R], w.at[1], tmp, R)
        z[pl.ds(pl.multiple_of((k + 5) * PAD, PAD), R)] = (tmp[...] * inv).astype(BF16)

    for copy in late:
        copy.wait()

    @pl.loop(0, 3)
    def _(k):
        rows = pl.ds(pl.multiple_of(k * 384, 384), 384)
        fta[rows] = nt_dot(pv[rows], f[0:3].reshape(3 * PAD, D)).astype(BF16)

    def spread(m, cols, y0, y1, kept, unit, inverse, base):
        @pl.loop(0, 3)
        def _(k):
            at = pl.ds(pl.multiple_of(k * 384, 384), 384)
            d = scal_ref[0] * jnp.dot(gs[0:m, 0:cols], z[y0 * PAD : y1 * PAD, at], preferred_element_type=F32)
            if kept:
                d = d + dz[:, at]
            da[0:m, at] = d

        along = jnp.sum(da[0:m] * unit[0:m], axis=1, keepdims=True)
        dp[base : base + m] = ((da[0:m] - unit[0:m] * along) * inverse[0:m, 0:1]).astype(BF16)

    @pl.when(role == 0)
    def _():
        pair_weights(scal_ref, zx[...], z[5 * PAD : 7 * PAD], (0, 1), R, (2, 3), gs)
        spread(2 * R, 2 * PAD, 5, 7, True, uo, io_, 0)
        pair_weights(scal_ref, z[0 : 2 * PAD], z[4 * PAD : 7 * PAD], (2, 3), PAD, (1, 2, 3), gs)
        spread(2 * PAD, 3 * PAD, 4, 7, False, ua, ia, 2 * PAD)
        pair_weights(scal_ref, z[2 * PAD : 3 * PAD], z[4 * PAD : 5 * PAD], (4,), PAD, (1,), gs)
        spread(PAD, PAD, 4, 5, False, ua.at[2 * PAD : 3 * PAD], ia.at[2 * PAD : 3 * PAD], 4 * PAD)

    @pl.when(role == 1)
    def _():
        pair_weights(scal_ref, zx[...], z[5 * PAD : 8 * PAD], (0, 1), R, (2, 3, 4), gs)
        spread(2 * R, 3 * PAD, 5, 8, True, uo, io_, 0)
        pair_weights(scal_ref, z[0 : 2 * PAD], z[3 * PAD : 7 * PAD], (2, 3), PAD, (0, 1, 2, 3), gs)
        spread(2 * PAD, 4 * PAD, 3, 7, False, ua, ia, 2 * PAD)
        dp[4 * PAD : 5 * PAD] = jnp.zeros((PAD, D), BF16)

    @pl.loop(0, 3)
    def _(k):
        at = pl.ds(pl.multiple_of(k * 384, 384), 384)
        own = dp[0 : 2 * PAD, at]
        rest = dp[2 * PAD : 5 * PAD, at]
        for i, out in enumerate((out0, out1, out2, out3)):
            rows = slice(i * 288, (i + 1) * 288)
            out[:, at] = (
                jnp.dot(fto[rows], own, preferred_element_type=F32)
                + jnp.dot(fta[rows], rest, preferred_element_type=F32)
            ).astype(BF16)


def arrived_part(core, scal, *operands):
    smem = pl.BlockSpec(memory_space=pltpu.SMEM)
    vmem = pl.BlockSpec(memory_space=pltpu.VMEM)
    return pl.pallas_call(
        arrived_kernel,
        out_shape=[jax.ShapeDtypeStruct((D // 4, D), BF16)] * 4,
        in_specs=[smem, smem] + [pl.BlockSpec(memory_space=pl.ANY)] * 15,
        out_specs=[vmem] * 4,
        scratch_shapes=[
            pltpu.VMEM((6, PAD, D), BF16),
            pltpu.VMEM((2, D, D), BF16),
            pltpu.VMEM((D, D), BF16),
            pltpu.VMEM((2 * R, D), BF16),
            pltpu.VMEM((8 * PAD, D), BF16),
            pltpu.VMEM((2 * R, D), F32),
            pltpu.VMEM((3 * PAD, D), F32),
            pltpu.VMEM((2 * R, 128), F32),
            pltpu.VMEM((3 * PAD, 128), F32),
            pltpu.VMEM((D, 2 * PAD), BF16),
            pltpu.VMEM((D, 3 * PAD), BF16),
            pltpu.VMEM((2 * R, D), F32),
            pltpu.VMEM((3 * PAD, D), F32),
            pltpu.VMEM((3 * PAD, 4 * PAD), BF16),
            pltpu.VMEM((5 * PAD, D), BF16),
            pltpu.VMEM((R, D), F32),
            pltpu.SemaphoreType.DMA((14,)),
        ],
        compiler_params=pltpu.CompilerParams(vmem_limit_bytes=60 * 2**20),
        cost_estimate=pl.CostEstimate(flops=14 * 10**9, bytes_accessed=20 * 10**6, transcendentals=800000),
    )(core, scal, *operands)


def local(
    picture_encoder_features,
    text_encoder_features,
    picture_projector,
    text_projector,
    matching_target,
    sharpness_param,
    offset_shift,
    objective_multiplier,
):
    place = lax.axis_index("dp")
    core, y_lo = place % 2, (place // 2) % 2
    x, y_hi = lax.axis_index("replica") // 2, lax.axis_index("replica") % 2
    y = y_hi * 2 + y_lo
    coefficient = objective_multiplier[0] / (lax.axis_size("dp") * R)

    cap_sib = swap_chips(text_encoder_features)
    img_far = image_to_neighbour(picture_encoder_features)
    img_extra = image_down(picture_encoder_features)
    target_other = swap_cores(matching_target)
    cap_sib_other = swap_cores(cap_sib)
    img_far_other = swap_cores(img_far)
    img_extra_other = swap_cores(img_extra)

    even = y_lo == 0
    img_at = np.array([[0, 1, 4, 5, 100], [2, 3, -2, -1, 6]])
    cap_at = np.array([[0, 1, 2, 3], [2, 3, 0, 1]])
    apart = cap_at[:, None, :] - img_at[:, :, None]
    taken = np.pad(((apart >= -3) & (apart <= 2)).astype(np.float32), ((0, 0), (0, 0), (0, 1)))
    first = core == 0
    taken = jnp.where(even, taken[0], taken[1])
    scales = coefficient * jnp.where(first, taken, taken.T)
    scalars = jnp.concatenate([sharpness_param, offset_shift, scales.reshape(-1)])
    targets = jnp.stack(
        [jnp.where(first, matching_target, target_other), jnp.where(first, target_other, matching_target)]
    )
    column = lax.broadcasted_iota(jnp.int32, (2, R, PAD), 2)
    row = lax.broadcasted_iota(jnp.int32, (2, R, PAD), 1)
    wide = jnp.pad(targets, ((0, 0), (0, PAD - R)), constant_values=-1)
    match = jnp.where(first, column == targets[:, :, None], row == wide[:, None, :])
    signs = jnp.where(match, -1.0, 1.0).astype(F32)
    order = row_order(core, x, y).astype(jnp.int32)
    one_hot = (lax.broadcasted_iota(jnp.int32, (D, D), 1) == order[:, None]).astype(BF16)

    role = core[None].astype(jnp.int32)
    img, cap, one_hot = lax.optimization_barrier(
        (picture_encoder_features, text_encoder_features, one_hot)
    )
    own_img = swap_cores(img)
    own_cap = swap_cores(cap)
    kept = own_part(
        role, scalars, signs, picture_encoder_features, own_img, text_encoder_features, own_cap,
        picture_projector, text_projector, one_hot,
    )
    parts = arrived_part(
        role, scalars, cap_sib, cap_sib_other, img_far, img_far_other, img_extra, img_extra_other,
        picture_projector, text_projector, one_hot, *kept,
    )

    one = [parts[0]] + [first_axis(parts[by], by) for by in (1, 3, 2)]
    one = sum(v.astype(F32) for v in one).astype(BF16)
    pieces = [one[by * 72 : (by + 1) * 72] for by in range(4)]
    two = [pieces[0]] + [second_axis(pieces[by], by) for by in (1, 3, 2)]
    two = sum(v.astype(F32) for v in two).astype(BF16).reshape(NZ, 81, 128)
    three = lax.all_to_all(two, AXES, 0, 0, axis_index_groups=ALONG_Z)
    mine = jnp.sum(three.astype(F32), axis=0)

    ring, cross = pass_on(mine), pass_across(mine)
    home = core == y_hi
    image_piece = jnp.where(home & first, mine, jnp.where(home | first, ring, cross))
    caption_piece = jnp.where(home & first, ring, jnp.where(home, mine, jnp.where(first, cross, ring)))
    both = jnp.stack([image_piece, caption_piece])
    held = jnp.stack([both] + [along_x(both, by) for by in (1, 2, 3)])
    rows = jnp.take(held, (x - jnp.arange(NX)) % NX, axis=0).transpose(1, 0, 2, 3).reshape(2, 36, D)
    return (rows[0], rows[1])


def solution(mesh):
    placed = (
        P(("dp", "replica"), None),
        P(("dp", "replica"), None),
        P(),
        P(),
        P(("dp", "replica")),
        P(),
        P(),
        P(),
    )
    return jax.shard_map(
        local, mesh=mesh, in_specs=placed, out_specs=(P("dp", None), P("dp", None)), check_vma=False
    )
```

```python
import jax
import jax.numpy as jnp
import numpy as np
from jax import lax
from jax.experimental import pallas as pl
from jax.experimental.pallas import tpu as pltpu
from jax.sharding import PartitionSpec as P

AXES = ("dp", "replica")
NX, NY, NZ = 4, 4, 8
R, D, PAD = 224, 1152, 256
F32, BF16 = jnp.float32, jnp.bfloat16


def device_at(x, y, z, core):
    x, y, z = x % NX, y % NY, z % NZ
    return (z * 4 + (y % 2) * 2 + core) * 8 + x * 2 + y // 2


PLACES = [(x, y, z, c) for x in range(NX) for y in range(NY) for z in range(NZ) for c in range(2)]


ALONG_Z = [[device_at(x, y, z, c) for z in range(NZ)] for x in range(NX) for y in range(NY) for c in range(2)]


def row_order(core, x, y):
    rows = np.arange(D)
    ninth, z = rows % 9, rows // 9 % 8
    one, two = rows // 288, rows // 72 % 4
    to_x = (x + jnp.where(core == 0, one, two)) % NX
    to_y = (y + jnp.where(core == 0, two, one)) % NY
    return (z * 2 + to_y % 2) * 72 + to_y // 2 * 36 + to_x * 9 + ninth


def moved(value, to):
    pairs = []
    for place in PLACES:
        target = to(*place)
        if target is not None:
            pairs.append((device_at(*place), device_at(*target)))
    return lax.ppermute(value, AXES, pairs)


def swap_cores(value):
    return moved(value, lambda x, y, z, c: (x, y, z, 1 - c))


def swap_chips(value):
    return moved(value, lambda x, y, z, c: (x, y ^ 1, z, c))


def image_to_neighbour(value):
    return moved(value, lambda x, y, z, c: (x, y, z - 1, c) if y % 2 == 0 else (x, y, z + 1, c))


def first_axis(value, by):
    return moved(value, lambda x, y, z, c: (x + by, y, z, c) if c == 0 else (x, y + by, z, c))


def second_axis(value, by):
    return moved(value, lambda x, y, z, c: (x, y + by, z, c) if c == 0 else (x + by, y, z, c))


def along_x(value, by):
    return moved(value, lambda x, y, z, c: (x + by, y, z, c))


def pass_on(value):
    def to(x, y, z, c):
        if c == y // 2:
            return (x, y ^ 2, z, c)
        return (x, y, z, 1 - c)

    return moved(value, to)


def pass_across(value):
    return moved(value, lambda x, y, z, c: (x, y ^ 2, z, 1 - c) if c != y // 2 else None)


def image_down(value):
    return moved(value, lambda x, y, z, c: (x, y, z - 1, c) if y % 2 == 1 and c == 0 else None)


THIRDS = [(n, 384) for n in range(0, D, 384)]


IMAGE_AT = np.array([[0, 1, 4, 5, 100], [2, 3, -2, -1, 6]])
CAPTION_AT = np.array([[0, 1, 2, 3], [2, 3, 0, 1]])
APART = CAPTION_AT[:, None, :] - IMAGE_AT[:, :, None]
TAKEN = ((APART >= -3) & (APART <= 2)).astype(float).tolist()


def nt_dot(a, b):
    return lax.dot_general(a, b, (((1,), (1,)), ((), ())), preferred_element_type=F32)


def fetch(src, dst, sem):
    copy = pltpu.make_async_copy(src, dst, sem)
    copy.start()
    return copy


def by_role(place_ref, choices, sems):
    waits = []
    for k, (zero, one, dst) in enumerate(choices):

        @pl.when(place_ref[0] == 0)
        def _():
            fetch(zero, dst, sems.at[k])

        @pl.when(place_ref[0] == 1)
        def _():
            fetch(one, dst, sems.at[k])

        waits.append(pltpu.make_async_copy(zero, dst, sems.at[k]))
    return waits


def project(feats, head, tmp, rows):
    squares = jnp.zeros((rows, 1), F32)
    for n, w in THIRDS:
        p = jnp.dot(feats, head[:, n : n + w], preferred_element_type=F32)
        tmp[0:rows, n : n + w] = p
        squares = squares + jnp.sum(p * p, axis=1, keepdims=True)
    return lax.rsqrt(squares + 1e-6)


def pair_weights(scalars, rows, cols, xs, height, ys, scale_of, gs, label=None):
    sharpness, shift = scalars
    logits = nt_dot(rows, cols) * sharpness + shift
    for i, x in enumerate(xs):
        for j, y in enumerate(ys):
            part = logits[i * height : (i + 1) * height, j * PAD : (j + 1) * PAD]
            scale = scale_of(x, y)
            if label is not None and x == y:
                match = label(x)
                g = jnp.where(match, -scale, scale) * jax.nn.sigmoid(jnp.where(match, -part, part))
            else:
                g = scale * jax.nn.sigmoid(part)
            gs[i * height : (i + 1) * height, j * PAD : (j + 1) * PAD] = g.astype(BF16)


def own_kernel(
    place_ref, sharp_ref, shift_ref, coef_ref, mine_c, other_c, mine_r, other_r, im, io, cm, co, wi, wc, order,
    zx_out, zy_out, ux_out, ix_out, ft_out, dz_out,
    f, w, pv, tmp, zx, zy, ux, ix, gs, ft, dz, sems,
):
    core = place_ref[0]
    first = by_role(
        place_ref, [(im, co, f.at[0, pl.ds(0, R)]), (io, cm, f.at[0, pl.ds(R, R)]), (wi, wc, w.at[0])],
        sems.at[pl.ds(0, 3)],
    )
    second = by_role(
        place_ref, [(cm, io, f.at[1, pl.ds(0, R)]), (co, im, f.at[1, pl.ds(R, R)]), (wc, wi, w.at[1])],
        sems.at[pl.ds(3, 3)],
    )
    for wait in first:
        wait.wait()
    inv = project(f[0], w.at[0], tmp, 2 * R)
    ix[...] = jnp.broadcast_to(inv, (2 * R, 128))
    unit = tmp[...] * inv
    ux[...] = unit
    zx[...] = unit.astype(BF16)
    outs = [fetch(ux, ux_out, sems.at[6]), fetch(zx, zx_out, sems.at[7]), fetch(ix, ix_out, sems.at[8])]
    for wait in second:
        wait.wait()
    late = fetch(order, pv, sems.at[9])
    inv = project(f[1], w.at[1], tmp, 2 * R)
    for b in range(2):
        zy[b * PAD : b * PAD + R] = (tmp[b * R : (b + 1) * R] * inv[b * R : (b + 1) * R]).astype(BF16)
        zy[b * PAD + R : (b + 1) * PAD] = jnp.zeros((PAD - R, D), BF16)
    outs.append(fetch(zy, zy_out, sems.at[10]))

    def label(k):
        mine = core == k
        by_col = jnp.where(mine, mine_c[...], other_c[...])
        by_row = jnp.where(mine, mine_r[...], other_r[...])
        shape = (R, PAD)
        target = jnp.where(core == 0, jnp.broadcast_to(by_col, shape), jnp.broadcast_to(by_row, shape))
        place = jnp.where(
            core == 0, lax.broadcasted_iota(jnp.int32, shape, 1), lax.broadcasted_iota(jnp.int32, shape, 0)
        )
        return place == target

    scalars = (sharp_ref[0], shift_ref[0])
    pair_weights(scalars, zx[...], zy[...], (0, 1), R, (0, 1), lambda x, y: coef_ref[0], gs, label)

    @pl.loop(0, 3)
    def _(k):
        cols = pl.ds(pl.multiple_of(k * 384, 384), 384)
        dz[:, cols] = sharp_ref[0] * jnp.dot(gs[...], zy[:, cols], preferred_element_type=F32)

    outs.append(fetch(dz, dz_out, sems.at[11]))
    late.wait()

    @pl.loop(0, 3)
    def _(k):
        rows = pl.ds(pl.multiple_of(k * 384, 384), 384)
        ft[rows, 0 : 2 * R] = nt_dot(pv[rows], f[0]).astype(BF16)

    ft[:, 2 * R :] = jnp.zeros((D, 2 * PAD - 2 * R), BF16)
    for copy in outs + [fetch(ft, ft_out, sems.at[12])]:
        copy.wait()


def own_part(place, sharp, shift, coef, mine_c, other_c, mine_r, other_r, *operands):
    smem = pl.BlockSpec(memory_space=pltpu.SMEM)
    vmem = pl.BlockSpec(memory_space=pltpu.VMEM)
    hbm = pl.BlockSpec(memory_space=pl.ANY)
    results = [
        ((2 * R, D), BF16), ((2 * PAD, D), BF16), ((2 * R, D), F32), ((2 * R, 128), F32), ((D, 2 * PAD), BF16),
        ((2 * R, D), F32),
    ]
    return pl.pallas_call(
        own_kernel,
        out_shape=[jax.ShapeDtypeStruct(*result) for result in results],
        in_specs=[smem] * 4 + [vmem] * 4 + [hbm] * 7,
        out_specs=[hbm] * 6,
        scratch_shapes=[
            pltpu.VMEM((2, 2 * R, D), BF16),
            pltpu.VMEM((2, D, D), BF16),
            pltpu.VMEM((D, D), BF16),
            pltpu.VMEM((2 * R, D), F32),
            pltpu.VMEM((2 * R, D), BF16),
            pltpu.VMEM((2 * PAD, D), BF16),
            pltpu.VMEM((2 * R, D), F32),
            pltpu.VMEM((2 * R, 128), F32),
            pltpu.VMEM((2 * R, 2 * PAD), BF16),
            pltpu.VMEM((D, 2 * PAD), BF16),
            pltpu.VMEM((2 * R, D), F32),
            pltpu.SemaphoreType.DMA((13,)),
        ],
        compiler_params=pltpu.CompilerParams(vmem_limit_bytes=60 * 2**20),
        cost_estimate=pl.CostEstimate(flops=6 * 10**9, bytes_accessed=16 * 10**6, transcendentals=500000),
    )(place, sharp, shift, coef, mine_c, other_c, mine_r, other_r, *operands)


def arrived_kernel(
    place_ref, sharp_ref, shift_ref, coef_ref,
    sm, so, fm, fo, em, eo, wi, wc, order, zx_in, zy_in, ux_in, ix_in, ft_in, dz_in,
    out0, out1, out2, out3,
    f, w, pv, zx, z, uo, ua, io_, ia, fto, fta, dz, da, gs, dp, tmp, sems,
):
    role, y_lo = place_ref[0], place_ref[1]
    scalars = (sharp_ref[0], shift_ref[0])
    gap = PAD - R
    rows_first = by_role(
        place_ref,
        [(fm, so, f.at[0, pl.ds(0, R)]), (fo, sm, f.at[1, pl.ds(0, R)]), (wi, wc, w.at[0])],
        sems.at[pl.ds(0, 3)],
    )
    cols_next = by_role(
        place_ref,
        [(sm, fo, f.at[3, pl.ds(0, R)]), (so, fm, f.at[4, pl.ds(0, R)]), (wc, wi, w.at[1])],
        sems.at[pl.ds(3, 3)],
    )

    @pl.when(role == 0)
    def _():
        fetch(em, f.at[2, pl.ds(0, R)], sems.at[6])
        f[5] = jnp.zeros((PAD, D), BF16)
        z[7 * PAD : 8 * PAD] = jnp.zeros((PAD, D), BF16)

    @pl.when(role == 1)
    def _():
        fetch(eo, f.at[5, pl.ds(0, R)], sems.at[6])
        f[2] = jnp.zeros((PAD, D), BF16)
        z[2 * PAD : 3 * PAD] = jnp.zeros((PAD, D), BF16)
        ua[2 * PAD : 3 * PAD] = jnp.zeros((PAD, D), F32)
        ia[2 * PAD : 3 * PAD] = jnp.zeros((PAD, 128), F32)

    for s in range(3):
        f[s, R:PAD] = jnp.zeros((gap, D), BF16)
        ua[s * PAD + R : (s + 1) * PAD] = jnp.zeros((gap, D), F32)
        ia[s * PAD + R : (s + 1) * PAD] = jnp.zeros((gap, 128), F32)
        z[s * PAD + R : (s + 1) * PAD] = jnp.zeros((gap, D), BF16)
        z[(s + 5) * PAD + R : (s + 6) * PAD] = jnp.zeros((gap, D), BF16)
    dp[2 * R : 2 * PAD] = jnp.zeros((2 * gap, D), BF16)
    extra = pltpu.make_async_copy(em, f.at[2, pl.ds(0, R)], sems.at[6])
    for wait in rows_first + [extra]:
        wait.wait()
    order_copy = fetch(order, pv, sems.at[7])
    late = [
        fetch(zx_in, zx, sems.at[8]),
        fetch(zy_in, z.at[pl.ds(3 * PAD, 2 * PAD)], sems.at[9]),
        fetch(ux_in, uo, sems.at[10]),
        fetch(ix_in, io_, sems.at[11]),
        fetch(dz_in, dz, sems.at[12]),
        fetch(ft_in, fto, sems.at[13]),
    ]

    @pl.loop(0, 3 - role)
    def _(k):
        inv = project(f[k, 0:R], w.at[0], tmp, R)
        rows = pl.ds(pl.multiple_of(k * PAD, PAD), R)
        unit = tmp[...] * inv
        z[rows] = unit.astype(BF16)
        ua[rows] = unit
        ia[rows] = jnp.broadcast_to(inv, (R, 128))

    for wait in cols_next:
        wait.wait()

    @pl.loop(0, 2 + role)
    def _(k):
        inv = project(f[k + 3, 0:R], w.at[1], tmp, R)
        z[pl.ds(pl.multiple_of((k + 5) * PAD, PAD), R)] = (tmp[...] * inv).astype(BF16)

    order_copy.wait()

    @pl.loop(0, 3)
    def _(k):
        rows = pl.ds(pl.multiple_of(k * 384, 384), 384)
        fta[rows] = nt_dot(pv[rows], f[0:3].reshape(3 * PAD, D)).astype(BF16)

    for copy in late:
        copy.wait()

    def spread(m, cols, y0, y1, kept, unit, inverse, base):
        @pl.loop(0, 3)
        def _(k):
            at = pl.ds(pl.multiple_of(k * 384, 384), 384)
            d = sharp_ref[0] * jnp.dot(gs[0:m, 0:cols], z[y0 * PAD : y1 * PAD, at], preferred_element_type=F32)
            if kept:
                d = d + dz[:, at]
            da[0:m, at] = d

        along = jnp.sum(da[0:m] * unit[0:m], axis=1, keepdims=True)
        dp[base : base + m] = ((da[0:m] - unit[0:m] * along) * inverse[0:m, 0:1]).astype(BF16)

    def scale(image, caption):
        return coef_ref[0] * jnp.where(y_lo == 0, TAKEN[0][image][caption], TAKEN[1][image][caption])

    def by_image(x, y):
        return scale(x, y)

    def by_caption(x, y):
        return scale(y, x)

    @pl.when(role == 0)
    def _():
        pair_weights(scalars, zx[...], z[5 * PAD : 7 * PAD], (0, 1), R, (2, 3), by_image, gs)
        spread(2 * R, 2 * PAD, 5, 7, True, uo, io_, 0)
        pair_weights(scalars, z[0 : 2 * PAD], z[4 * PAD : 7 * PAD], (2, 3), PAD, (1, 2, 3), by_image, gs)
        spread(2 * PAD, 3 * PAD, 4, 7, False, ua, ia, 2 * PAD)
        pair_weights(scalars, z[2 * PAD : 3 * PAD], z[4 * PAD : 5 * PAD], (4,), PAD, (1,), by_image, gs)
        spread(PAD, PAD, 4, 5, False, ua.at[2 * PAD : 3 * PAD], ia.at[2 * PAD : 3 * PAD], 4 * PAD)

    @pl.when(role == 1)
    def _():
        pair_weights(scalars, zx[...], z[5 * PAD : 8 * PAD], (0, 1), R, (2, 3, 4), by_caption, gs)
        spread(2 * R, 3 * PAD, 5, 8, True, uo, io_, 0)
        pair_weights(scalars, z[0 : 2 * PAD], z[3 * PAD : 7 * PAD], (2, 3), PAD, (0, 1, 2, 3), by_caption, gs)
        spread(2 * PAD, 4 * PAD, 3, 7, False, ua, ia, 2 * PAD)
        dp[4 * PAD : 5 * PAD] = jnp.zeros((PAD, D), BF16)

    @pl.loop(0, 3)
    def _(k):
        at = pl.ds(pl.multiple_of(k * 384, 384), 384)
        own = dp[0 : 2 * PAD, at]
        rest = dp[2 * PAD : 5 * PAD, at]
        for i, out in enumerate((out0, out1, out2, out3)):
            rows = slice(i * 288, (i + 1) * 288)
            out[:, at] = (
                jnp.dot(fto[rows], own, preferred_element_type=F32)
                + jnp.dot(fta[rows], rest, preferred_element_type=F32)
            ).astype(BF16)


def arrived_part(place, sharp, shift, coef, *operands):
    smem = pl.BlockSpec(memory_space=pltpu.SMEM)
    vmem = pl.BlockSpec(memory_space=pltpu.VMEM)
    return pl.pallas_call(
        arrived_kernel,
        out_shape=[jax.ShapeDtypeStruct((D // 4, D), BF16)] * 4,
        in_specs=[smem] * 4 + [pl.BlockSpec(memory_space=pl.ANY)] * 15,
        out_specs=[vmem] * 4,
        scratch_shapes=[
            pltpu.VMEM((6, PAD, D), BF16),
            pltpu.VMEM((2, D, D), BF16),
            pltpu.VMEM((D, D), BF16),
            pltpu.VMEM((2 * R, D), BF16),
            pltpu.VMEM((8 * PAD, D), BF16),
            pltpu.VMEM((2 * R, D), F32),
            pltpu.VMEM((3 * PAD, D), F32),
            pltpu.VMEM((2 * R, 128), F32),
            pltpu.VMEM((3 * PAD, 128), F32),
            pltpu.VMEM((D, 2 * PAD), BF16),
            pltpu.VMEM((D, 3 * PAD), BF16),
            pltpu.VMEM((2 * R, D), F32),
            pltpu.VMEM((3 * PAD, D), F32),
            pltpu.VMEM((3 * PAD, 4 * PAD), BF16),
            pltpu.VMEM((5 * PAD, D), BF16),
            pltpu.VMEM((R, D), F32),
            pltpu.SemaphoreType.DMA((14,)),
        ],
        compiler_params=pltpu.CompilerParams(vmem_limit_bytes=60 * 2**20),
        cost_estimate=pl.CostEstimate(flops=14 * 10**9, bytes_accessed=20 * 10**6, transcendentals=800000),
    )(place, sharp, shift, coef, *operands)


def local(
    picture_encoder_features,
    text_encoder_features,
    picture_projector,
    text_projector,
    matching_target,
    sharpness_param,
    offset_shift,
    objective_multiplier,
):
    place = lax.axis_index("dp")
    core, y_lo = place % 2, (place // 2) % 2
    x, y_hi = lax.axis_index("replica") // 2, lax.axis_index("replica") % 2
    y = y_hi * 2 + y_lo
    role = jnp.stack([core, y_lo, x, y]).astype(jnp.int32)
    coefficient = objective_multiplier / (lax.axis_size("dp") * R)

    own_img = swap_cores(picture_encoder_features)
    own_cap = swap_cores(text_encoder_features)
    target_other = swap_cores(matching_target)
    cap, img, coefficient = lax.optimization_barrier(
        (text_encoder_features, picture_encoder_features, coefficient)
    )
    cap_sib = swap_chips(cap)
    img_far = image_to_neighbour(img)
    img_extra = image_down(img)

    def wide(target):
        return jnp.pad(target, (0, PAD - R), constant_values=-1)[None]

    order = row_order(core, x, y).astype(jnp.int32)
    one_hot = (lax.broadcasted_iota(jnp.int32, (D, D), 1) == order[:, None]).astype(BF16)
    kept = own_part(
        role, sharpness_param, offset_shift, coefficient,
        matching_target[:, None], target_other[:, None], wide(matching_target), wide(target_other),
        picture_encoder_features, own_img, text_encoder_features, own_cap,
        picture_projector, text_projector, one_hot,
    )
    cap_sib, img_far, img_extra, kept = lax.optimization_barrier((cap_sib, img_far, img_extra, kept))
    cap_sib_other = swap_cores(cap_sib)
    img_far_other = swap_cores(img_far)
    img_extra_other = swap_cores(img_extra)
    parts = arrived_part(
        role, sharpness_param, offset_shift, coefficient,
        cap_sib, cap_sib_other, img_far, img_far_other, img_extra, img_extra_other,
        picture_projector, text_projector, one_hot, *kept,
    )

    one = [parts[0]] + [first_axis(parts[by], by) for by in (1, 3, 2)]
    one = sum(v.astype(F32) for v in one).astype(BF16)
    pieces = [one[by * 72 : (by + 1) * 72] for by in range(4)]
    two = [pieces[0]] + [second_axis(pieces[by], by) for by in (1, 3, 2)]
    two = sum(v.astype(F32) for v in two).astype(BF16).reshape(NZ, 81, 128)
    three = lax.all_to_all(two, AXES, 0, 0, axis_index_groups=ALONG_Z)
    mine = jnp.sum(three.astype(F32), axis=0)

    first = core == 0
    ring, cross = pass_on(mine), pass_across(mine)
    home = core == y_hi
    image_piece = jnp.where(home & first, mine, jnp.where(home | first, ring, cross))
    caption_piece = jnp.where(home & first, ring, jnp.where(home, mine, jnp.where(first, cross, ring)))
    both = jnp.stack([image_piece, caption_piece])
    held = jnp.stack([both] + [along_x(both, by) for by in (1, 2, 3)])
    rows = jnp.take(held, (x - jnp.arange(NX)) % NX, axis=0).transpose(1, 0, 2, 3).reshape(2, 36, D)
    return (rows[0], rows[1])


def solution(mesh):
    placed = (
        P(("dp", "replica"), None),
        P(("dp", "replica"), None),
        P(),
        P(),
        P(("dp", "replica")),
        P(),
        P(),
        P(),
    )
    return jax.shard_map(
        local, mesh=mesh, in_specs=placed, out_specs=(P("dp", None), P("dp", None)), check_vma=False
    )
```

```python
import jax
import jax.numpy as jnp
import numpy as np
from jax import lax
from jax.experimental import pallas as pl
from jax.experimental.pallas import tpu as pltpu
from jax.sharding import PartitionSpec as P

AXES = ("dp", "replica")
NX, NY, NZ = 4, 4, 8
R, D, PAD = 224, 1152, 256
F32, BF16 = jnp.float32, jnp.bfloat16


def device_at(x, y, z, core):
    x, y, z = x % NX, y % NY, z % NZ
    return (z * 4 + (y % 2) * 2 + core) * 8 + x * 2 + y // 2


PLACES = [(x, y, z, c) for x in range(NX) for y in range(NY) for z in range(NZ) for c in range(2)]


ALONG_Z = [[device_at(x, y, z, c) for z in range(NZ)] for x in range(NX) for y in range(NY) for c in range(2)]


def moved(value, to):
    pairs = []
    for place in PLACES:
        target = to(*place)
        if target is not None:
            pairs.append((device_at(*place), device_at(*target)))
    return lax.ppermute(value, AXES, pairs)


def swap_cores(value):
    return moved(value, lambda x, y, z, c: (x, y, z, 1 - c))


def swap_chips(value):
    return moved(value, lambda x, y, z, c: (x, y ^ 1, z, c))


def image_to_neighbour(value):
    return moved(value, lambda x, y, z, c: (x, y, z - 1, c) if y % 2 == 0 else (x, y, z + 1, c))


def first_axis(value, by):
    return moved(value, lambda x, y, z, c: (x + by, y, z, c) if c == 0 else (x, y + by, z, c))


def second_axis(value, by):
    return moved(value, lambda x, y, z, c: (x, y + by, z, c) if c == 0 else (x + by, y, z, c))


def along_x(value, by):
    return moved(value, lambda x, y, z, c: (x + by, y, z, c))


def pass_on(value):
    def to(x, y, z, c):
        if c == y // 2:
            return (x, y ^ 2, z, c)
        return (x, y, z, 1 - c)

    return moved(value, to)


def pass_across(value):
    return moved(value, lambda x, y, z, c: (x, y ^ 2, z, 1 - c) if c != y // 2 else None)


def image_down(value):
    return moved(value, lambda x, y, z, c: (x, y, z - 1, c) if y % 2 == 1 and c == 0 else None)


THIRDS = [(n, 384) for n in range(0, D, 384)]


IMAGE_AT = np.array([[0, 1, 4, 5, 100], [2, 3, -2, -1, 6]])
CAPTION_AT = np.array([[0, 1, 2, 3], [2, 3, 0, 1]])
APART = CAPTION_AT[:, None, :] - IMAGE_AT[:, :, None]
TAKEN = ((APART >= -3) & (APART <= 2)).astype(float).tolist()


def row_code():
    rows = np.arange(D)
    base = rows // 9 % 8 * 144 + rows % 9
    return (base + (rows // 288 << 12) + (rows // 72 % 4 << 14)).astype(np.int32)[:, None]


def nt_dot(a, b):
    return lax.dot_general(a, b, (((1,), (1,)), ((), ())), preferred_element_type=F32)


def fetch(src, dst, sem):
    copy = pltpu.make_async_copy(src, dst, sem)
    copy.start()
    return copy


def by_role(place_ref, choices, sems):
    waits = []
    for k, (zero, one, dst) in enumerate(choices):

        @pl.when(place_ref[0] == 0)
        def _():
            fetch(zero, dst, sems.at[k])

        @pl.when(place_ref[0] == 1)
        def _():
            fetch(one, dst, sems.at[k])

        waits.append(pltpu.make_async_copy(zero, dst, sems.at[k]))
    return waits


def project(feats, head, tmp, rows):
    squares = jnp.zeros((rows, 1), F32)
    for n, w in THIRDS:
        p = jnp.dot(feats, head[:, n : n + w], preferred_element_type=F32)
        tmp[0:rows, n : n + w] = p
        squares = squares + jnp.sum(p * p, axis=1, keepdims=True)
    return lax.rsqrt(squares + 1e-6)


def one_hot(place_ref, code_ref, pv):
    core, x, y = place_ref[0], place_ref[2], place_ref[3]
    for n, w in THIRDS:
        code = code_ref[n : n + w]
        one, two = (code >> 12) & 3, (code >> 14) & 3
        to_x = (x + jnp.where(core == 0, one, two)) & 3
        to_y = (y + jnp.where(core == 0, two, one)) & 3
        order = (code & 4095) + (to_y & 1) * 72 + (to_y >> 1) * 36 + to_x * 9
        pv[n : n + w] = jnp.where(lax.broadcasted_iota(jnp.int32, (w, D), 1) == order, 1.0, 0.0).astype(BF16)


def pair_weights(scalars, rows, cols, xs, height, ys, scale_of, gs, label=None):
    sharpness, shift = scalars
    logits = nt_dot(rows, cols) * sharpness + shift
    for i, x in enumerate(xs):
        for j, y in enumerate(ys):
            part = logits[i * height : (i + 1) * height, j * PAD : (j + 1) * PAD]
            scale = scale_of(x, y)
            if label is not None and x == y:
                match = label(x)
                g = jnp.where(match, -scale, scale) * jax.nn.sigmoid(jnp.where(match, -part, part))
            else:
                g = scale * jax.nn.sigmoid(part)
            gs[i * height : (i + 1) * height, j * PAD : (j + 1) * PAD] = g.astype(BF16)


def own_kernel(
    place_ref, sharp_ref, shift_ref, coef_ref, code_ref, mine_ref, other_ref, im, io, cm, co, wi, wc,
    pv_out, zx_out, zy_out, ux_out, ix_out, ft_out, dz_out,
    f, w, pv, tmp, zx, zy, ux, ix, gs, ft, dz, targets, sems,
):
    core = place_ref[0]
    first = by_role(
        place_ref, [(im, co, f.at[0, pl.ds(0, R)]), (io, cm, f.at[0, pl.ds(R, R)]), (wi, wc, w.at[0])],
        sems.at[pl.ds(0, 3)],
    )
    second = by_role(
        place_ref, [(cm, io, f.at[1, pl.ds(0, R)]), (co, im, f.at[1, pl.ds(R, R)]), (wc, wi, w.at[1])],
        sems.at[pl.ds(3, 3)],
    )
    one_hot(place_ref, code_ref, pv)
    outs = [fetch(pv, pv_out, sems.at[9])]
    targets[...] = jnp.full((2, PAD), -1, jnp.int32)
    targets[0:1, 0:R] = jnp.where(core == 0, mine_ref[...], other_ref[...])
    targets[1:2, 0:R] = jnp.where(core == 0, other_ref[...], mine_ref[...])
    for wait in first:
        wait.wait()
    inv = project(f[0], w.at[0], tmp, 2 * R)
    ix[...] = jnp.broadcast_to(inv, (2 * R, 128))
    unit = tmp[...] * inv
    ux[...] = unit
    zx[...] = unit.astype(BF16)
    outs += [fetch(ux, ux_out, sems.at[6]), fetch(zx, zx_out, sems.at[7]), fetch(ix, ix_out, sems.at[8])]
    for wait in second:
        wait.wait()
    inv = project(f[1], w.at[1], tmp, 2 * R)
    for b in range(2):
        zy[b * PAD : b * PAD + R] = (tmp[b * R : (b + 1) * R] * inv[b * R : (b + 1) * R]).astype(BF16)
        zy[b * PAD + R : (b + 1) * PAD] = jnp.zeros((PAD - R, D), BF16)
    outs.append(fetch(zy, zy_out, sems.at[10]))

    def label(k):
        down, across = lax.broadcasted_iota(jnp.int32, (R, PAD), 0), lax.broadcasted_iota(jnp.int32, (R, PAD), 1)
        by_row = jnp.broadcast_to(targets[k : k + 1], (R, PAD))
        by_col = jnp.sum(jnp.where(down == across, by_row, 0), axis=1, keepdims=True)
        target = jnp.where(core == 0, jnp.broadcast_to(by_col, (R, PAD)), by_row)
        return jnp.where(core == 0, across, down) == target

    scalars = (sharp_ref[0], shift_ref[0])
    pair_weights(scalars, zx[...], zy[...], (0, 1), R, (0, 1), lambda x, y: coef_ref[0], gs, label)

    @pl.loop(0, 3)
    def _(k):
        cols = pl.ds(pl.multiple_of(k * 384, 384), 384)
        dz[:, cols] = sharp_ref[0] * jnp.dot(gs[...], zy[:, cols], preferred_element_type=F32)

    outs.append(fetch(dz, dz_out, sems.at[11]))

    @pl.loop(0, 3)
    def _(k):
        rows = pl.ds(pl.multiple_of(k * 384, 384), 384)
        ft[rows, 0 : 2 * R] = nt_dot(pv[rows], f[0]).astype(BF16)

    ft[:, 2 * R :] = jnp.zeros((D, 2 * PAD - 2 * R), BF16)
    for copy in outs + [fetch(ft, ft_out, sems.at[12])]:
        copy.wait()


def own_part(place, sharp, shift, coef, code, mine, other, *operands):
    smem = pl.BlockSpec(memory_space=pltpu.SMEM)
    vmem = pl.BlockSpec(memory_space=pltpu.VMEM)
    hbm = pl.BlockSpec(memory_space=pl.ANY)
    results = [
        ((D, D), BF16), ((2 * R, D), BF16), ((2 * PAD, D), BF16), ((2 * R, D), F32), ((2 * R, 128), F32), ((D, 2 * PAD), BF16),
        ((2 * R, D), F32),
    ]
    return pl.pallas_call(
        own_kernel,
        out_shape=[jax.ShapeDtypeStruct(*result) for result in results],
        in_specs=[smem] * 4 + [vmem] * 3 + [hbm] * 6,
        out_specs=[hbm] * 7,
        scratch_shapes=[
            pltpu.VMEM((2, 2 * R, D), BF16),
            pltpu.VMEM((2, D, D), BF16),
            pltpu.VMEM((D, D), BF16),
            pltpu.VMEM((2 * R, D), F32),
            pltpu.VMEM((2 * R, D), BF16),
            pltpu.VMEM((2 * PAD, D), BF16),
            pltpu.VMEM((2 * R, D), F32),
            pltpu.VMEM((2 * R, 128), F32),
            pltpu.VMEM((2 * R, 2 * PAD), BF16),
            pltpu.VMEM((D, 2 * PAD), BF16),
            pltpu.VMEM((2 * R, D), F32),
            pltpu.VMEM((2, PAD), jnp.int32),
            pltpu.SemaphoreType.DMA((13,)),
        ],
        compiler_params=pltpu.CompilerParams(vmem_limit_bytes=30 * 2**20),
        cost_estimate=pl.CostEstimate(flops=6 * 10**9, bytes_accessed=16 * 10**6, transcendentals=500000),
    )(place, sharp, shift, coef, code, mine, other, *operands)


def arrived_kernel(
    place_ref, sharp_ref, shift_ref, coef_ref,
    sm, so, fm, fo, em, eo, wi, wc, order, zx_in, zy_in, ux_in, ix_in, ft_in, dz_in,
    out0, out1, out2, out3,
    f, w, pv, zx, z, uo, ua, io_, ia, fto, fta, dz, da, gs, dp, tmp, sems,
):
    role, y_lo = place_ref[0], place_ref[1]
    scalars = (sharp_ref[0], shift_ref[0])
    gap = PAD - R
    rows_first = by_role(
        place_ref,
        [(fm, so, f.at[0, pl.ds(0, R)]), (fo, sm, f.at[1, pl.ds(0, R)]), (wi, wc, w.at[0])],
        sems.at[pl.ds(0, 3)],
    )
    cols_next = by_role(
        place_ref,
        [(sm, fo, f.at[3, pl.ds(0, R)]), (so, fm, f.at[4, pl.ds(0, R)]), (wc, wi, w.at[1])],
        sems.at[pl.ds(3, 3)],
    )

    @pl.when(role == 0)
    def _():
        fetch(em, f.at[2, pl.ds(0, R)], sems.at[6])
        f[5] = jnp.zeros((PAD, D), BF16)
        z[7 * PAD : 8 * PAD] = jnp.zeros((PAD, D), BF16)

    @pl.when(role == 1)
    def _():
        fetch(eo, f.at[5, pl.ds(0, R)], sems.at[6])
        f[2] = jnp.zeros((PAD, D), BF16)
        z[2 * PAD : 3 * PAD] = jnp.zeros((PAD, D), BF16)
        ua[2 * PAD : 3 * PAD] = jnp.zeros((PAD, D), F32)
        ia[2 * PAD : 3 * PAD] = jnp.zeros((PAD, 128), F32)

    for s in range(3):
        f[s, R:PAD] = jnp.zeros((gap, D), BF16)
        ua[s * PAD + R : (s + 1) * PAD] = jnp.zeros((gap, D), F32)
        ia[s * PAD + R : (s + 1) * PAD] = jnp.zeros((gap, 128), F32)
        z[s * PAD + R : (s + 1) * PAD] = jnp.zeros((gap, D), BF16)
        z[(s + 5) * PAD + R : (s + 6) * PAD] = jnp.zeros((gap, D), BF16)
    dp[2 * R : 2 * PAD] = jnp.zeros((2 * gap, D), BF16)
    extra = pltpu.make_async_copy(em, f.at[2, pl.ds(0, R)], sems.at[6])
    for wait in rows_first + [extra]:
        wait.wait()
    order_copy = fetch(order, pv, sems.at[7])
    late = [
        fetch(zx_in, zx, sems.at[8]),
        fetch(zy_in, z.at[pl.ds(3 * PAD, 2 * PAD)], sems.at[9]),
        fetch(ux_in, uo, sems.at[10]),
        fetch(ix_in, io_, sems.at[11]),
        fetch(dz_in, dz, sems.at[12]),
        fetch(ft_in, fto, sems.at[13]),
    ]

    @pl.loop(0, 3 - role)
    def _(k):
        inv = project(f[k, 0:R], w.at[0], tmp, R)
        rows = pl.ds(pl.multiple_of(k * PAD, PAD), R)
        unit = tmp[...] * inv
        z[rows] = unit.astype(BF16)
        ua[rows] = unit
        ia[rows] = jnp.broadcast_to(inv, (R, 128))

    for wait in cols_next:
        wait.wait()

    @pl.loop(0, 2 + role)
    def _(k):
        inv = project(f[k + 3, 0:R], w.at[1], tmp, R)
        z[pl.ds(pl.multiple_of((k + 5) * PAD, PAD), R)] = (tmp[...] * inv).astype(BF16)

    order_copy.wait()

    @pl.loop(0, 3)
    def _(k):
        rows = pl.ds(pl.multiple_of(k * 384, 384), 384)
        fta[rows] = nt_dot(pv[rows], f[0:3].reshape(3 * PAD, D)).astype(BF16)

    for copy in late:
        copy.wait()

    def spread(m, cols, y0, y1, kept, unit, inverse, base):
        @pl.loop(0, 3)
        def _(k):
            at = pl.ds(pl.multiple_of(k * 384, 384), 384)
            d = sharp_ref[0] * jnp.dot(gs[0:m, 0:cols], z[y0 * PAD : y1 * PAD, at], preferred_element_type=F32)
            if kept:
                d = d + dz[:, at]
            da[0:m, at] = d

        along = jnp.sum(da[0:m] * unit[0:m], axis=1, keepdims=True)
        dp[base : base + m] = ((da[0:m] - unit[0:m] * along) * inverse[0:m, 0:1]).astype(BF16)

    def scale(image, caption):
        return coef_ref[0] * jnp.where(y_lo == 0, TAKEN[0][image][caption], TAKEN[1][image][caption])

    def by_image(x, y):
        return scale(x, y)

    def by_caption(x, y):
        return scale(y, x)

    @pl.when(role == 0)
    def _():
        pair_weights(scalars, zx[...], z[5 * PAD : 7 * PAD], (0, 1), R, (2, 3), by_image, gs)
        spread(2 * R, 2 * PAD, 5, 7, True, uo, io_, 0)
        pair_weights(scalars, z[0 : 2 * PAD], z[4 * PAD : 7 * PAD], (2, 3), PAD, (1, 2, 3), by_image, gs)
        spread(2 * PAD, 3 * PAD, 4, 7, False, ua, ia, 2 * PAD)
        pair_weights(scalars, z[2 * PAD : 3 * PAD], z[4 * PAD : 5 * PAD], (4,), PAD, (1,), by_image, gs)
        spread(PAD, PAD, 4, 5, False, ua.at[2 * PAD : 3 * PAD], ia.at[2 * PAD : 3 * PAD], 4 * PAD)

    @pl.when(role == 1)
    def _():
        pair_weights(scalars, zx[...], z[5 * PAD : 8 * PAD], (0, 1), R, (2, 3, 4), by_caption, gs)
        spread(2 * R, 3 * PAD, 5, 8, True, uo, io_, 0)
        pair_weights(scalars, z[0 : 2 * PAD], z[3 * PAD : 7 * PAD], (2, 3), PAD, (0, 1, 2, 3), by_caption, gs)
        spread(2 * PAD, 4 * PAD, 3, 7, False, ua, ia, 2 * PAD)
        dp[4 * PAD : 5 * PAD] = jnp.zeros((PAD, D), BF16)

    @pl.loop(0, 3)
    def _(k):
        at = pl.ds(pl.multiple_of(k * 384, 384), 384)
        own = dp[0 : 2 * PAD, at]
        rest = dp[2 * PAD : 5 * PAD, at]
        for i, out in enumerate((out0, out1, out2, out3)):
            rows = slice(i * 288, (i + 1) * 288)
            out[:, at] = (
                jnp.dot(fto[rows], own, preferred_element_type=F32)
                + jnp.dot(fta[rows], rest, preferred_element_type=F32)
            ).astype(BF16)


def arrived_part(place, sharp, shift, coef, *operands):
    smem = pl.BlockSpec(memory_space=pltpu.SMEM)
    vmem = pl.BlockSpec(memory_space=pltpu.VMEM)
    return pl.pallas_call(
        arrived_kernel,
        out_shape=[jax.ShapeDtypeStruct((D // 4, D), BF16)] * 4,
        in_specs=[smem] * 4 + [pl.BlockSpec(memory_space=pl.ANY)] * 15,
        out_specs=[vmem] * 4,
        scratch_shapes=[
            pltpu.VMEM((6, PAD, D), BF16),
            pltpu.VMEM((2, D, D), BF16),
            pltpu.VMEM((D, D), BF16),
            pltpu.VMEM((2 * R, D), BF16),
            pltpu.VMEM((8 * PAD, D), BF16),
            pltpu.VMEM((2 * R, D), F32),
            pltpu.VMEM((3 * PAD, D), F32),
            pltpu.VMEM((2 * R, 128), F32),
            pltpu.VMEM((3 * PAD, 128), F32),
            pltpu.VMEM((D, 2 * PAD), BF16),
            pltpu.VMEM((D, 3 * PAD), BF16),
            pltpu.VMEM((2 * R, D), F32),
            pltpu.VMEM((3 * PAD, D), F32),
            pltpu.VMEM((3 * PAD, 4 * PAD), BF16),
            pltpu.VMEM((5 * PAD, D), BF16),
            pltpu.VMEM((R, D), F32),
            pltpu.SemaphoreType.DMA((14,)),
        ],
        compiler_params=pltpu.CompilerParams(vmem_limit_bytes=46 * 2**20),
        cost_estimate=pl.CostEstimate(flops=14 * 10**9, bytes_accessed=20 * 10**6, transcendentals=800000),
    )(place, sharp, shift, coef, *operands)


def join_kernel(place_ref, one, two, three, four, image_out, caption_out, held):
    for k, piece in enumerate((one, two, three, four)):
        held[k] = piece[...]
    for place in range(NX):
        back = (place_ref[2] - place) & 3
        for head, out in enumerate((image_out, caption_out)):
            for row in range(9):
                at = place * 9 + row
                for n in range(9):
                    out[at : at + 1, n * 128 : (n + 1) * 128] = held[back, head, row * 9 + n : row * 9 + n + 1]


def join_rows(place, *pieces):
    vmem = pl.BlockSpec(memory_space=pltpu.VMEM)
    return pl.pallas_call(
        join_kernel,
        out_shape=[jax.ShapeDtypeStruct((36, D), F32)] * 2,
        in_specs=[pl.BlockSpec(memory_space=pltpu.SMEM)] + [vmem] * 4,
        out_specs=[vmem] * 2,
        scratch_shapes=[pltpu.VMEM((4, 2, 81, 128), F32)],
    )(place, *pieces)


def local(
    picture_encoder_features,
    text_encoder_features,
    picture_projector,
    text_projector,
    matching_target,
    sharpness_param,
    offset_shift,
    objective_multiplier,
):
    place = lax.axis_index("dp")
    core, y_lo = place % 2, (place // 2) % 2
    x, y_hi = lax.axis_index("replica") // 2, lax.axis_index("replica") % 2
    y = y_hi * 2 + y_lo
    role = jnp.stack([core, y_lo, x, y]).astype(jnp.int32)
    coefficient = objective_multiplier / (lax.axis_size("dp") * R)

    own_img = swap_cores(picture_encoder_features)
    own_cap = swap_cores(text_encoder_features)
    target_other = swap_cores(matching_target)
    cap, img, target_other = lax.optimization_barrier(
        (text_encoder_features, picture_encoder_features, target_other)
    )
    cap_sib = swap_chips(cap)
    img_far = image_to_neighbour(img)
    img_extra = image_down(img)

    order, *kept = own_part(
        role, sharpness_param, offset_shift, coefficient, row_code(),
        matching_target[None], target_other[None],
        picture_encoder_features, own_img, text_encoder_features, own_cap,
        picture_projector, text_projector,
    )
    cap_sib, img_far, img_extra, order, kept = lax.optimization_barrier(
        (cap_sib, img_far, img_extra, order, kept)
    )
    cap_sib_other = swap_cores(cap_sib)
    img_far_other = swap_cores(img_far)
    img_extra_other = swap_cores(img_extra)
    parts = arrived_part(
        role, sharpness_param, offset_shift, coefficient,
        cap_sib, cap_sib_other, img_far, img_far_other, img_extra, img_extra_other,
        picture_projector, text_projector, order, *kept,
    )

    one = [parts[0]] + [first_axis(parts[by], by) for by in (1, 3, 2)]
    one = sum(v.astype(F32) for v in one).astype(BF16)
    pieces = [one[by * 72 : (by + 1) * 72] for by in range(4)]
    two = [pieces[0]] + [second_axis(pieces[by], by) for by in (1, 3, 2)]
    two = sum(v.astype(F32) for v in two).astype(BF16).reshape(NZ, 81, 128)
    three = lax.all_to_all(two, AXES, 0, 0, axis_index_groups=ALONG_Z)
    mine = jnp.sum(three.astype(F32), axis=0)

    first = core == 0
    ring, cross = pass_on(mine), pass_across(mine)
    home = core == y_hi
    image_piece = jnp.where(home & first, mine, jnp.where(home | first, ring, cross))
    caption_piece = jnp.where(home & first, ring, jnp.where(home, mine, jnp.where(first, cross, ring)))
    both = jnp.stack([image_piece, caption_piece])
    return join_rows(role, both, *[along_x(both, by) for by in (1, 2, 3)])


def solution(mesh):
    placed = (
        P(("dp", "replica"), None),
        P(("dp", "replica"), None),
        P(),
        P(),
        P(("dp", "replica")),
        P(),
        P(),
        P(),
    )
    return jax.shard_map(
        local, mesh=mesh, in_specs=placed, out_specs=(P("dp", None), P("dp", None)), check_vma=False
    )
```

```python
import jax
import jax.numpy as jnp
import numpy as np
from jax import lax
from jax.experimental import pallas as pl
from jax.experimental.pallas import tpu as pltpu
from jax.sharding import PartitionSpec as P

AXES = ("dp", "replica")
NX, NY, NZ = 4, 4, 8
R, D, PAD = 224, 1152, 256
F32, BF16 = jnp.float32, jnp.bfloat16


def device_at(x, y, z, core):
    x, y, z = x % NX, y % NY, z % NZ
    return (z * 4 + (y % 2) * 2 + core) * 8 + x * 2 + y // 2


PLACES = [(x, y, z, c) for x in range(NX) for y in range(NY) for z in range(NZ) for c in range(2)]


ALONG_Z = [[device_at(x, y, z, c) for z in range(NZ)] for x in range(NX) for y in range(NY) for c in range(2)]


def moved(value, to):
    pairs = []
    for place in PLACES:
        target = to(*place)
        if target is not None:
            pairs.append((device_at(*place), device_at(*target)))
    return lax.ppermute(value, AXES, pairs)


def swap_cores(value):
    return moved(value, lambda x, y, z, c: (x, y, z, 1 - c))


def swap_chips(value):
    return moved(value, lambda x, y, z, c: (x, y ^ 1, z, c))


def image_to_neighbour(value):
    return moved(value, lambda x, y, z, c: (x, y, z - 1, c) if y % 2 == 0 else (x, y, z + 1, c))


def first_axis(value, by):
    return moved(value, lambda x, y, z, c: (x + by, y, z, c) if c == 0 else (x, y + by, z, c))


def second_axis(value, by):
    return moved(value, lambda x, y, z, c: (x, y + by, z, c) if c == 0 else (x + by, y, z, c))


def along_x(value, by):
    return moved(value, lambda x, y, z, c: (x + by, y, z, c))


def pass_on(value):
    def to(x, y, z, c):
        if c == y // 2:
            return (x, y ^ 2, z, c)
        return (x, y, z, 1 - c)

    return moved(value, to)


def pass_across(value):
    return moved(value, lambda x, y, z, c: (x, y ^ 2, z, 1 - c) if c != y // 2 else None)


def image_down(value):
    return moved(value, lambda x, y, z, c: (x, y, z - 1, c) if y % 2 == 1 and c == 0 else None)


THIRDS = [(n, 384) for n in range(0, D, 384)]


IMAGE_AT = np.array([[0, 1, 4, 5, 100], [2, 3, -2, -1, 6]])
CAPTION_AT = np.array([[0, 1, 2, 3], [2, 3, 0, 1]])
APART = CAPTION_AT[:, None, :] - IMAGE_AT[:, :, None]
TAKEN = ((APART >= -3) & (APART <= 2)).astype(float).tolist()


def row_code():
    rows = np.arange(D)
    base = rows // 9 % 8 * 144 + rows % 9
    return (base + (rows // 288 << 12) + (rows // 72 % 4 << 14)).astype(np.int32)[:, None]


def nt_dot(a, b):
    return lax.dot_general(a, b, (((1,), (1,)), ((), ())), preferred_element_type=F32)


def fetch(src, dst, sem):
    copy = pltpu.make_async_copy(src, dst, sem)
    copy.start()
    return copy


def by_role(place_ref, choices, sems):
    waits = []
    for k, (zero, one, dst) in enumerate(choices):

        @pl.when(place_ref[0] == 0)
        def _():
            fetch(zero, dst, sems.at[k])

        @pl.when(place_ref[0] == 1)
        def _():
            fetch(one, dst, sems.at[k])

        waits.append(pltpu.make_async_copy(zero, dst, sems.at[k]))
    return waits


def project(feats, head, tmp, rows):
    squares = jnp.zeros((rows, 1), F32)
    for n, w in THIRDS:
        p = jnp.dot(feats, head[:, n : n + w], preferred_element_type=F32)
        tmp[0:rows, n : n + w] = p
        squares = squares + jnp.sum(p * p, axis=1, keepdims=True)
    return lax.rsqrt(squares + 1e-6)


def one_hot(place_ref, code_ref, pv):
    core, x, y = place_ref[0], place_ref[2], place_ref[3]
    for n, w in THIRDS:
        code = code_ref[n : n + w]
        one, two = (code >> 12) & 3, (code >> 14) & 3
        to_x = (x + jnp.where(core == 0, one, two)) & 3
        to_y = (y + jnp.where(core == 0, two, one)) & 3
        order = (code & 4095) + (to_y & 1) * 72 + (to_y >> 1) * 36 + to_x * 9
        pv[n : n + w] = jnp.where(lax.broadcasted_iota(jnp.int32, (w, D), 1) == order, 1.0, 0.0).astype(BF16)


def pair_weights(scalars, rows, cols, xs, height, ys, scale_of, gs, label=None):
    sharpness, shift = scalars
    logits = nt_dot(rows, cols) * sharpness + shift
    for i, x in enumerate(xs):
        for j, y in enumerate(ys):
            part = logits[i * height : (i + 1) * height, j * PAD : (j + 1) * PAD]
            scale = scale_of(x, y)
            if label is not None and x == y:
                match = label(x)
                g = jnp.where(match, -scale, scale) * jax.nn.sigmoid(jnp.where(match, -part, part))
            else:
                g = scale * jax.nn.sigmoid(part)
            gs[i * height : (i + 1) * height, j * PAD : (j + 1) * PAD] = g.astype(BF16)


def own_kernel(
    place_ref, sharp_ref, shift_ref, coef_ref, mine_ref, other_ref, im, io, cm, co, wi, wc,
    zx_out, zy_out, ux_out, ix_out, dz_out,
    f, w, tmp, zx, zy, ux, ix, gs, dz, targets, sems,
):
    core = place_ref[0]
    first = by_role(
        place_ref, [(im, co, f.at[0, pl.ds(0, R)]), (io, cm, f.at[0, pl.ds(R, R)]), (wi, wc, w.at[0])],
        sems.at[pl.ds(0, 3)],
    )
    second = by_role(
        place_ref, [(cm, io, f.at[1, pl.ds(0, R)]), (co, im, f.at[1, pl.ds(R, R)]), (wc, wi, w.at[1])],
        sems.at[pl.ds(3, 3)],
    )
    targets[...] = jnp.full((2, PAD), -1, jnp.int32)
    targets[0:1, 0:R] = jnp.where(core == 0, mine_ref[...], other_ref[...])
    targets[1:2, 0:R] = jnp.where(core == 0, other_ref[...], mine_ref[...])
    for wait in first:
        wait.wait()
    inv = project(f[0], w.at[0], tmp, 2 * R)
    ix[...] = jnp.broadcast_to(inv, (2 * R, 128))
    unit = tmp[...] * inv
    ux[...] = unit
    zx[...] = unit.astype(BF16)
    outs = [fetch(ux, ux_out, sems.at[6]), fetch(zx, zx_out, sems.at[7]), fetch(ix, ix_out, sems.at[8])]
    for wait in second:
        wait.wait()
    inv = project(f[1], w.at[1], tmp, 2 * R)
    for b in range(2):
        zy[b * PAD : b * PAD + R] = (tmp[b * R : (b + 1) * R] * inv[b * R : (b + 1) * R]).astype(BF16)
        zy[b * PAD + R : (b + 1) * PAD] = jnp.zeros((PAD - R, D), BF16)
    outs.append(fetch(zy, zy_out, sems.at[10]))

    def label(k):
        down, across = lax.broadcasted_iota(jnp.int32, (R, PAD), 0), lax.broadcasted_iota(jnp.int32, (R, PAD), 1)
        by_row = jnp.broadcast_to(targets[k : k + 1], (R, PAD))
        by_col = jnp.sum(jnp.where(down == across, by_row, 0), axis=1, keepdims=True)
        target = jnp.where(core == 0, jnp.broadcast_to(by_col, (R, PAD)), by_row)
        return jnp.where(core == 0, across, down) == target

    scalars = (sharp_ref[0], shift_ref[0])
    pair_weights(scalars, zx[...], zy[...], (0, 1), R, (0, 1), lambda x, y: coef_ref[0], gs, label)

    @pl.loop(0, 3)
    def _(k):
        cols = pl.ds(pl.multiple_of(k * 384, 384), 384)
        dz[:, cols] = sharp_ref[0] * jnp.dot(gs[...], zy[:, cols], preferred_element_type=F32)

    outs.append(fetch(dz, dz_out, sems.at[11]))

    for copy in outs:
        copy.wait()


def own_part(place, sharp, shift, coef, mine, other, *operands):
    smem = pl.BlockSpec(memory_space=pltpu.SMEM)
    vmem = pl.BlockSpec(memory_space=pltpu.VMEM)
    hbm = pl.BlockSpec(memory_space=pl.ANY)
    results = [
        ((2 * R, D), BF16), ((2 * PAD, D), BF16), ((2 * R, D), F32), ((2 * R, 128), F32),
        ((2 * R, D), F32),
    ]
    return pl.pallas_call(
        own_kernel,
        out_shape=[jax.ShapeDtypeStruct(*result) for result in results],
        in_specs=[smem] * 4 + [vmem] * 2 + [hbm] * 6,
        out_specs=[hbm] * 5,
        scratch_shapes=[
            pltpu.VMEM((2, 2 * R, D), BF16),
            pltpu.VMEM((2, D, D), BF16),
            pltpu.VMEM((2 * R, D), F32),
            pltpu.VMEM((2 * R, D), BF16),
            pltpu.VMEM((2 * PAD, D), BF16),
            pltpu.VMEM((2 * R, D), F32),
            pltpu.VMEM((2 * R, 128), F32),
            pltpu.VMEM((2 * R, 2 * PAD), BF16),
            pltpu.VMEM((2 * R, D), F32),
            pltpu.VMEM((2, PAD), jnp.int32),
            pltpu.SemaphoreType.DMA((13,)),
        ],
        compiler_params=pltpu.CompilerParams(vmem_limit_bytes=60 * 2**20),
        cost_estimate=pl.CostEstimate(flops=6 * 10**9, bytes_accessed=16 * 10**6, transcendentals=500000),
    )(place, sharp, shift, coef, mine, other, *operands)


def turn_kernel(place_ref, code_ref, im, io, cm, co, pv_out, ft_out, f, pv, ft, sems):
    feats = by_role(
        place_ref, [(im, co, f.at[pl.ds(0, R)]), (io, cm, f.at[pl.ds(R, R)])], sems.at[pl.ds(0, 2)]
    )
    one_hot(place_ref, code_ref, pv)
    outs = [fetch(pv, pv_out, sems.at[2])]
    for wait in feats:
        wait.wait()

    @pl.loop(0, 3)
    def _(k):
        rows = pl.ds(pl.multiple_of(k * 384, 384), 384)
        ft[rows, 0 : 2 * R] = nt_dot(pv[rows], f[...]).astype(BF16)

    ft[:, 2 * R :] = jnp.zeros((D, 2 * PAD - 2 * R), BF16)
    for copy in outs + [fetch(ft, ft_out, sems.at[3])]:
        copy.wait()


def turn_own(place, code, *operands):
    hbm = pl.BlockSpec(memory_space=pl.ANY)
    return pl.pallas_call(
        turn_kernel,
        out_shape=[jax.ShapeDtypeStruct((D, D), BF16), jax.ShapeDtypeStruct((D, 2 * PAD), BF16)],
        in_specs=[pl.BlockSpec(memory_space=pltpu.SMEM), pl.BlockSpec(memory_space=pltpu.VMEM)] + [hbm] * 4,
        out_specs=[hbm] * 2,
        scratch_shapes=[
            pltpu.VMEM((2 * R, D), BF16),
            pltpu.VMEM((D, D), BF16),
            pltpu.VMEM((D, 2 * PAD), BF16),
            pltpu.SemaphoreType.DMA((4,)),
        ],
        compiler_params=pltpu.CompilerParams(vmem_limit_bytes=60 * 2**20),
        cost_estimate=pl.CostEstimate(flops=2 * 10**9, bytes_accessed=6 * 10**6, transcendentals=0),
    )(place, code, *operands)


def arrived_kernel(
    place_ref, sharp_ref, shift_ref, coef_ref,
    sm, so, fm, fo, em, eo, wi, wc, order, zx_in, zy_in, ux_in, ix_in, ft_in, dz_in,
    out0, out1, out2, out3,
    f, w, pv, zx, z, uo, ua, io_, ia, fto, fta, dz, da, gs, dp, tmp, sems,
):
    role, y_lo = place_ref[0], place_ref[1]
    scalars = (sharp_ref[0], shift_ref[0])
    gap = PAD - R
    rows_first = by_role(
        place_ref,
        [(fm, so, f.at[0, pl.ds(0, R)]), (fo, sm, f.at[1, pl.ds(0, R)]), (wi, wc, w.at[0])],
        sems.at[pl.ds(0, 3)],
    )
    cols_next = by_role(
        place_ref,
        [(sm, fo, f.at[3, pl.ds(0, R)]), (so, fm, f.at[4, pl.ds(0, R)]), (wc, wi, w.at[1])],
        sems.at[pl.ds(3, 3)],
    )

    @pl.when(role == 0)
    def _():
        fetch(em, f.at[2, pl.ds(0, R)], sems.at[6])
        f[5] = jnp.zeros((PAD, D), BF16)
        z[7 * PAD : 8 * PAD] = jnp.zeros((PAD, D), BF16)

    @pl.when(role == 1)
    def _():
        fetch(eo, f.at[5, pl.ds(0, R)], sems.at[6])
        f[2] = jnp.zeros((PAD, D), BF16)
        z[2 * PAD : 3 * PAD] = jnp.zeros((PAD, D), BF16)
        ua[2 * PAD : 3 * PAD] = jnp.zeros((PAD, D), F32)
        ia[2 * PAD : 3 * PAD] = jnp.zeros((PAD, 128), F32)

    for s in range(3):
        f[s, R:PAD] = jnp.zeros((gap, D), BF16)
        ua[s * PAD + R : (s + 1) * PAD] = jnp.zeros((gap, D), F32)
        ia[s * PAD + R : (s + 1) * PAD] = jnp.zeros((gap, 128), F32)
        z[s * PAD + R : (s + 1) * PAD] = jnp.zeros((gap, D), BF16)
        z[(s + 5) * PAD + R : (s + 6) * PAD] = jnp.zeros((gap, D), BF16)
    dp[2 * R : 2 * PAD] = jnp.zeros((2 * gap, D), BF16)
    extra = pltpu.make_async_copy(em, f.at[2, pl.ds(0, R)], sems.at[6])
    for wait in rows_first + [extra]:
        wait.wait()
    order_copy = fetch(order, pv, sems.at[7])
    late = [
        fetch(zx_in, zx, sems.at[8]),
        fetch(zy_in, z.at[pl.ds(3 * PAD, 2 * PAD)], sems.at[9]),
        fetch(ux_in, uo, sems.at[10]),
        fetch(ix_in, io_, sems.at[11]),
        fetch(dz_in, dz, sems.at[12]),
        fetch(ft_in, fto, sems.at[13]),
    ]

    @pl.loop(0, 3 - role)
    def _(k):
        inv = project(f[k, 0:R], w.at[0], tmp, R)
        rows = pl.ds(pl.multiple_of(k * PAD, PAD), R)
        unit = tmp[...] * inv
        z[rows] = unit.astype(BF16)
        ua[rows] = unit
        ia[rows] = jnp.broadcast_to(inv, (R, 128))

    for wait in cols_next:
        wait.wait()

    @pl.loop(0, 2 + role)
    def _(k):
        inv = project(f[k + 3, 0:R], w.at[1], tmp, R)
        z[pl.ds(pl.multiple_of((k + 5) * PAD, PAD), R)] = (tmp[...] * inv).astype(BF16)

    order_copy.wait()

    @pl.loop(0, 3)
    def _(k):
        rows = pl.ds(pl.multiple_of(k * 384, 384), 384)
        fta[rows] = nt_dot(pv[rows], f[0:3].reshape(3 * PAD, D)).astype(BF16)

    for copy in late:
        copy.wait()

    def spread(m, cols, y0, y1, kept, unit, inverse, base):
        @pl.loop(0, 3)
        def _(k):
            at = pl.ds(pl.multiple_of(k * 384, 384), 384)
            d = sharp_ref[0] * jnp.dot(gs[0:m, 0:cols], z[y0 * PAD : y1 * PAD, at], preferred_element_type=F32)
            if kept:
                d = d + dz[:, at]
            da[0:m, at] = d

        along = jnp.sum(da[0:m] * unit[0:m], axis=1, keepdims=True)
        dp[base : base + m] = ((da[0:m] - unit[0:m] * along) * inverse[0:m, 0:1]).astype(BF16)

    def scale(image, caption):
        return coef_ref[0] * jnp.where(y_lo == 0, TAKEN[0][image][caption], TAKEN[1][image][caption])

    def by_image(x, y):
        return scale(x, y)

    def by_caption(x, y):
        return scale(y, x)

    @pl.when(role == 0)
    def _():
        pair_weights(scalars, zx[...], z[5 * PAD : 7 * PAD], (0, 1), R, (2, 3), by_image, gs)
        spread(2 * R, 2 * PAD, 5, 7, True, uo, io_, 0)
        pair_weights(scalars, z[0 : 2 * PAD], z[4 * PAD : 7 * PAD], (2, 3), PAD, (1, 2, 3), by_image, gs)
        spread(2 * PAD, 3 * PAD, 4, 7, False, ua, ia, 2 * PAD)
        pair_weights(scalars, z[2 * PAD : 3 * PAD], z[4 * PAD : 5 * PAD], (4,), PAD, (1,), by_image, gs)
        spread(PAD, PAD, 4, 5, False, ua.at[2 * PAD : 3 * PAD], ia.at[2 * PAD : 3 * PAD], 4 * PAD)

    @pl.when(role == 1)
    def _():
        pair_weights(scalars, zx[...], z[5 * PAD : 8 * PAD], (0, 1), R, (2, 3, 4), by_caption, gs)
        spread(2 * R, 3 * PAD, 5, 8, True, uo, io_, 0)
        pair_weights(scalars, z[0 : 2 * PAD], z[3 * PAD : 7 * PAD], (2, 3), PAD, (0, 1, 2, 3), by_caption, gs)
        spread(2 * PAD, 4 * PAD, 3, 7, False, ua, ia, 2 * PAD)
        dp[4 * PAD : 5 * PAD] = jnp.zeros((PAD, D), BF16)

    @pl.loop(0, 3)
    def _(k):
        at = pl.ds(pl.multiple_of(k * 384, 384), 384)
        own = dp[0 : 2 * PAD, at]
        rest = dp[2 * PAD : 5 * PAD, at]
        for i, out in enumerate((out0, out1, out2, out3)):
            rows = slice(i * 288, (i + 1) * 288)
            out[:, at] = (
                jnp.dot(fto[rows], own, preferred_element_type=F32)
                + jnp.dot(fta[rows], rest, preferred_element_type=F32)
            ).astype(BF16)


def arrived_part(place, sharp, shift, coef, *operands):
    smem = pl.BlockSpec(memory_space=pltpu.SMEM)
    vmem = pl.BlockSpec(memory_space=pltpu.VMEM)
    return pl.pallas_call(
        arrived_kernel,
        out_shape=[jax.ShapeDtypeStruct((D // 4, D), BF16)] * 4,
        in_specs=[smem] * 4 + [pl.BlockSpec(memory_space=pl.ANY)] * 15,
        out_specs=[vmem] * 4,
        scratch_shapes=[
            pltpu.VMEM((6, PAD, D), BF16),
            pltpu.VMEM((2, D, D), BF16),
            pltpu.VMEM((D, D), BF16),
            pltpu.VMEM((2 * R, D), BF16),
            pltpu.VMEM((8 * PAD, D), BF16),
            pltpu.VMEM((2 * R, D), F32),
            pltpu.VMEM((3 * PAD, D), F32),
            pltpu.VMEM((2 * R, 128), F32),
            pltpu.VMEM((3 * PAD, 128), F32),
            pltpu.VMEM((D, 2 * PAD), BF16),
            pltpu.VMEM((D, 3 * PAD), BF16),
            pltpu.VMEM((2 * R, D), F32),
            pltpu.VMEM((3 * PAD, D), F32),
            pltpu.VMEM((3 * PAD, 4 * PAD), BF16),
            pltpu.VMEM((5 * PAD, D), BF16),
            pltpu.VMEM((R, D), F32),
            pltpu.SemaphoreType.DMA((14,)),
        ],
        compiler_params=pltpu.CompilerParams(vmem_limit_bytes=60 * 2**20),
        cost_estimate=pl.CostEstimate(flops=14 * 10**9, bytes_accessed=20 * 10**6, transcendentals=800000),
    )(place, sharp, shift, coef, *operands)


def join_kernel(place_ref, one, two, three, four, image_out, caption_out, held):
    for k, piece in enumerate((one, two, three, four)):
        held[k] = piece[...]
    for place in range(NX):
        back = (place_ref[2] - place) & 3
        for head, out in enumerate((image_out, caption_out)):
            for row in range(9):
                at = place * 9 + row
                for n in range(9):
                    out[at : at + 1, n * 128 : (n + 1) * 128] = held[back, head, row * 9 + n : row * 9 + n + 1]


def join_rows(place, *pieces):
    vmem = pl.BlockSpec(memory_space=pltpu.VMEM)
    return pl.pallas_call(
        join_kernel,
        out_shape=[jax.ShapeDtypeStruct((36, D), F32)] * 2,
        in_specs=[pl.BlockSpec(memory_space=pltpu.SMEM)] + [vmem] * 4,
        out_specs=[vmem] * 2,
        scratch_shapes=[pltpu.VMEM((4, 2, 81, 128), F32)],
    )(place, *pieces)


def local(
    picture_encoder_features,
    text_encoder_features,
    picture_projector,
    text_projector,
    matching_target,
    sharpness_param,
    offset_shift,
    objective_multiplier,
):
    place = lax.axis_index("dp")
    core, y_lo = place % 2, (place // 2) % 2
    x, y_hi = lax.axis_index("replica") // 2, lax.axis_index("replica") % 2
    y = y_hi * 2 + y_lo
    role = jnp.stack([core, y_lo, x, y]).astype(jnp.int32)
    coefficient = objective_multiplier / (lax.axis_size("dp") * R)

    own_img = swap_cores(picture_encoder_features)
    own_cap = swap_cores(text_encoder_features)
    target_other = swap_cores(matching_target)
    cap, img, target_other = lax.optimization_barrier(
        (text_encoder_features, picture_encoder_features, target_other)
    )
    cap_sib = swap_chips(cap)
    img_far = image_to_neighbour(img)
    img_extra = image_down(img)

    blocks = (picture_encoder_features, own_img, text_encoder_features, own_cap)
    *kept, from_own = own_part(
        role, sharpness_param, offset_shift, coefficient, matching_target[None], target_other[None],
        *blocks, picture_projector, text_projector,
    )
    cap_sib, img_far, img_extra, kept, from_own, blocks = lax.optimization_barrier(
        (cap_sib, img_far, img_extra, kept, from_own, blocks)
    )
    cap_sib_other = swap_cores(cap_sib)
    img_far_other = swap_cores(img_far)
    img_extra_other = swap_cores(img_extra)
    order, turned = turn_own(role, row_code(), *blocks)
    parts = arrived_part(
        role, sharpness_param, offset_shift, coefficient,
        cap_sib, cap_sib_other, img_far, img_far_other, img_extra, img_extra_other,
        picture_projector, text_projector, order, *kept, turned, from_own,
    )

    one = [parts[0]] + [first_axis(parts[by], by) for by in (1, 3, 2)]
    one = sum(v.astype(F32) for v in one).astype(BF16)
    pieces = [one[by * 72 : (by + 1) * 72] for by in range(4)]
    two = [pieces[0]] + [second_axis(pieces[by], by) for by in (1, 3, 2)]
    two = sum(v.astype(F32) for v in two).astype(BF16).reshape(NZ, 81, 128)
    three = lax.all_to_all(two, AXES, 0, 0, axis_index_groups=ALONG_Z)
    mine = jnp.sum(three.astype(F32), axis=0)

    first = core == 0
    ring, cross = pass_on(mine), pass_across(mine)
    home = core == y_hi
    image_piece = jnp.where(home & first, mine, jnp.where(home | first, ring, cross))
    caption_piece = jnp.where(home & first, ring, jnp.where(home, mine, jnp.where(first, cross, ring)))
    both = jnp.stack([image_piece, caption_piece])
    return join_rows(role, both, *[along_x(both, by) for by in (1, 2, 3)])


def solution(mesh):
    placed = (
        P(("dp", "replica"), None),
        P(("dp", "replica"), None),
        P(),
        P(),
        P(("dp", "replica")),
        P(),
        P(),
        P(),
    )
    return jax.shard_map(
        local, mesh=mesh, in_specs=placed, out_specs=(P("dp", None), P("dp", None)), check_vma=False
    )
```

```python
import jax
import jax.numpy as jnp
import numpy as np
from jax import lax
from jax.experimental import pallas as pl
from jax.experimental.pallas import tpu as pltpu
from jax.sharding import PartitionSpec as P

AXES = ("dp", "replica")
NX, NY, NZ = 4, 4, 8
R, D, PAD = 224, 1152, 256
F32, BF16 = jnp.float32, jnp.bfloat16


def device_at(x, y, z, core):
    x, y, z = x % NX, y % NY, z % NZ
    return (z * 4 + (y % 2) * 2 + core) * 8 + x * 2 + y // 2


PLACES = [(x, y, z, c) for x in range(NX) for y in range(NY) for z in range(NZ) for c in range(2)]


ALONG_Z = [[device_at(x, y, z, c) for z in range(NZ)] for x in range(NX) for y in range(NY) for c in range(2)]


def moved(value, to):
    pairs = []
    for place in PLACES:
        target = to(*place)
        if target is not None:
            pairs.append((device_at(*place), device_at(*target)))
    return lax.ppermute(value, AXES, pairs)


def swap_cores(value):
    return moved(value, lambda x, y, z, c: (x, y, z, 1 - c))


def swap_chips(value):
    return moved(value, lambda x, y, z, c: (x, y ^ 1, z, c))


def image_to_neighbour(value):
    return moved(value, lambda x, y, z, c: (x, y, z - 1, c) if y % 2 == 0 else (x, y, z + 1, c))


def first_axis(value, by):
    return moved(value, lambda x, y, z, c: (x + by, y, z, c) if c == 0 else (x, y + by, z, c))


def second_axis(value, by):
    return moved(value, lambda x, y, z, c: (x, y + by, z, c) if c == 0 else (x + by, y, z, c))


def along_x(value, by):
    return moved(value, lambda x, y, z, c: (x + by, y, z, c))


def pass_on(value):
    def to(x, y, z, c):
        if c == y // 2:
            return (x, y ^ 2, z, c)
        return (x, y, z, 1 - c)

    return moved(value, to)


def pass_across(value):
    return moved(value, lambda x, y, z, c: (x, y ^ 2, z, 1 - c) if c != y // 2 else None)


def image_down(value):
    return moved(value, lambda x, y, z, c: (x, y, z - 1, c) if y % 2 == 1 and c == 0 else None)


THIRDS = [(n, 384) for n in range(0, D, 384)]


IMAGE_AT = np.array([[0, 1, 4, 5, 100], [2, 3, -2, -1, 6]])
CAPTION_AT = np.array([[0, 1, 2, 3], [2, 3, 0, 1]])
APART = CAPTION_AT[:, None, :] - IMAGE_AT[:, :, None]
TAKEN = ((APART >= -3) & (APART <= 2)).astype(float).tolist()


def row_code():
    rows = np.arange(D)
    base = rows // 9 % 8 * 144 + rows % 9
    return (base + (rows // 288 << 12) + (rows // 72 % 4 << 14)).astype(np.int32)[:, None]


def nt_dot(a, b):
    return lax.dot_general(a, b, (((1,), (1,)), ((), ())), preferred_element_type=F32)


def fetch(src, dst, sem):
    copy = pltpu.make_async_copy(src, dst, sem)
    copy.start()
    return copy


def by_role(place_ref, choices, sems):
    waits = []
    for k, (zero, one, dst) in enumerate(choices):

        @pl.when(place_ref[0] == 0)
        def _():
            fetch(zero, dst, sems.at[k])

        @pl.when(place_ref[0] == 1)
        def _():
            fetch(one, dst, sems.at[k])

        waits.append(pltpu.make_async_copy(zero, dst, sems.at[k]))
    return waits


def project(feats, head, tmp, rows):
    squares = jnp.zeros((rows, 1), F32)
    for n, w in THIRDS:
        p = jnp.dot(feats, head[:, n : n + w], preferred_element_type=F32)
        tmp[0:rows, n : n + w] = p
        squares = squares + jnp.sum(p * p, axis=1, keepdims=True)
    return lax.rsqrt(squares + 1e-6)


def one_hot(place_ref, code_ref, pv):
    core, x, y = place_ref[0], place_ref[2], place_ref[3]
    for n, w in THIRDS:
        code = code_ref[n : n + w]
        one, two = (code >> 12) & 3, (code >> 14) & 3
        to_x = (x + jnp.where(core == 0, one, two)) & 3
        to_y = (y + jnp.where(core == 0, two, one)) & 3
        order = (code & 4095) + (to_y & 1) * 72 + (to_y >> 1) * 36 + to_x * 9
        pv[n : n + w] = jnp.where(lax.broadcasted_iota(jnp.int32, (w, D), 1) == order, 1.0, 0.0).astype(BF16)


def pair_weights(scalars, rows, cols, xs, height, ys, scale_of, gs, label=None):
    sharpness, shift = scalars
    logits = nt_dot(rows, cols) * sharpness + shift
    for i, x in enumerate(xs):
        for j, y in enumerate(ys):
            part = logits[i * height : (i + 1) * height, j * PAD : (j + 1) * PAD]
            scale = scale_of(x, y)
            if label is not None and x == y:
                match = label(x)
                g = jnp.where(match, -scale, scale) * jax.nn.sigmoid(jnp.where(match, -part, part))
            else:
                g = scale * jax.nn.sigmoid(part)
            gs[i * height : (i + 1) * height, j * PAD : (j + 1) * PAD] = g.astype(BF16)


def own_kernel(
    place_ref, sharp_ref, shift_ref, coef_ref, mine_ref, other_ref, im, io, cm, co, wi, wc,
    zx_out, zy_out, ux_out, ix_out, dz_out,
    f, w, tmp, zx, zy, ux, ix, gs, dz, targets, sems,
):
    core = place_ref[0]
    first = by_role(
        place_ref, [(im, co, f.at[0, pl.ds(0, R)]), (io, cm, f.at[0, pl.ds(R, R)]), (wi, wc, w.at[0])],
        sems.at[pl.ds(0, 3)],
    )
    second = by_role(
        place_ref, [(cm, io, f.at[1, pl.ds(0, R)]), (co, im, f.at[1, pl.ds(R, R)]), (wc, wi, w.at[1])],
        sems.at[pl.ds(3, 3)],
    )
    targets[...] = jnp.full((2, PAD), -1, jnp.int32)
    targets[0:1, 0:R] = jnp.where(core == 0, mine_ref[...], other_ref[...])
    targets[1:2, 0:R] = jnp.where(core == 0, other_ref[...], mine_ref[...])
    for wait in first:
        wait.wait()
    inv = project(f[0], w.at[0], tmp, 2 * R)
    ix[...] = jnp.broadcast_to(inv, (2 * R, 128))
    unit = tmp[...] * inv
    ux[...] = unit
    zx[...] = unit.astype(BF16)
    outs = [fetch(ux, ux_out, sems.at[6]), fetch(zx, zx_out, sems.at[7]), fetch(ix, ix_out, sems.at[8])]
    for wait in second:
        wait.wait()
    inv = project(f[1], w.at[1], tmp, 2 * R)
    for b in range(2):
        zy[b * PAD : b * PAD + R] = (tmp[b * R : (b + 1) * R] * inv[b * R : (b + 1) * R]).astype(BF16)
        zy[b * PAD + R : (b + 1) * PAD] = jnp.zeros((PAD - R, D), BF16)
    outs.append(fetch(zy, zy_out, sems.at[10]))

    def label(k):
        down, across = lax.broadcasted_iota(jnp.int32, (R, PAD), 0), lax.broadcasted_iota(jnp.int32, (R, PAD), 1)
        by_row = jnp.broadcast_to(targets[k : k + 1], (R, PAD))
        by_col = jnp.sum(jnp.where(down == across, by_row, 0), axis=1, keepdims=True)
        target = jnp.where(core == 0, jnp.broadcast_to(by_col, (R, PAD)), by_row)
        return jnp.where(core == 0, across, down) == target

    scalars = (sharp_ref[0], shift_ref[0])
    pair_weights(scalars, zx[...], zy[...], (0, 1), R, (0, 1), lambda x, y: coef_ref[0], gs, label)

    @pl.loop(0, 3)
    def _(k):
        cols = pl.ds(pl.multiple_of(k * 384, 384), 384)
        dz[:, cols] = sharp_ref[0] * jnp.dot(gs[...], zy[:, cols], preferred_element_type=F32)

    outs.append(fetch(dz, dz_out, sems.at[11]))

    for copy in outs:
        copy.wait()


def own_part(place, sharp, shift, coef, mine, other, *operands):
    smem = pl.BlockSpec(memory_space=pltpu.SMEM)
    vmem = pl.BlockSpec(memory_space=pltpu.VMEM)
    hbm = pl.BlockSpec(memory_space=pl.ANY)
    results = [
        ((2 * R, D), BF16), ((2 * PAD, D), BF16), ((2 * R, D), F32), ((2 * R, 128), F32),
        ((2 * R, D), F32),
    ]
    return pl.pallas_call(
        own_kernel,
        out_shape=[jax.ShapeDtypeStruct(*result) for result in results],
        in_specs=[smem] * 4 + [vmem] * 2 + [hbm] * 6,
        out_specs=[hbm] * 5,
        scratch_shapes=[
            pltpu.VMEM((2, 2 * R, D), BF16),
            pltpu.VMEM((2, D, D), BF16),
            pltpu.VMEM((2 * R, D), F32),
            pltpu.VMEM((2 * R, D), BF16),
            pltpu.VMEM((2 * PAD, D), BF16),
            pltpu.VMEM((2 * R, D), F32),
            pltpu.VMEM((2 * R, 128), F32),
            pltpu.VMEM((2 * R, 2 * PAD), BF16),
            pltpu.VMEM((2 * R, D), F32),
            pltpu.VMEM((2, PAD), jnp.int32),
            pltpu.SemaphoreType.DMA((13,)),
        ],
        compiler_params=pltpu.CompilerParams(vmem_limit_bytes=60 * 2**20),
        cost_estimate=pl.CostEstimate(flops=6 * 10**9, bytes_accessed=16 * 10**6, transcendentals=500000),
    )(place, sharp, shift, coef, mine, other, *operands)


def turn_kernel(place_ref, code_ref, im, io, cm, co, pv_out, ft_out, f, pv, ft, sems):
    feats = by_role(
        place_ref, [(im, co, f.at[pl.ds(0, R)]), (io, cm, f.at[pl.ds(R, R)])], sems.at[pl.ds(0, 2)]
    )
    one_hot(place_ref, code_ref, pv)
    outs = [fetch(pv, pv_out, sems.at[2])]
    for wait in feats:
        wait.wait()

    @pl.loop(0, 3)
    def _(k):
        rows = pl.ds(pl.multiple_of(k * 384, 384), 384)
        ft[rows, 0 : 2 * R] = nt_dot(pv[rows], f[...]).astype(BF16)

    ft[:, 2 * R :] = jnp.zeros((D, 2 * PAD - 2 * R), BF16)
    for copy in outs + [fetch(ft, ft_out, sems.at[3])]:
        copy.wait()


def turn_own(place, code, *operands):
    hbm = pl.BlockSpec(memory_space=pl.ANY)
    return pl.pallas_call(
        turn_kernel,
        out_shape=[jax.ShapeDtypeStruct((D, D), BF16), jax.ShapeDtypeStruct((D, 2 * PAD), BF16)],
        in_specs=[pl.BlockSpec(memory_space=pltpu.SMEM), pl.BlockSpec(memory_space=pltpu.VMEM)] + [hbm] * 4,
        out_specs=[hbm] * 2,
        scratch_shapes=[
            pltpu.VMEM((2 * R, D), BF16),
            pltpu.VMEM((D, D), BF16),
            pltpu.VMEM((D, 2 * PAD), BF16),
            pltpu.SemaphoreType.DMA((4,)),
        ],
        compiler_params=pltpu.CompilerParams(vmem_limit_bytes=60 * 2**20),
        cost_estimate=pl.CostEstimate(flops=2 * 10**9, bytes_accessed=6 * 10**6, transcendentals=0),
    )(place, code, *operands)


def arrived_kernel(
    place_ref, sharp_ref, shift_ref, coef_ref,
    sm, so, fm, fo, em, eo, wi, wc, order, zx_in, zy_in, ux_in, ix_in, ft_in, dz_in,
    out0, out1, out2, out3,
    f, w, pv, zx, z, uo, ua, io_, ia, fto, fta, dz, da, gs, dp, sems,
):
    role, y_lo = place_ref[0], place_ref[1]
    scalars = (sharp_ref[0], shift_ref[0])

    def slot(k):
        return f.at[pl.ds(k * PAD, R)]

    rows_first = by_role(place_ref, [(fm, so, slot(0)), (fo, sm, slot(1)), (wi, wc, w.at[0])], sems.at[pl.ds(0, 3)])

    @pl.when(role == 0)
    def _():
        fetch(em, slot(2), sems.at[6])

    @pl.when(role == 1)
    def _():
        fetch(eo, slot(5), sems.at[6])
        f[2 * PAD : 3 * PAD] = jnp.zeros((PAD, D), BF16)

    for s in range(6):
        f[s * PAD + R : (s + 1) * PAD] = jnp.zeros((PAD - R, D), BF16)
    dp[2 * R : 2 * PAD] = jnp.zeros((2 * (PAD - R), D), BF16)
    for wait in rows_first + [pltpu.make_async_copy(em, slot(2), sems.at[6])]:
        wait.wait()
    cols_next = by_role(place_ref, [(sm, fo, slot(3)), (so, fm, slot(4)), (wc, wi, w.at[1])], sems.at[pl.ds(3, 3)])

    def unit_rows(start, m, side, base):
        inv = project(f[start : start + m], w.at[side], da, m)
        unit = da[0:m] * inv
        z[base : base + m] = unit.astype(BF16)
        if side == 0:
            ua[0:m] = unit
            ia[0:m] = jnp.broadcast_to(inv, (m, 128))

    @pl.when(role == 0)
    def _():
        unit_rows(0, 3 * PAD, 0, 0)

    @pl.when(role == 1)
    def _():
        unit_rows(0, 2 * PAD, 0, 0)

    for wait in cols_next:
        wait.wait()
    order_copy = fetch(order, pv, sems.at[7])
    late = [
        fetch(zx_in, zx, sems.at[8]),
        fetch(zy_in, z.at[pl.ds(3 * PAD, 2 * PAD)], sems.at[9]),
        fetch(ux_in, uo, sems.at[10]),
        fetch(ix_in, io_, sems.at[11]),
        fetch(dz_in, dz, sems.at[12]),
        fetch(ft_in, fto, sems.at[13]),
    ]

    @pl.when(role == 0)
    def _():
        unit_rows(3 * PAD, 2 * PAD, 1, 5 * PAD)

    @pl.when(role == 1)
    def _():
        unit_rows(3 * PAD, 3 * PAD, 1, 5 * PAD)

    order_copy.wait()

    @pl.loop(0, 3)
    def _(k):
        rows = pl.ds(pl.multiple_of(k * 384, 384), 384)
        fta[rows] = nt_dot(pv[rows], f[0 : 3 * PAD]).astype(BF16)

    for copy in late:
        copy.wait()

    def spread(m, cols, y0, y1, kept, unit, inverse, base):
        for n, wd in THIRDS:
            d = scalars[0] * jnp.dot(gs[0:m, 0:cols], z[y0 * PAD : y1 * PAD, n : n + wd], preferred_element_type=F32)
            if kept:
                d = d + dz[:, n : n + wd]
            da[0:m, n : n + wd] = d

        along = jnp.sum(da[0:m] * unit[0:m], axis=1, keepdims=True)
        dp[base : base + m] = ((da[0:m] - unit[0:m] * along) * inverse[0:m, 0:1]).astype(BF16)

    def scale(image, caption):
        return coef_ref[0] * jnp.where(y_lo == 0, TAKEN[0][image][caption], TAKEN[1][image][caption])

    def by_image(x, y):
        return scale(x, y)

    def by_caption(x, y):
        return scale(y, x)

    @pl.when(role == 0)
    def _():
        pair_weights(scalars, zx[...], z[5 * PAD : 7 * PAD], (0, 1), R, (2, 3), by_image, gs)
        spread(2 * R, 2 * PAD, 5, 7, True, uo, io_, 0)
        pair_weights(scalars, z[0 : 2 * PAD], z[4 * PAD : 7 * PAD], (2, 3), PAD, (1, 2, 3), by_image, gs)
        spread(2 * PAD, 3 * PAD, 4, 7, False, ua, ia, 2 * PAD)
        pair_weights(scalars, z[2 * PAD : 3 * PAD], z[4 * PAD : 5 * PAD], (4,), PAD, (1,), by_image, gs)
        spread(PAD, PAD, 4, 5, False, ua.at[2 * PAD : 3 * PAD], ia.at[2 * PAD : 3 * PAD], 4 * PAD)

    @pl.when(role == 1)
    def _():
        pair_weights(scalars, zx[...], z[5 * PAD : 8 * PAD], (0, 1), R, (2, 3, 4), by_caption, gs)
        spread(2 * R, 3 * PAD, 5, 8, True, uo, io_, 0)
        pair_weights(scalars, z[0 : 2 * PAD], z[3 * PAD : 7 * PAD], (2, 3), PAD, (0, 1, 2, 3), by_caption, gs)
        spread(2 * PAD, 4 * PAD, 3, 7, False, ua, ia, 2 * PAD)
        dp[4 * PAD : 5 * PAD] = jnp.zeros((PAD, D), BF16)

    @pl.loop(0, 3)
    def _(k):
        at = pl.ds(pl.multiple_of(k * 384, 384), 384)
        own = dp[0 : 2 * PAD, at]
        rest = dp[2 * PAD : 5 * PAD, at]
        for i, out in enumerate((out0, out1, out2, out3)):
            rows = slice(i * 288, (i + 1) * 288)
            out[:, at] = (
                jnp.dot(fto[rows], own, preferred_element_type=F32)
                + jnp.dot(fta[rows], rest, preferred_element_type=F32)
            ).astype(BF16)


def arrived_part(place, sharp, shift, coef, *operands):
    smem = pl.BlockSpec(memory_space=pltpu.SMEM)
    vmem = pl.BlockSpec(memory_space=pltpu.VMEM)
    return pl.pallas_call(
        arrived_kernel,
        out_shape=[jax.ShapeDtypeStruct((D // 4, D), BF16)] * 4,
        in_specs=[smem] * 4 + [pl.BlockSpec(memory_space=pl.ANY)] * 15,
        out_specs=[vmem] * 4,
        scratch_shapes=[
            pltpu.VMEM((6 * PAD, D), BF16),
            pltpu.VMEM((2, D, D), BF16),
            pltpu.VMEM((D, D), BF16),
            pltpu.VMEM((2 * R, D), BF16),
            pltpu.VMEM((8 * PAD, D), BF16),
            pltpu.VMEM((2 * R, D), F32),
            pltpu.VMEM((3 * PAD, D), F32),
            pltpu.VMEM((2 * R, 128), F32),
            pltpu.VMEM((3 * PAD, 128), F32),
            pltpu.VMEM((D, 2 * PAD), BF16),
            pltpu.VMEM((D, 3 * PAD), BF16),
            pltpu.VMEM((2 * R, D), F32),
            pltpu.VMEM((3 * PAD, D), F32),
            pltpu.VMEM((3 * PAD, 4 * PAD), BF16),
            pltpu.VMEM((5 * PAD, D), BF16),
            pltpu.SemaphoreType.DMA((14,)),
        ],
        compiler_params=pltpu.CompilerParams(vmem_limit_bytes=60 * 2**20),
        cost_estimate=pl.CostEstimate(flops=14 * 10**9, bytes_accessed=20 * 10**6, transcendentals=800000),
    )(place, sharp, shift, coef, *operands)


def join_kernel(place_ref, one, two, three, four, image_out, caption_out, held):
    for k, piece in enumerate((one, two, three, four)):
        held[k] = piece[...]
    for place in range(NX):
        back = (place_ref[2] - place) & 3
        for head, out in enumerate((image_out, caption_out)):
            for row in range(9):
                at = place * 9 + row
                for n in range(9):
                    out[at : at + 1, n * 128 : (n + 1) * 128] = held[back, head, row * 9 + n : row * 9 + n + 1]


def join_rows(place, *pieces):
    vmem = pl.BlockSpec(memory_space=pltpu.VMEM)
    return pl.pallas_call(
        join_kernel,
        out_shape=[jax.ShapeDtypeStruct((36, D), F32)] * 2,
        in_specs=[pl.BlockSpec(memory_space=pltpu.SMEM)] + [vmem] * 4,
        out_specs=[vmem] * 2,
        scratch_shapes=[pltpu.VMEM((4, 2, 81, 128), F32)],
    )(place, *pieces)


def local(
    picture_encoder_features,
    text_encoder_features,
    picture_projector,
    text_projector,
    matching_target,
    sharpness_param,
    offset_shift,
    objective_multiplier,
):
    place = lax.axis_index("dp")
    core, y_lo = place % 2, (place // 2) % 2
    x, y_hi = lax.axis_index("replica") // 2, lax.axis_index("replica") % 2
    y = y_hi * 2 + y_lo
    role = jnp.stack([core, y_lo, x, y]).astype(jnp.int32)
    coefficient = objective_multiplier / (lax.axis_size("dp") * R)

    own_img = swap_cores(picture_encoder_features)
    own_cap = swap_cores(text_encoder_features)
    target_other = swap_cores(matching_target)
    cap, img, target_other = lax.optimization_barrier(
        (text_encoder_features, picture_encoder_features, target_other)
    )
    cap_sib = swap_chips(cap)
    img_far = image_to_neighbour(img)
    img_extra = image_down(img)

    blocks = (picture_encoder_features, own_img, text_encoder_features, own_cap)
    *kept, from_own = own_part(
        role, sharpness_param, offset_shift, coefficient, matching_target[None], target_other[None],
        *blocks, picture_projector, text_projector,
    )
    cap_sib, img_far, img_extra, kept, from_own, blocks = lax.optimization_barrier(
        (cap_sib, img_far, img_extra, kept, from_own, blocks)
    )
    cap_sib_other = swap_cores(cap_sib)
    img_far_other = swap_cores(img_far)
    img_extra_other = swap_cores(img_extra)
    order, turned = turn_own(role, row_code(), *blocks)
    parts = arrived_part(
        role, sharpness_param, offset_shift, coefficient,
        cap_sib, cap_sib_other, img_far, img_far_other, img_extra, img_extra_other,
        picture_projector, text_projector, order, *kept, turned, from_own,
    )

    one = [parts[0]] + [first_axis(parts[by], by) for by in (1, 3, 2)]
    one = sum(v.astype(F32) for v in one).astype(BF16)
    pieces = [one[by * 72 : (by + 1) * 72] for by in range(4)]
    two = [pieces[0]] + [second_axis(pieces[by], by) for by in (1, 3, 2)]
    two = sum(v.astype(F32) for v in two).astype(BF16).reshape(NZ, 81, 128)
    three = lax.all_to_all(two, AXES, 0, 0, axis_index_groups=ALONG_Z)
    mine = jnp.sum(three.astype(F32), axis=0)

    first = core == 0
    ring, cross = pass_on(mine), pass_across(mine)
    home = core == y_hi
    image_piece = jnp.where(home & first, mine, jnp.where(home | first, ring, cross))
    caption_piece = jnp.where(home & first, ring, jnp.where(home, mine, jnp.where(first, cross, ring)))
    both = jnp.stack([image_piece, caption_piece])
    return join_rows(role, both, *[along_x(both, by) for by in (1, 2, 3)])


def solution(mesh):
    placed = (
        P(("dp", "replica"), None),
        P(("dp", "replica"), None),
        P(),
        P(),
        P(("dp", "replica")),
        P(),
        P(),
        P(),
    )
    return jax.shard_map(
        local, mesh=mesh, in_specs=placed, out_specs=(P("dp", None), P("dp", None)), check_vma=False
    )
```

```python
import jax
import jax.numpy as jnp
import numpy as np
from jax import lax
from jax.experimental import pallas as pl
from jax.experimental.pallas import tpu as pltpu
from jax.sharding import PartitionSpec as P

AXES = ("dp", "replica")
NX, NY, NZ = 4, 4, 8
R, D, PAD = 224, 1152, 256
F32, BF16 = jnp.float32, jnp.bfloat16


def device_at(x, y, z, core):
    x, y, z = x % NX, y % NY, z % NZ
    return (z * 4 + (y % 2) * 2 + core) * 8 + x * 2 + y // 2


PLACES = [(x, y, z, c) for x in range(NX) for y in range(NY) for z in range(NZ) for c in range(2)]


ALONG_Z = [[device_at(x, y, z, c) for z in range(NZ)] for x in range(NX) for y in range(NY) for c in range(2)]


def moved(value, to):
    pairs = []
    for place in PLACES:
        target = to(*place)
        if target is not None:
            pairs.append((device_at(*place), device_at(*target)))
    return lax.ppermute(value, AXES, pairs)


def swap_cores(value):
    return moved(value, lambda x, y, z, c: (x, y, z, 1 - c))


def swap_chips(value):
    return moved(value, lambda x, y, z, c: (x, y ^ 1, z, c))


def image_to_neighbour(value):
    return moved(value, lambda x, y, z, c: (x, y, z - 1, c) if y % 2 == 0 else (x, y, z + 1, c))


def first_axis(value, by):
    return moved(value, lambda x, y, z, c: (x + by, y, z, c) if c == 0 else (x, y + by, z, c))


def second_axis(value, by):
    return moved(value, lambda x, y, z, c: (x, y + by, z, c) if c == 0 else (x + by, y, z, c))


def along_x(value, by):
    return moved(value, lambda x, y, z, c: (x + by, y, z, c))


def pass_on(value):
    def to(x, y, z, c):
        if c == y // 2:
            return (x, y ^ 2, z, c)
        return (x, y, z, 1 - c)

    return moved(value, to)


def pass_across(value):
    return moved(value, lambda x, y, z, c: (x, y ^ 2, z, 1 - c) if c != y // 2 else None)


def image_down(value):
    return moved(value, lambda x, y, z, c: (x, y, z - 1, c) if y % 2 == 1 and c == 0 else None)


THIRDS = [(n, 384) for n in range(0, D, 384)]


IMAGE_AT = np.array([[0, 1, 4, 5, 100], [2, 3, -2, -1, 6]])
CAPTION_AT = np.array([[0, 1, 2, 3], [2, 3, 0, 1]])
APART = CAPTION_AT[:, None, :] - IMAGE_AT[:, :, None]
TAKEN = ((APART >= -3) & (APART <= 2)).astype(float).tolist()


def nt_dot(a, b):
    return lax.dot_general(a, b, (((1,), (1,)), ((), ())), preferred_element_type=F32)


def fetch(src, dst, sem):
    copy = pltpu.make_async_copy(src, dst, sem)
    copy.start()
    return copy


def by_role(place_ref, choices, sems):
    waits = []
    for k, (zero, one, dst) in enumerate(choices):

        @pl.when(place_ref[0] == 0)
        def _():
            fetch(zero, dst, sems.at[k])

        @pl.when(place_ref[0] == 1)
        def _():
            fetch(one, dst, sems.at[k])

        waits.append(pltpu.make_async_copy(zero, dst, sems.at[k]))
    return waits


def project(feats, head, tmp, rows, squares):
    squares[0:rows] = jnp.zeros((rows, 128), F32)

    @pl.loop(0, 3)
    def _(k):
        at = pl.ds(pl.multiple_of(k * 384, 384), 384)
        p = jnp.dot(feats[0:rows], head[:, at], preferred_element_type=F32)
        tmp[0:rows, at] = p
        p = p * p
        squares[0:rows] += p[:, 0:128] + p[:, 128:256] + p[:, 256:384]

    return lax.rsqrt(jnp.sum(squares[0:rows], axis=1, keepdims=True) + 1e-6)


def one_hot(place_ref, pv):
    core, x, y = place_ref[0], place_ref[2], place_ref[3]

    @pl.loop(0, 3)
    def _(k):
        base = pl.multiple_of(k * 384, 384)
        row = lax.broadcasted_iota(jnp.int32, (384, 1), 0) + base
        group = (row * 7282) >> 16
        one, two = (group >> 5) & 3, (group >> 3) & 3
        to_x = (x + jnp.where(core == 0, one, two)) & 3
        to_y = (y + jnp.where(core == 0, two, one)) & 3
        order = (group & 7) * 144 + row - group * 9 + (to_y & 1) * 72 + (to_y >> 1) * 36 + to_x * 9
        hit = lax.broadcasted_iota(jnp.int32, (384, D), 1) == order
        pv[pl.ds(base, 384)] = jnp.where(hit, 1.0, 0.0).astype(BF16)


def pair_weights(scalars, rows, cols, xs, height, ys, scale_of, gs, label=None):
    sharpness, shift = scalars
    logits = nt_dot(rows, cols) * sharpness + shift
    for i, x in enumerate(xs):
        for j, y in enumerate(ys):
            part = logits[i * height : (i + 1) * height, j * PAD : (j + 1) * PAD]
            scale = scale_of(x, y)
            if label is not None and x == y:
                match = label(x)
                g = jnp.where(match, -scale, scale) * jax.nn.sigmoid(jnp.where(match, -part, part))
            else:
                g = scale * jax.nn.sigmoid(part)
            gs[i * height : (i + 1) * height, j * PAD : (j + 1) * PAD] = g.astype(BF16)


def own_kernel(
    place_ref, sharp_ref, shift_ref, coef_ref, mine_ref, other_ref, im, io, cm, co, wi, wc,
    zx_out, zy_out, ux_out, ix_out, dz_out,
    f, w, tmp, zx, zy, ux, ix, squares, gs, dz, targets, sems,
):
    core = place_ref[0]
    first = by_role(
        place_ref, [(im, co, f.at[0, pl.ds(0, R)]), (io, cm, f.at[0, pl.ds(R, R)]), (wi, wc, w.at[0])],
        sems.at[pl.ds(0, 3)],
    )
    second = by_role(
        place_ref, [(cm, io, f.at[1, pl.ds(0, R)]), (co, im, f.at[1, pl.ds(R, R)]), (wc, wi, w.at[1])],
        sems.at[pl.ds(3, 3)],
    )
    targets[...] = jnp.full((2, PAD), -1, jnp.int32)
    targets[0:1, 0:R] = jnp.where(core == 0, mine_ref[...], other_ref[...])
    targets[1:2, 0:R] = jnp.where(core == 0, other_ref[...], mine_ref[...])
    for wait in first:
        wait.wait()
    inv = project(f.at[0], w.at[0], tmp, 2 * R, ix)
    ix[...] = jnp.broadcast_to(inv, (2 * R, 128))
    unit = tmp[...] * inv
    ux[...] = unit
    zx[...] = unit.astype(BF16)
    outs = [fetch(ux, ux_out, sems.at[6]), fetch(zx, zx_out, sems.at[7]), fetch(ix, ix_out, sems.at[8])]
    for wait in second:
        wait.wait()
    inv = project(f.at[1], w.at[1], tmp, 2 * R, squares)
    for b in range(2):
        zy[b * PAD : b * PAD + R] = (tmp[b * R : (b + 1) * R] * inv[b * R : (b + 1) * R]).astype(BF16)
        zy[b * PAD + R : (b + 1) * PAD] = jnp.zeros((PAD - R, D), BF16)
    outs.append(fetch(zy, zy_out, sems.at[10]))

    def label(k):
        down, across = lax.broadcasted_iota(jnp.int32, (R, PAD), 0), lax.broadcasted_iota(jnp.int32, (R, PAD), 1)
        by_row = jnp.broadcast_to(targets[k : k + 1], (R, PAD))
        by_col = jnp.sum(jnp.where(down == across, by_row, 0), axis=1, keepdims=True)
        target = jnp.where(core == 0, jnp.broadcast_to(by_col, (R, PAD)), by_row)
        return jnp.where(core == 0, across, down) == target

    scalars = (sharp_ref[0], shift_ref[0])
    pair_weights(scalars, zx[...], zy[...], (0, 1), R, (0, 1), lambda x, y: coef_ref[0], gs, label)

    @pl.loop(0, 3)
    def _(k):
        cols = pl.ds(pl.multiple_of(k * 384, 384), 384)
        dz[:, cols] = sharp_ref[0] * jnp.dot(gs[...], zy[:, cols], preferred_element_type=F32)

    outs.append(fetch(dz, dz_out, sems.at[11]))

    for copy in outs:
        copy.wait()


def own_part(place, sharp, shift, coef, mine, other, *operands):
    smem = pl.BlockSpec(memory_space=pltpu.SMEM)
    vmem = pl.BlockSpec(memory_space=pltpu.VMEM)
    hbm = pl.BlockSpec(memory_space=pl.ANY)
    results = [
        ((2 * R, D), BF16), ((2 * PAD, D), BF16), ((2 * R, D), F32), ((2 * R, 128), F32),
        ((2 * R, D), F32),
    ]
    return pl.pallas_call(
        own_kernel,
        out_shape=[jax.ShapeDtypeStruct(*result) for result in results],
        in_specs=[smem] * 4 + [vmem] * 2 + [hbm] * 6,
        out_specs=[hbm] * 5,
        scratch_shapes=[
            pltpu.VMEM((2, 2 * R, D), BF16),
            pltpu.VMEM((2, D, D), BF16),
            pltpu.VMEM((2 * R, D), F32),
            pltpu.VMEM((2 * R, D), BF16),
            pltpu.VMEM((2 * PAD, D), BF16),
            pltpu.VMEM((2 * R, D), F32),
            pltpu.VMEM((2 * R, 128), F32),
            pltpu.VMEM((2 * R, 128), F32),
            pltpu.VMEM((2 * R, 2 * PAD), BF16),
            pltpu.VMEM((2 * R, D), F32),
            pltpu.VMEM((2, PAD), jnp.int32),
            pltpu.SemaphoreType.DMA((13,)),
        ],
        compiler_params=pltpu.CompilerParams(vmem_limit_bytes=60 * 2**20),
        cost_estimate=pl.CostEstimate(flops=6 * 10**9, bytes_accessed=16 * 10**6, transcendentals=500000),
    )(place, sharp, shift, coef, mine, other, *operands)


def turn_kernel(place_ref, im, io, cm, co, pv_out, ft_out, f, pv, ft, sems):
    feats = by_role(
        place_ref, [(im, co, f.at[pl.ds(0, R)]), (io, cm, f.at[pl.ds(R, R)])], sems.at[pl.ds(0, 2)]
    )
    one_hot(place_ref, pv)
    outs = [fetch(pv, pv_out, sems.at[2])]
    for wait in feats:
        wait.wait()

    @pl.loop(0, 3)
    def _(k):
        rows = pl.ds(pl.multiple_of(k * 384, 384), 384)
        ft[rows, 0 : 2 * R] = nt_dot(pv[rows], f[...]).astype(BF16)

    ft[:, 2 * R :] = jnp.zeros((D, 2 * PAD - 2 * R), BF16)
    for copy in outs + [fetch(ft, ft_out, sems.at[3])]:
        copy.wait()


def turn_own(place, *operands):
    hbm = pl.BlockSpec(memory_space=pl.ANY)
    return pl.pallas_call(
        turn_kernel,
        out_shape=[jax.ShapeDtypeStruct((D, D), BF16), jax.ShapeDtypeStruct((D, 2 * PAD), BF16)],
        in_specs=[pl.BlockSpec(memory_space=pltpu.SMEM)] + [hbm] * 4,
        out_specs=[hbm] * 2,
        scratch_shapes=[
            pltpu.VMEM((2 * R, D), BF16),
            pltpu.VMEM((D, D), BF16),
            pltpu.VMEM((D, 2 * PAD), BF16),
            pltpu.SemaphoreType.DMA((4,)),
        ],
        compiler_params=pltpu.CompilerParams(vmem_limit_bytes=60 * 2**20),
        cost_estimate=pl.CostEstimate(flops=2 * 10**9, bytes_accessed=6 * 10**6, transcendentals=0),
    )(place, *operands)


def arrived_kernel(
    place_ref, sharp_ref, shift_ref, coef_ref,
    sm, so, fm, fo, em, eo, wi, wc, order, zx_in, zy_in, ux_in, ix_in, ft_in, dz_in,
    out0, out1, out2, out3,
    fi, fc, w, pv, zx, z, uo, ui, uc, io_, ii, ic, fto, fta, dz, da, gs, dp, sems,
):
    role, y_lo = place_ref[0], place_ref[1]
    scalars = (sharp_ref[0], shift_ref[0])

    def slot(blocks, k):
        return blocks.at[pl.ds(k * PAD, R)]

    images = by_role(place_ref, [(fm, fo, slot(fi, 0)), (fo, fm, slot(fi, 1)), (em, eo, slot(fi, 2))], sems.at[pl.ds(0, 3)])
    images.append(fetch(wi, w.at[0], sems.at[3]))
    for s in range(3):
        fi[s * PAD + R : (s + 1) * PAD] = jnp.zeros((PAD - R, D), BF16)
    for s in range(2):
        fc[s * PAD + R : (s + 1) * PAD] = jnp.zeros((PAD - R, D), BF16)
    dp[2 * R : 2 * PAD] = jnp.zeros((2 * (PAD - R), D), BF16)
    for wait in images:
        wait.wait()
    captions = by_role(place_ref, [(sm, so, slot(fc, 0)), (so, sm, slot(fc, 1))], sems.at[pl.ds(4, 2)])
    captions.append(fetch(wc, w.at[1], sems.at[6]))

    def unit_rows(feats, head, unit, inverse, m, base):
        inv = project(feats, head, unit, m, inverse)
        inverse[...] = jnp.broadcast_to(inv, (m, 128))
        unit[...] = unit[...] * inv
        z[pl.ds(pl.multiple_of(base, PAD), m)] = unit[...].astype(BF16)

    unit_rows(fi, w.at[0], ui, ii, 3 * PAD, role * 5 * PAD)
    for wait in captions:
        wait.wait()
    order_copy = fetch(order, pv, sems.at[7])
    late = [
        fetch(zx_in, zx, sems.at[8]),
        fetch(zy_in, z.at[pl.ds(3 * PAD, 2 * PAD)], sems.at[9]),
        fetch(ux_in, uo, sems.at[10]),
        fetch(ix_in, io_, sems.at[11]),
        fetch(dz_in, dz, sems.at[12]),
        fetch(ft_in, fto, sems.at[13]),
    ]
    unit_rows(fc, w.at[1], uc, ic, 2 * PAD, (1 - role) * 5 * PAD)
    order_copy.wait()

    def turn(feats, m):
        @pl.loop(0, 3)
        def _(k):
            rows = pl.ds(pl.multiple_of(k * 384, 384), 384)
            fta[rows, 0:m] = nt_dot(pv[rows], feats[...]).astype(BF16)

    @pl.when(role == 0)
    def _():
        turn(fi, 3 * PAD)

    @pl.when(role == 1)
    def _():
        turn(fc, 2 * PAD)
        fta[:, 2 * PAD : 3 * PAD] = jnp.zeros((D, PAD), BF16)

    for copy in late:
        copy.wait()

    def spread(m, cols, y0, y1, kept, unit, inverse, base):
        @pl.loop(0, 3)
        def _(k):
            at = pl.ds(pl.multiple_of(k * 384, 384), 384)
            d = scalars[0] * jnp.dot(gs[0:m, 0:cols], z[y0 * PAD : y1 * PAD, at], preferred_element_type=F32)
            if kept:
                d = d + dz[:, at]
            da[0:m, at] = d

        along = jnp.sum(da[0:m] * unit[0:m], axis=1, keepdims=True)
        dp[base : base + m] = ((da[0:m] - unit[0:m] * along) * inverse[0:m, 0:1]).astype(BF16)

    def scale(image, caption):
        return coef_ref[0] * jnp.where(y_lo == 0, TAKEN[0][image][caption], TAKEN[1][image][caption])

    def by_image(x, y):
        return scale(x, y)

    def by_caption(x, y):
        return scale(y, x)

    @pl.when(role == 0)
    def _():
        pair_weights(scalars, zx[...], z[5 * PAD : 7 * PAD], (0, 1), R, (2, 3), by_image, gs)
        spread(2 * R, 2 * PAD, 5, 7, True, uo, io_, 0)
        pair_weights(scalars, z[0 : 2 * PAD], z[4 * PAD : 7 * PAD], (2, 3), PAD, (1, 2, 3), by_image, gs)
        spread(2 * PAD, 3 * PAD, 4, 7, False, ui, ii, 2 * PAD)
        pair_weights(scalars, z[2 * PAD : 3 * PAD], z[4 * PAD : 5 * PAD], (4,), PAD, (1,), by_image, gs)
        spread(PAD, PAD, 4, 5, False, ui.at[2 * PAD : 3 * PAD], ii.at[2 * PAD : 3 * PAD], 4 * PAD)

    @pl.when(role == 1)
    def _():
        pair_weights(scalars, zx[...], z[5 * PAD : 8 * PAD], (0, 1), R, (2, 3, 4), by_caption, gs)
        spread(2 * R, 3 * PAD, 5, 8, True, uo, io_, 0)
        pair_weights(scalars, z[0 : 2 * PAD], z[3 * PAD : 7 * PAD], (2, 3), PAD, (0, 1, 2, 3), by_caption, gs)
        spread(2 * PAD, 4 * PAD, 3, 7, False, uc, ic, 2 * PAD)
        dp[4 * PAD : 5 * PAD] = jnp.zeros((PAD, D), BF16)

    @pl.loop(0, 3)
    def _(k):
        at = pl.ds(pl.multiple_of(k * 384, 384), 384)
        own = dp[0 : 2 * PAD, at]
        rest = dp[2 * PAD : 5 * PAD, at]
        for i, out in enumerate((out0, out1, out2, out3)):
            rows = slice(i * 288, (i + 1) * 288)
            out[:, at] = (
                jnp.dot(fto[rows], own, preferred_element_type=F32)
                + jnp.dot(fta[rows], rest, preferred_element_type=F32)
            ).astype(BF16)


def arrived_part(place, sharp, shift, coef, *operands):
    smem = pl.BlockSpec(memory_space=pltpu.SMEM)
    vmem = pl.BlockSpec(memory_space=pltpu.VMEM)
    return pl.pallas_call(
        arrived_kernel,
        out_shape=[jax.ShapeDtypeStruct((D // 4, D), BF16)] * 4,
        in_specs=[smem] * 4 + [pl.BlockSpec(memory_space=pl.ANY)] * 15,
        out_specs=[vmem] * 4,
        scratch_shapes=[
            pltpu.VMEM((3 * PAD, D), BF16),
            pltpu.VMEM((2 * PAD, D), BF16),
            pltpu.VMEM((2, D, D), BF16),
            pltpu.VMEM((D, D), BF16),
            pltpu.VMEM((2 * R, D), BF16),
            pltpu.VMEM((8 * PAD, D), BF16),
            pltpu.VMEM((2 * R, D), F32),
            pltpu.VMEM((3 * PAD, D), F32),
            pltpu.VMEM((2 * PAD, D), F32),
            pltpu.VMEM((2 * R, 128), F32),
            pltpu.VMEM((3 * PAD, 128), F32),
            pltpu.VMEM((2 * PAD, 128), F32),
            pltpu.VMEM((D, 2 * PAD), BF16),
            pltpu.VMEM((D, 3 * PAD), BF16),
            pltpu.VMEM((2 * R, D), F32),
            pltpu.VMEM((3 * PAD, D), F32),
            pltpu.VMEM((3 * PAD, 4 * PAD), BF16),
            pltpu.VMEM((5 * PAD, D), BF16),
            pltpu.SemaphoreType.DMA((14,)),
        ],
        compiler_params=pltpu.CompilerParams(vmem_limit_bytes=60 * 2**20),
        cost_estimate=pl.CostEstimate(flops=14 * 10**9, bytes_accessed=20 * 10**6, transcendentals=800000),
    )(place, sharp, shift, coef, *operands)


def join_kernel(place_ref, one, two, three, four, image_out, caption_out, held):
    for k, piece in enumerate((one, two, three, four)):
        held[k] = piece[...]
    for place in range(NX):
        back = (place_ref[2] - place) & 3
        for head, out in enumerate((image_out, caption_out)):
            for row in range(9):
                at = place * 9 + row
                for n in range(9):
                    out[at : at + 1, n * 128 : (n + 1) * 128] = held[back, head, row * 9 + n : row * 9 + n + 1]


def join_rows(place, *pieces):
    vmem = pl.BlockSpec(memory_space=pltpu.VMEM)
    return pl.pallas_call(
        join_kernel,
        out_shape=[jax.ShapeDtypeStruct((36, D), F32)] * 2,
        in_specs=[pl.BlockSpec(memory_space=pltpu.SMEM)] + [vmem] * 4,
        out_specs=[vmem] * 2,
        scratch_shapes=[pltpu.VMEM((4, 2, 81, 128), F32)],
    )(place, *pieces)


def local(
    picture_encoder_features,
    text_encoder_features,
    picture_projector,
    text_projector,
    matching_target,
    sharpness_param,
    offset_shift,
    objective_multiplier,
):
    place = lax.axis_index("dp")
    core, y_lo = place % 2, (place // 2) % 2
    x, y_hi = lax.axis_index("replica") // 2, lax.axis_index("replica") % 2
    y = y_hi * 2 + y_lo
    role = jnp.stack([core, y_lo, x, y]).astype(jnp.int32)
    coefficient = objective_multiplier / (lax.axis_size("dp") * R)

    own_img = swap_cores(picture_encoder_features)
    own_cap = swap_cores(text_encoder_features)
    target_other = swap_cores(matching_target)
    cap, img, target_other = lax.optimization_barrier(
        (text_encoder_features, picture_encoder_features, target_other)
    )
    cap_sib = swap_chips(cap)
    img_far = image_to_neighbour(img)
    img_extra = image_down(img)

    blocks = (picture_encoder_features, own_img, text_encoder_features, own_cap)
    *kept, from_own = own_part(
        role, sharpness_param, offset_shift, coefficient, matching_target[None], target_other[None],
        *blocks, picture_projector, text_projector,
    )
    cap_sib, img_far, img_extra, kept, from_own, blocks = lax.optimization_barrier(
        (cap_sib, img_far, img_extra, kept, from_own, blocks)
    )
    cap_sib_other = swap_cores(cap_sib)
    img_far_other = swap_cores(img_far)
    img_extra_other = swap_cores(img_extra)
    order, turned = turn_own(role, *blocks)
    parts = arrived_part(
        role, sharpness_param, offset_shift, coefficient,
        cap_sib, cap_sib_other, img_far, img_far_other, img_extra, img_extra_other,
        picture_projector, text_projector, order, *kept, turned, from_own,
    )

    one = [parts[0]] + [first_axis(parts[by], by) for by in (1, 3, 2)]
    one = sum(v.astype(F32) for v in one).astype(BF16)
    pieces = [one[by * 72 : (by + 1) * 72] for by in range(4)]
    two = [pieces[0]] + [second_axis(pieces[by], by) for by in (1, 3, 2)]
    two = sum(v.astype(F32) for v in two).astype(BF16).reshape(NZ, 81, 128)
    three = lax.all_to_all(two, AXES, 0, 0, axis_index_groups=ALONG_Z)
    mine = jnp.sum(three.astype(F32), axis=0)

    first = core == 0
    ring, cross = pass_on(mine), pass_across(mine)
    home = core == y_hi
    image_piece = jnp.where(home & first, mine, jnp.where(home | first, ring, cross))
    caption_piece = jnp.where(home & first, ring, jnp.where(home, mine, jnp.where(first, cross, ring)))
    both = jnp.stack([image_piece, caption_piece])
    return join_rows(role, both, *[along_x(both, by) for by in (1, 2, 3)])


def solution(mesh):
    placed = (
        P(("dp", "replica"), None),
        P(("dp", "replica"), None),
        P(),
        P(),
        P(("dp", "replica")),
        P(),
        P(),
        P(),
    )
    return jax.shard_map(
        local, mesh=mesh, in_specs=placed, out_specs=(P("dp", None), P("dp", None)), check_vma=False
    )
```

```python
import jax
import jax.numpy as jnp
import numpy as np
from jax import lax
from jax.experimental import pallas as pl
from jax.experimental.pallas import tpu as pltpu
from jax.sharding import PartitionSpec as P

AXES = ("dp", "replica")
NX, NY, NZ = 4, 4, 8
R, D, PAD = 224, 1152, 256
F32, BF16 = jnp.float32, jnp.bfloat16


def device_at(x, y, z, core):
    x, y, z = x % NX, y % NY, z % NZ
    return (z * 4 + (y % 2) * 2 + core) * 8 + x * 2 + y // 2


PLACES = [(x, y, z, c) for x in range(NX) for y in range(NY) for z in range(NZ) for c in range(2)]


ALONG_Z = [[device_at(x, y, z, c) for z in range(NZ)] for x in range(NX) for y in range(NY) for c in range(2)]


def moved(value, to):
    pairs = []
    for place in PLACES:
        target = to(*place)
        if target is not None:
            pairs.append((device_at(*place), device_at(*target)))
    return lax.ppermute(value, AXES, pairs)


def swap_cores(value):
    return moved(value, lambda x, y, z, c: (x, y, z, 1 - c))


def swap_chips(value):
    return moved(value, lambda x, y, z, c: (x, y ^ 1, z, c))


def image_to_neighbour(value):
    return moved(value, lambda x, y, z, c: (x, y, z - 1, c) if y % 2 == 0 else (x, y, z + 1, c))


def first_axis(value, by):
    return moved(value, lambda x, y, z, c: (x + by, y, z, c) if c == 0 else (x, y + by, z, c))


def second_axis(value, by):
    return moved(value, lambda x, y, z, c: (x, y + by, z, c) if c == 0 else (x + by, y, z, c))


def along_x(value, by):
    return moved(value, lambda x, y, z, c: (x + by, y, z, c))


def pass_on(value):
    def to(x, y, z, c):
        if c == y // 2:
            return (x, y ^ 2, z, c)
        return (x, y, z, 1 - c)

    return moved(value, to)


def pass_across(value):
    return moved(value, lambda x, y, z, c: (x, y ^ 2, z, 1 - c) if c != y // 2 else None)


def image_down(value):
    return moved(value, lambda x, y, z, c: (x, y, z - 1, c) if y % 2 == 1 and c == 0 else None)


THIRDS = [(n, 384) for n in range(0, D, 384)]


IMAGE_AT = np.array([[0, 1, 4, 5, 100], [2, 3, -2, -1, 6]])
CAPTION_AT = np.array([[0, 1, 2, 3], [2, 3, 0, 1]])
APART = CAPTION_AT[:, None, :] - IMAGE_AT[:, :, None]
TAKEN = ((APART >= -3) & (APART <= 2)).astype(float).tolist()


def nt_dot(a, b):
    return lax.dot_general(a, b, (((1,), (1,)), ((), ())), preferred_element_type=F32)


def fetch(src, dst, sem):
    copy = pltpu.make_async_copy(src, dst, sem)
    copy.start()
    return copy


def by_role(place_ref, choices, sems):
    waits = []
    for k, (zero, one, dst) in enumerate(choices):

        @pl.when(place_ref[0] == 0)
        def _():
            fetch(zero, dst, sems.at[k])

        @pl.when(place_ref[0] == 1)
        def _():
            fetch(one, dst, sems.at[k])

        waits.append(pltpu.make_async_copy(zero, dst, sems.at[k]))
    return waits


def project(feats, head, tmp, rows):
    squares = jnp.zeros((rows, 1), F32)
    for n, w in THIRDS:
        p = jnp.dot(feats[0:rows], head[:, n : n + w], preferred_element_type=F32)
        tmp[0:rows, n : n + w] = p
        squares = squares + jnp.sum(p * p, axis=1, keepdims=True)
    return lax.rsqrt(squares + 1e-6)


def one_hot(place_ref, pv):
    core, x, y = place_ref[0], place_ref[2], place_ref[3]

    @pl.loop(0, 3)
    def _(k):
        base = pl.multiple_of(k * 384, 384)
        row = lax.broadcasted_iota(jnp.int32, (384, 1), 0) + base
        group = (row * 7282) >> 16
        one, two = (group >> 5) & 3, (group >> 3) & 3
        to_x = (x + jnp.where(core == 0, one, two)) & 3
        to_y = (y + jnp.where(core == 0, two, one)) & 3
        order = (group & 7) * 144 + row - group * 9 + (to_y & 1) * 72 + (to_y >> 1) * 36 + to_x * 9
        hit = lax.broadcasted_iota(jnp.int32, (384, D), 1) == order
        pv[pl.ds(base, 384)] = jnp.where(hit, 1.0, 0.0).astype(BF16)


def pair_weights(scalars, rows, cols, xs, height, ys, scale_of, gs, label=None):
    sharpness, shift = scalars
    logits = nt_dot(rows, cols) * sharpness + shift
    for i, x in enumerate(xs):
        for j, y in enumerate(ys):
            part = logits[i * height : (i + 1) * height, j * PAD : (j + 1) * PAD]
            scale = scale_of(x, y)
            if label is not None and x == y:
                match = label(x)
                g = jnp.where(match, -scale, scale) * jax.nn.sigmoid(jnp.where(match, -part, part))
            else:
                g = scale * jax.nn.sigmoid(part)
            gs[i * height : (i + 1) * height, j * PAD : (j + 1) * PAD] = g.astype(BF16)


def own_kernel(
    place_ref, sharp_ref, shift_ref, coef_ref, mine_ref, other_ref, im, io, cm, co, wi, wc,
    zx_out, zy_out, ux_out, ix_out, dz_out,
    f, w, tmp, zx, zy, ux, ix, gs, dz, targets, sems,
):
    core = place_ref[0]
    first = by_role(
        place_ref, [(im, co, f.at[0, pl.ds(0, R)]), (io, cm, f.at[0, pl.ds(R, R)]), (wi, wc, w.at[0])],
        sems.at[pl.ds(0, 3)],
    )
    second = by_role(
        place_ref, [(cm, io, f.at[1, pl.ds(0, R)]), (co, im, f.at[1, pl.ds(R, R)]), (wc, wi, w.at[1])],
        sems.at[pl.ds(3, 3)],
    )
    targets[...] = jnp.full((2, PAD), -1, jnp.int32)
    targets[0:1, 0:R] = jnp.where(core == 0, mine_ref[...], other_ref[...])
    targets[1:2, 0:R] = jnp.where(core == 0, other_ref[...], mine_ref[...])
    for wait in first:
        wait.wait()
    inv = project(f.at[0], w.at[0], tmp, 2 * R)
    ix[...] = jnp.broadcast_to(inv, (2 * R, 128))
    unit = tmp[...] * inv
    ux[...] = unit
    zx[...] = unit.astype(BF16)
    outs = [fetch(ux, ux_out, sems.at[6]), fetch(zx, zx_out, sems.at[7]), fetch(ix, ix_out, sems.at[8])]
    for wait in second:
        wait.wait()
    inv = project(f.at[1], w.at[1], tmp, 2 * R)
    for b in range(2):
        zy[b * PAD : b * PAD + R] = (tmp[b * R : (b + 1) * R] * inv[b * R : (b + 1) * R]).astype(BF16)
        zy[b * PAD + R : (b + 1) * PAD] = jnp.zeros((PAD - R, D), BF16)
    outs.append(fetch(zy, zy_out, sems.at[10]))

    def label(k):
        down, across = lax.broadcasted_iota(jnp.int32, (R, PAD), 0), lax.broadcasted_iota(jnp.int32, (R, PAD), 1)
        by_row = jnp.broadcast_to(targets[k : k + 1], (R, PAD))
        by_col = jnp.sum(jnp.where(down == across, by_row, 0), axis=1, keepdims=True)
        target = jnp.where(core == 0, jnp.broadcast_to(by_col, (R, PAD)), by_row)
        return jnp.where(core == 0, across, down) == target

    scalars = (sharp_ref[0], shift_ref[0])
    pair_weights(scalars, zx[...], zy[...], (0, 1), R, (0, 1), lambda x, y: coef_ref[0], gs, label)

    @pl.loop(0, 3)
    def _(k):
        cols = pl.ds(pl.multiple_of(k * 384, 384), 384)
        dz[:, cols] = sharp_ref[0] * jnp.dot(gs[...], zy[:, cols], preferred_element_type=F32)

    outs.append(fetch(dz, dz_out, sems.at[11]))

    for copy in outs:
        copy.wait()


def own_part(place, sharp, shift, coef, mine, other, *operands):
    smem = pl.BlockSpec(memory_space=pltpu.SMEM)
    vmem = pl.BlockSpec(memory_space=pltpu.VMEM)
    hbm = pl.BlockSpec(memory_space=pl.ANY)
    results = [
        ((2 * R, D), BF16), ((2 * PAD, D), BF16), ((2 * R, D), F32), ((2 * R, 128), F32),
        ((2 * R, D), F32),
    ]
    return pl.pallas_call(
        own_kernel,
        out_shape=[jax.ShapeDtypeStruct(*result) for result in results],
        in_specs=[smem] * 4 + [vmem] * 2 + [hbm] * 6,
        out_specs=[hbm] * 5,
        scratch_shapes=[
            pltpu.VMEM((2, 2 * R, D), BF16),
            pltpu.VMEM((2, D, D), BF16),
            pltpu.VMEM((2 * R, D), F32),
            pltpu.VMEM((2 * R, D), BF16),
            pltpu.VMEM((2 * PAD, D), BF16),
            pltpu.VMEM((2 * R, D), F32),
            pltpu.VMEM((2 * R, 128), F32),
            pltpu.VMEM((2 * R, 2 * PAD), BF16),
            pltpu.VMEM((2 * R, D), F32),
            pltpu.VMEM((2, PAD), jnp.int32),
            pltpu.SemaphoreType.DMA((13,)),
        ],
        compiler_params=pltpu.CompilerParams(vmem_limit_bytes=60 * 2**20),
        cost_estimate=pl.CostEstimate(flops=6 * 10**9, bytes_accessed=16 * 10**6, transcendentals=500000),
    )(place, sharp, shift, coef, mine, other, *operands)


def turn_kernel(place_ref, im, io, cm, co, pv_out, ft_out, f, pv, ft, sems):
    feats = by_role(
        place_ref, [(im, co, f.at[pl.ds(0, R)]), (io, cm, f.at[pl.ds(R, R)])], sems.at[pl.ds(0, 2)]
    )
    one_hot(place_ref, pv)
    outs = [fetch(pv, pv_out, sems.at[2])]
    for wait in feats:
        wait.wait()

    @pl.loop(0, 3)
    def _(k):
        rows = pl.ds(pl.multiple_of(k * 384, 384), 384)
        ft[rows, 0 : 2 * R] = nt_dot(pv[rows], f[...]).astype(BF16)

    ft[:, 2 * R :] = jnp.zeros((D, 2 * PAD - 2 * R), BF16)
    for copy in outs + [fetch(ft, ft_out, sems.at[3])]:
        copy.wait()


def turn_own(place, *operands):
    hbm = pl.BlockSpec(memory_space=pl.ANY)
    return pl.pallas_call(
        turn_kernel,
        out_shape=[jax.ShapeDtypeStruct((D, D), BF16), jax.ShapeDtypeStruct((D, 2 * PAD), BF16)],
        in_specs=[pl.BlockSpec(memory_space=pltpu.SMEM)] + [hbm] * 4,
        out_specs=[hbm] * 2,
        scratch_shapes=[
            pltpu.VMEM((2 * R, D), BF16),
            pltpu.VMEM((D, D), BF16),
            pltpu.VMEM((D, 2 * PAD), BF16),
            pltpu.SemaphoreType.DMA((4,)),
        ],
        compiler_params=pltpu.CompilerParams(vmem_limit_bytes=60 * 2**20),
        cost_estimate=pl.CostEstimate(flops=2 * 10**9, bytes_accessed=6 * 10**6, transcendentals=0),
    )(place, *operands)


def arrived_kernel(
    place_ref, sharp_ref, shift_ref, coef_ref,
    sm, so, fm, fo, em, eo, wi, wc, order, zx_in, zy_in, ux_in, ix_in, ft_in, dz_in,
    out0, out1, out2, out3,
    fi, fc, w, pv, zx, z, uo, ui, uc, io_, ii, ic, fto, fta, dz, da, gs, dp, sems,
):
    role, y_lo = place_ref[0], place_ref[1]
    scalars = (sharp_ref[0], shift_ref[0])

    def slot(blocks, k):
        return blocks.at[pl.ds(k * PAD, R)]

    images = by_role(place_ref, [(fm, fo, slot(fi, 0)), (fo, fm, slot(fi, 1)), (em, eo, slot(fi, 2))], sems.at[pl.ds(0, 3)])
    images.append(fetch(wi, w.at[0], sems.at[3]))
    for s in range(3):
        fi[s * PAD + R : (s + 1) * PAD] = jnp.zeros((PAD - R, D), BF16)
    for s in range(2):
        fc[s * PAD + R : (s + 1) * PAD] = jnp.zeros((PAD - R, D), BF16)
    dp[2 * R : 2 * PAD] = jnp.zeros((2 * (PAD - R), D), BF16)
    for wait in images:
        wait.wait()
    captions = by_role(place_ref, [(sm, so, slot(fc, 0)), (so, sm, slot(fc, 1))], sems.at[pl.ds(4, 2)])
    captions.append(fetch(wc, w.at[1], sems.at[6]))

    def unit_rows(feats, head, unit, inverse, m, base):
        inv = project(feats, head, unit, m)
        inverse[...] = jnp.broadcast_to(inv, (m, 128))
        unit[...] = unit[...] * inv
        z[pl.ds(pl.multiple_of(base, PAD), m)] = unit[...].astype(BF16)

    unit_rows(fi, w.at[0], ui, ii, 3 * PAD, role * 5 * PAD)
    for wait in captions:
        wait.wait()
    order_copy = fetch(order, pv, sems.at[7])
    late = [
        fetch(zx_in, zx, sems.at[8]),
        fetch(zy_in, z.at[pl.ds(3 * PAD, 2 * PAD)], sems.at[9]),
        fetch(ux_in, uo, sems.at[10]),
        fetch(ix_in, io_, sems.at[11]),
        fetch(dz_in, dz, sems.at[12]),
        fetch(ft_in, fto, sems.at[13]),
    ]
    unit_rows(fc, w.at[1], uc, ic, 2 * PAD, (1 - role) * 5 * PAD)
    order_copy.wait()

    def turn(feats, m):
        @pl.loop(0, 3)
        def _(k):
            rows = pl.ds(pl.multiple_of(k * 384, 384), 384)
            fta[rows, 0:m] = nt_dot(pv[rows], feats[...]).astype(BF16)

    @pl.when(role == 0)
    def _():
        turn(fi, 3 * PAD)

    @pl.when(role == 1)
    def _():
        turn(fc, 2 * PAD)
        fta[:, 2 * PAD : 3 * PAD] = jnp.zeros((D, PAD), BF16)

    for copy in late:
        copy.wait()

    def spread(m, cols, y0, y1, kept, unit, inverse, base):
        for n, wd in THIRDS:
            d = scalars[0] * jnp.dot(gs[0:m, 0:cols], z[y0 * PAD : y1 * PAD, n : n + wd], preferred_element_type=F32)
            if kept:
                d = d + dz[:, n : n + wd]
            da[0:m, n : n + wd] = d

        along = jnp.sum(da[0:m] * unit[0:m], axis=1, keepdims=True)
        dp[base : base + m] = ((da[0:m] - unit[0:m] * along) * inverse[0:m, 0:1]).astype(BF16)

    def scale(image, caption):
        return coef_ref[0] * jnp.where(y_lo == 0, TAKEN[0][image][caption], TAKEN[1][image][caption])

    def by_image(x, y):
        return scale(x, y)

    def by_caption(x, y):
        return scale(y, x)

    @pl.when(role == 0)
    def _():
        pair_weights(scalars, zx[...], z[5 * PAD : 7 * PAD], (0, 1), R, (2, 3), by_image, gs)
        spread(2 * R, 2 * PAD, 5, 7, True, uo, io_, 0)
        pair_weights(scalars, z[0 : 2 * PAD], z[4 * PAD : 7 * PAD], (2, 3), PAD, (1, 2, 3), by_image, gs)
        spread(2 * PAD, 3 * PAD, 4, 7, False, ui, ii, 2 * PAD)
        pair_weights(scalars, z[2 * PAD : 3 * PAD], z[4 * PAD : 5 * PAD], (4,), PAD, (1,), by_image, gs)
        spread(PAD, PAD, 4, 5, False, ui.at[2 * PAD : 3 * PAD], ii.at[2 * PAD : 3 * PAD], 4 * PAD)

    @pl.when(role == 1)
    def _():
        pair_weights(scalars, zx[...], z[5 * PAD : 8 * PAD], (0, 1), R, (2, 3, 4), by_caption, gs)
        spread(2 * R, 3 * PAD, 5, 8, True, uo, io_, 0)
        pair_weights(scalars, z[0 : 2 * PAD], z[3 * PAD : 7 * PAD], (2, 3), PAD, (0, 1, 2, 3), by_caption, gs)
        spread(2 * PAD, 4 * PAD, 3, 7, False, uc, ic, 2 * PAD)
        dp[4 * PAD : 5 * PAD] = jnp.zeros((PAD, D), BF16)

    @pl.loop(0, 3)
    def _(k):
        at = pl.ds(pl.multiple_of(k * 384, 384), 384)
        own = dp[0 : 2 * PAD, at]
        rest = dp[2 * PAD : 5 * PAD, at]
        for i, out in enumerate((out0, out1, out2, out3)):
            rows = slice(i * 288, (i + 1) * 288)
            out[:, at] = (
                jnp.dot(fto[rows], own, preferred_element_type=F32)
                + jnp.dot(fta[rows], rest, preferred_element_type=F32)
            ).astype(BF16)


def arrived_part(place, sharp, shift, coef, *operands):
    smem = pl.BlockSpec(memory_space=pltpu.SMEM)
    vmem = pl.BlockSpec(memory_space=pltpu.VMEM)
    return pl.pallas_call(
        arrived_kernel,
        out_shape=[jax.ShapeDtypeStruct((D // 4, D), BF16)] * 4,
        in_specs=[smem] * 4 + [pl.BlockSpec(memory_space=pl.ANY)] * 15,
        out_specs=[vmem] * 4,
        scratch_shapes=[
            pltpu.VMEM((3 * PAD, D), BF16),
            pltpu.VMEM((2 * PAD, D), BF16),
            pltpu.VMEM((2, D, D), BF16),
            pltpu.VMEM((D, D), BF16),
            pltpu.VMEM((2 * R, D), BF16),
            pltpu.VMEM((8 * PAD, D), BF16),
            pltpu.VMEM((2 * R, D), F32),
            pltpu.VMEM((3 * PAD, D), F32),
            pltpu.VMEM((2 * PAD, D), F32),
            pltpu.VMEM((2 * R, 128), F32),
            pltpu.VMEM((3 * PAD, 128), F32),
            pltpu.VMEM((2 * PAD, 128), F32),
            pltpu.VMEM((D, 2 * PAD), BF16),
            pltpu.VMEM((D, 3 * PAD), BF16),
            pltpu.VMEM((2 * R, D), F32),
            pltpu.VMEM((3 * PAD, D), F32),
            pltpu.VMEM((3 * PAD, 4 * PAD), BF16),
            pltpu.VMEM((5 * PAD, D), BF16),
            pltpu.SemaphoreType.DMA((14,)),
        ],
        compiler_params=pltpu.CompilerParams(vmem_limit_bytes=60 * 2**20),
        cost_estimate=pl.CostEstimate(flops=14 * 10**9, bytes_accessed=20 * 10**6, transcendentals=800000),
    )(place, sharp, shift, coef, *operands)


def join_kernel(place_ref, one, two, three, four, image_out, caption_out, held):
    for k, piece in enumerate((one, two, three, four)):
        held[k] = piece[...]
    for place in range(NX):
        back = (place_ref[2] - place) & 3
        for head, out in enumerate((image_out, caption_out)):
            for row in range(9):
                at = place * 9 + row
                for n in range(9):
                    out[at : at + 1, n * 128 : (n + 1) * 128] = held[back, head, row * 9 + n : row * 9 + n + 1]


def join_rows(place, *pieces):
    vmem = pl.BlockSpec(memory_space=pltpu.VMEM)
    return pl.pallas_call(
        join_kernel,
        out_shape=[jax.ShapeDtypeStruct((36, D), F32)] * 2,
        in_specs=[pl.BlockSpec(memory_space=pltpu.SMEM)] + [vmem] * 4,
        out_specs=[vmem] * 2,
        scratch_shapes=[pltpu.VMEM((4, 2, 81, 128), F32)],
    )(place, *pieces)


def local(
    picture_encoder_features,
    text_encoder_features,
    picture_projector,
    text_projector,
    matching_target,
    sharpness_param,
    offset_shift,
    objective_multiplier,
):
    place = lax.axis_index("dp")
    core, y_lo = place % 2, (place // 2) % 2
    x, y_hi = lax.axis_index("replica") // 2, lax.axis_index("replica") % 2
    y = y_hi * 2 + y_lo
    role = jnp.stack([core, y_lo, x, y]).astype(jnp.int32)
    coefficient = objective_multiplier / (lax.axis_size("dp") * R)

    own_img = swap_cores(picture_encoder_features)
    own_cap = swap_cores(text_encoder_features)
    target_other = swap_cores(matching_target)
    cap, img, target_other = lax.optimization_barrier(
        (text_encoder_features, picture_encoder_features, target_other)
    )
    cap_sib = swap_chips(cap)
    img_far = image_to_neighbour(img)
    img_extra = image_down(img)

    blocks = (picture_encoder_features, own_img, text_encoder_features, own_cap)
    *kept, from_own = own_part(
        role, sharpness_param, offset_shift, coefficient, matching_target[None], target_other[None],
        *blocks, picture_projector, text_projector,
    )
    cap_sib, img_far, img_extra, kept, from_own, blocks = lax.optimization_barrier(
        (cap_sib, img_far, img_extra, kept, from_own, blocks)
    )
    cap_sib_other = swap_cores(cap_sib)
    img_far_other = swap_cores(img_far)
    img_extra_other = swap_cores(img_extra)
    order, turned = turn_own(role, *blocks)
    parts = arrived_part(
        role, sharpness_param, offset_shift, coefficient,
        cap_sib, cap_sib_other, img_far, img_far_other, img_extra, img_extra_other,
        picture_projector, text_projector, order, *kept, turned, from_own,
    )

    one = [parts[0]] + [first_axis(parts[by], by) for by in (1, 3, 2)]
    one = sum(v.astype(F32) for v in one).astype(BF16)
    pieces = [one[by * 72 : (by + 1) * 72] for by in range(4)]
    two = [pieces[0]] + [second_axis(pieces[by], by) for by in (1, 3, 2)]
    two = sum(v.astype(F32) for v in two).astype(BF16).reshape(NZ, 81, 128)
    three = lax.all_to_all(two, AXES, 0, 0, axis_index_groups=ALONG_Z)
    mine = jnp.sum(three.astype(F32), axis=0)

    first = core == 0
    ring, cross = pass_on(mine), pass_across(mine)
    home = core == y_hi
    image_piece = jnp.where(home & first, mine, jnp.where(home | first, ring, cross))
    caption_piece = jnp.where(home & first, ring, jnp.where(home, mine, jnp.where(first, cross, ring)))
    both = jnp.stack([image_piece, caption_piece])
    return join_rows(role, both, *[along_x(both, by) for by in (1, 2, 3)])


def solution(mesh):
    placed = (
        P(("dp", "replica"), None),
        P(("dp", "replica"), None),
        P(),
        P(),
        P(("dp", "replica")),
        P(),
        P(),
        P(),
    )
    return jax.shard_map(
        local, mesh=mesh, in_specs=placed, out_specs=(P("dp", None), P("dp", None)), check_vma=False
    )
```

```python
import jax
import jax.numpy as jnp
import numpy as np
from jax import lax
from jax.experimental import pallas as pl
from jax.experimental.pallas import tpu as pltpu
from jax.sharding import PartitionSpec as P

AXES = ("dp", "replica")
NX, NY, NZ = 4, 4, 8
R, D, PAD = 224, 1152, 256
F32, BF16 = jnp.float32, jnp.bfloat16


def device_at(x, y, z, core):
    x, y, z = x % NX, y % NY, z % NZ
    return (z * 4 + (y % 2) * 2 + core) * 8 + x * 2 + y // 2


PLACES = [(x, y, z, c) for x in range(NX) for y in range(NY) for z in range(NZ) for c in range(2)]


ALONG_Z = [[device_at(x, y, z, c) for z in range(NZ)] for x in range(NX) for y in range(NY) for c in range(2)]


def moved(value, to):
    pairs = []
    for place in PLACES:
        target = to(*place)
        if target is not None:
            pairs.append((device_at(*place), device_at(*target)))
    return lax.ppermute(value, AXES, pairs)


def swap_cores(value):
    return moved(value, lambda x, y, z, c: (x, y, z, 1 - c))


def swap_chips(value):
    return moved(value, lambda x, y, z, c: (x, y ^ 1, z, c))


def image_to_neighbour(value):
    return moved(value, lambda x, y, z, c: (x, y, z - 1, c) if y % 2 == 0 else (x, y, z + 1, c))


def first_axis(value, by):
    return moved(value, lambda x, y, z, c: (x + by, y, z, c) if c == 0 else (x, y + by, z, c))


def second_axis(value, by):
    return moved(value, lambda x, y, z, c: (x, y + by, z, c) if c == 0 else (x + by, y, z, c))


def along_x(value, by):
    return moved(value, lambda x, y, z, c: (x + by, y, z, c))


def pass_on(value):
    def to(x, y, z, c):
        if c == y // 2:
            return (x, y ^ 2, z, c)
        return (x, y, z, 1 - c)

    return moved(value, to)


def pass_across(value):
    return moved(value, lambda x, y, z, c: (x, y ^ 2, z, 1 - c) if c != y // 2 else None)


def image_down(value):
    return moved(value, lambda x, y, z, c: (x, y, z - 1, c) if y % 2 == 1 and c == 0 else None)


THIRDS = [(n, 384) for n in range(0, D, 384)]


IMAGE_AT = np.array([[0, 1, 4, 5, 100], [2, 3, -2, -1, 6]])
CAPTION_AT = np.array([[0, 1, 2, 3], [2, 3, 0, 1]])
APART = CAPTION_AT[:, None, :] - IMAGE_AT[:, :, None]
TAKEN = ((APART >= -3) & (APART <= 2)).astype(float).tolist()


def nt_dot(a, b):
    return lax.dot_general(a, b, (((1,), (1,)), ((), ())), preferred_element_type=F32)


def fetch(src, dst, sem):
    copy = pltpu.make_async_copy(src, dst, sem)
    copy.start()
    return copy


def by_role(place_ref, choices, sems):
    waits = []
    for k, (zero, one, dst) in enumerate(choices):

        @pl.when(place_ref[0] == 0)
        def _():
            fetch(zero, dst, sems.at[k])

        @pl.when(place_ref[0] == 1)
        def _():
            fetch(one, dst, sems.at[k])

        waits.append(pltpu.make_async_copy(zero, dst, sems.at[k]))
    return waits


def project(feats, head, tmp, rows):
    squares = jnp.zeros((rows, 1), F32)
    for n, w in THIRDS:
        p = jnp.dot(feats[0:rows], head[:, n : n + w], preferred_element_type=F32)
        tmp[0:rows, n : n + w] = p
        squares = squares + jnp.sum(p * p, axis=1, keepdims=True)
    return lax.rsqrt(squares + 1e-6)


def one_hot(place_ref, pv):
    core, x, y = place_ref[0], place_ref[2], place_ref[3]

    @pl.loop(0, 3)
    def _(k):
        base = pl.multiple_of(k * 384, 384)
        row = lax.broadcasted_iota(jnp.int32, (384, 1), 0) + base
        group = (row * 7282) >> 16
        one, two = (group >> 5) & 3, (group >> 3) & 3
        to_x = (x + jnp.where(core == 0, one, two)) & 3
        to_y = (y + jnp.where(core == 0, two, one)) & 3
        order = (group & 7) * 144 + row - group * 9 + (to_y & 1) * 72 + (to_y >> 1) * 36 + to_x * 9
        hit = lax.broadcasted_iota(jnp.int32, (384, D), 1) == order
        pv[pl.ds(base, 384)] = jnp.where(hit, 1.0, 0.0).astype(BF16)


def pair_weights(scalars, rows, cols, xs, height, ys, scale_of, gs, label=None):
    sharpness, shift = scalars
    logits = nt_dot(rows, cols) * sharpness + shift
    for i, x in enumerate(xs):
        for j, y in enumerate(ys):
            part = logits[i * height : (i + 1) * height, j * PAD : (j + 1) * PAD]
            scale = scale_of(x, y)
            if label is not None and x == y:
                match = label(x)
                g = jnp.where(match, -scale, scale) * jax.nn.sigmoid(jnp.where(match, -part, part))
            else:
                g = scale * jax.nn.sigmoid(part)
            gs[i * height : (i + 1) * height, j * PAD : (j + 1) * PAD] = g.astype(BF16)


def own_kernel(
    place_ref, sharp_ref, shift_ref, coef_ref, mine_ref, other_ref, im, io, cm, co, wi, wc,
    zx_out, zy_out, ux_out, ix_out, dz_out,
    f, w, tmp, zx, zy, ux, ix, gs, dz, targets, sems,
):
    core = place_ref[0]
    first = by_role(
        place_ref, [(im, co, f.at[0, pl.ds(0, R)]), (io, cm, f.at[0, pl.ds(R, R)]), (wi, wc, w.at[0])],
        sems.at[pl.ds(0, 3)],
    )
    second = by_role(
        place_ref, [(cm, io, f.at[1, pl.ds(0, R)]), (co, im, f.at[1, pl.ds(R, R)]), (wc, wi, w.at[1])],
        sems.at[pl.ds(3, 3)],
    )
    targets[...] = jnp.full((2, PAD), -1, jnp.int32)
    targets[0:1, 0:R] = jnp.where(core == 0, mine_ref[...], other_ref[...])
    targets[1:2, 0:R] = jnp.where(core == 0, other_ref[...], mine_ref[...])
    for wait in first:
        wait.wait()
    inv = project(f.at[0], w.at[0], tmp, 2 * R)
    ix[...] = jnp.broadcast_to(inv, (2 * R, 128))
    unit = tmp[...] * inv
    ux[...] = unit
    zx[...] = unit.astype(BF16)
    outs = [fetch(ux, ux_out, sems.at[6]), fetch(zx, zx_out, sems.at[7]), fetch(ix, ix_out, sems.at[8])]
    for wait in second:
        wait.wait()
    inv = project(f.at[1], w.at[1], tmp, 2 * R)
    for b in range(2):
        zy[b * PAD : b * PAD + R] = (tmp[b * R : (b + 1) * R] * inv[b * R : (b + 1) * R]).astype(BF16)
        zy[b * PAD + R : (b + 1) * PAD] = jnp.zeros((PAD - R, D), BF16)
    outs.append(fetch(zy, zy_out, sems.at[10]))

    def label(k):
        down, across = lax.broadcasted_iota(jnp.int32, (R, PAD), 0), lax.broadcasted_iota(jnp.int32, (R, PAD), 1)
        by_row = jnp.broadcast_to(targets[k : k + 1], (R, PAD))
        by_col = jnp.sum(jnp.where(down == across, by_row, 0), axis=1, keepdims=True)
        target = jnp.where(core == 0, jnp.broadcast_to(by_col, (R, PAD)), by_row)
        return jnp.where(core == 0, across, down) == target

    scalars = (sharp_ref[0], shift_ref[0])
    pair_weights(scalars, zx[...], zy[...], (0, 1), R, (0, 1), lambda x, y: coef_ref[0], gs, label)

    @pl.loop(0, 3)
    def _(k):
        cols = pl.ds(pl.multiple_of(k * 384, 384), 384)
        dz[:, cols] = sharp_ref[0] * jnp.dot(gs[...], zy[:, cols], preferred_element_type=F32)

    outs.append(fetch(dz, dz_out, sems.at[11]))

    for copy in outs:
        copy.wait()


def own_part(place, sharp, shift, coef, mine, other, *operands):
    smem = pl.BlockSpec(memory_space=pltpu.SMEM)
    vmem = pl.BlockSpec(memory_space=pltpu.VMEM)
    hbm = pl.BlockSpec(memory_space=pl.ANY)
    results = [
        ((2 * R, D), BF16), ((2 * PAD, D), BF16), ((2 * R, D), F32), ((2 * R, 128), F32),
        ((2 * R, D), F32),
    ]
    return pl.pallas_call(
        own_kernel,
        out_shape=[jax.ShapeDtypeStruct(*result) for result in results],
        in_specs=[smem] * 4 + [vmem] * 2 + [hbm] * 6,
        out_specs=[hbm] * 5,
        scratch_shapes=[
            pltpu.VMEM((2, 2 * R, D), BF16),
            pltpu.VMEM((2, D, D), BF16),
            pltpu.VMEM((2 * R, D), F32),
            pltpu.VMEM((2 * R, D), BF16),
            pltpu.VMEM((2 * PAD, D), BF16),
            pltpu.VMEM((2 * R, D), F32),
            pltpu.VMEM((2 * R, 128), F32),
            pltpu.VMEM((2 * R, 2 * PAD), BF16),
            pltpu.VMEM((2 * R, D), F32),
            pltpu.VMEM((2, PAD), jnp.int32),
            pltpu.SemaphoreType.DMA((13,)),
        ],
        compiler_params=pltpu.CompilerParams(vmem_limit_bytes=60 * 2**20),
        cost_estimate=pl.CostEstimate(flops=6 * 10**9, bytes_accessed=16 * 10**6, transcendentals=500000),
    )(place, sharp, shift, coef, mine, other, *operands)


def turn_kernel(place_ref, im, io, cm, co, pv_out, ft_out, f, pv, ft, sems):
    feats = by_role(
        place_ref, [(im, co, f.at[pl.ds(0, R)]), (io, cm, f.at[pl.ds(R, R)])], sems.at[pl.ds(0, 2)]
    )
    one_hot(place_ref, pv)
    outs = [fetch(pv, pv_out, sems.at[2])]
    for wait in feats:
        wait.wait()

    @pl.loop(0, 3)
    def _(k):
        rows = pl.ds(pl.multiple_of(k * 384, 384), 384)
        ft[rows, 0 : 2 * R] = nt_dot(pv[rows], f[...]).astype(BF16)

    ft[:, 2 * R :] = jnp.zeros((D, 2 * PAD - 2 * R), BF16)
    for copy in outs + [fetch(ft, ft_out, sems.at[3])]:
        copy.wait()


def turn_own(place, *operands):
    hbm = pl.BlockSpec(memory_space=pl.ANY)
    return pl.pallas_call(
        turn_kernel,
        out_shape=[jax.ShapeDtypeStruct((D, D), BF16), jax.ShapeDtypeStruct((D, 2 * PAD), BF16)],
        in_specs=[pl.BlockSpec(memory_space=pltpu.SMEM)] + [hbm] * 4,
        out_specs=[hbm] * 2,
        scratch_shapes=[
            pltpu.VMEM((2 * R, D), BF16),
            pltpu.VMEM((D, D), BF16),
            pltpu.VMEM((D, 2 * PAD), BF16),
            pltpu.SemaphoreType.DMA((4,)),
        ],
        compiler_params=pltpu.CompilerParams(vmem_limit_bytes=60 * 2**20),
        cost_estimate=pl.CostEstimate(flops=2 * 10**9, bytes_accessed=6 * 10**6, transcendentals=0),
    )(place, *operands)


def arrived_kernel(
    place_ref, sharp_ref, shift_ref, coef_ref,
    sm, so, fm, fo, em, eo, wi, wc, order, zx_in, zy_in, ux_in, ix_in, ft_in, dz_in,
    out0, out1, out2, out3,
    fi, fc, w, pv, zx, z, uo, ui, uc, io_, ii, ic, fto, fta, dz, da, gs, dp, sems,
):
    role, y_lo = place_ref[0], place_ref[1]
    scalars = (sharp_ref[0], shift_ref[0])

    def slot(blocks, k):
        return blocks.at[pl.ds(k * PAD, R)]

    images = by_role(place_ref, [(fm, fo, slot(fi, 0)), (fo, fm, slot(fi, 1)), (em, eo, slot(fi, 2))], sems.at[pl.ds(0, 3)])
    images.append(fetch(wi, w.at[0], sems.at[3]))
    for s in range(3):
        fi[s * PAD + R : (s + 1) * PAD] = jnp.zeros((PAD - R, D), BF16)
    for s in range(2):
        fc[s * PAD + R : (s + 1) * PAD] = jnp.zeros((PAD - R, D), BF16)
    dp[2 * R : 2 * PAD] = jnp.zeros((2 * (PAD - R), D), BF16)
    for wait in images:
        wait.wait()
    captions = by_role(place_ref, [(sm, so, slot(fc, 0)), (so, sm, slot(fc, 1))], sems.at[pl.ds(4, 2)])
    captions.append(fetch(wc, w.at[1], sems.at[6]))

    def unit_rows(feats, head, unit, inverse, m, base):
        inv = project(feats, head, unit, m)
        inverse[...] = jnp.broadcast_to(inv, (m, 128))
        unit[...] = unit[...] * inv
        z[pl.ds(pl.multiple_of(base, PAD), m)] = unit[...].astype(BF16)

    unit_rows(fi, w.at[0], ui, ii, 3 * PAD, role * 5 * PAD)
    for wait in captions:
        wait.wait()
    order_copy = fetch(order, pv, sems.at[7])
    late = [
        fetch(zx_in, zx, sems.at[8]),
        fetch(zy_in, z.at[pl.ds(3 * PAD, 2 * PAD)], sems.at[9]),
        fetch(ux_in, uo, sems.at[10]),
        fetch(ix_in, io_, sems.at[11]),
        fetch(dz_in, dz, sems.at[12]),
        fetch(ft_in, fto, sems.at[13]),
    ]
    unit_rows(fc, w.at[1], uc, ic, 2 * PAD, (1 - role) * 5 * PAD)
    order_copy.wait()

    def turn(feats, m):
        @pl.loop(0, 3)
        def _(k):
            rows = pl.ds(pl.multiple_of(k * 384, 384), 384)
            fta[rows, 0:m] = nt_dot(pv[rows], feats[...]).astype(BF16)

    @pl.when(role == 0)
    def _():
        turn(fi, 3 * PAD)

    @pl.when(role == 1)
    def _():
        turn(fc, 2 * PAD)
        fta[:, 2 * PAD : 3 * PAD] = jnp.zeros((D, PAD), BF16)

    for copy in late:
        copy.wait()

    def spread(m, cols, y0, y1, kept, unit, inverse, base):
        for n, wd in THIRDS:
            d = scalars[0] * jnp.dot(gs[0:m, 0:cols], z[y0 * PAD : y1 * PAD, n : n + wd], preferred_element_type=F32)
            if kept:
                d = d + dz[:, n : n + wd]
            da[0:m, n : n + wd] = d

        along = jnp.sum(da[0:m] * unit[0:m], axis=1, keepdims=True)
        dp[base : base + m] = ((da[0:m] - unit[0:m] * along) * inverse[0:m, 0:1]).astype(BF16)

    def scale(image, caption):
        return coef_ref[0] * jnp.where(y_lo == 0, TAKEN[0][image][caption], TAKEN[1][image][caption])

    def by_image(x, y):
        return scale(x, y)

    def by_caption(x, y):
        return scale(y, x)

    @pl.when(role == 0)
    def _():
        pair_weights(scalars, zx[...], z[5 * PAD : 7 * PAD], (0, 1), R, (2, 3), by_image, gs)
        spread(2 * R, 2 * PAD, 5, 7, True, uo, io_, 0)
        pair_weights(scalars, z[0 : 2 * PAD], z[4 * PAD : 7 * PAD], (2, 3), PAD, (1, 2, 3), by_image, gs)
        spread(2 * PAD, 3 * PAD, 4, 7, False, ui, ii, 2 * PAD)
        pair_weights(scalars, z[2 * PAD : 3 * PAD], z[4 * PAD : 5 * PAD], (4,), PAD, (1,), by_image, gs)
        spread(PAD, PAD, 4, 5, False, ui.at[2 * PAD : 3 * PAD], ii.at[2 * PAD : 3 * PAD], 4 * PAD)

    @pl.when(role == 1)
    def _():
        pair_weights(scalars, zx[...], z[5 * PAD : 8 * PAD], (0, 1), R, (2, 3, 4), by_caption, gs)
        spread(2 * R, 3 * PAD, 5, 8, True, uo, io_, 0)
        pair_weights(scalars, z[0 : 2 * PAD], z[3 * PAD : 7 * PAD], (2, 3), PAD, (0, 1, 2, 3), by_caption, gs)
        spread(2 * PAD, 4 * PAD, 3, 7, False, uc, ic, 2 * PAD)
        dp[4 * PAD : 5 * PAD] = jnp.zeros((PAD, D), BF16)

    @pl.loop(0, 3)
    def _(k):
        at = pl.ds(pl.multiple_of(k * 384, 384), 384)
        own = dp[0 : 2 * PAD, at]
        rest = dp[2 * PAD : 5 * PAD, at]
        for i, out in enumerate((out0, out1, out2, out3)):
            rows = slice(i * 288, (i + 1) * 288)
            out[:, at] = (
                jnp.dot(fto[rows], own, preferred_element_type=F32)
                + jnp.dot(fta[rows], rest, preferred_element_type=F32)
            ).astype(BF16)


def arrived_part(place, sharp, shift, coef, *operands):
    smem = pl.BlockSpec(memory_space=pltpu.SMEM)
    vmem = pl.BlockSpec(memory_space=pltpu.VMEM)
    return pl.pallas_call(
        arrived_kernel,
        out_shape=[jax.ShapeDtypeStruct((D // 4, D), BF16)] * 4,
        in_specs=[smem] * 4 + [pl.BlockSpec(memory_space=pl.ANY)] * 15,
        out_specs=[vmem] * 4,
        scratch_shapes=[
            pltpu.VMEM((3 * PAD, D), BF16),
            pltpu.VMEM((2 * PAD, D), BF16),
            pltpu.VMEM((2, D, D), BF16),
            pltpu.VMEM((D, D), BF16),
            pltpu.VMEM((2 * R, D), BF16),
            pltpu.VMEM((8 * PAD, D), BF16),
            pltpu.VMEM((2 * R, D), F32),
            pltpu.VMEM((3 * PAD, D), F32),
            pltpu.VMEM((2 * PAD, D), F32),
            pltpu.VMEM((2 * R, 128), F32),
            pltpu.VMEM((3 * PAD, 128), F32),
            pltpu.VMEM((2 * PAD, 128), F32),
            pltpu.VMEM((D, 2 * PAD), BF16),
            pltpu.VMEM((D, 3 * PAD), BF16),
            pltpu.VMEM((2 * R, D), F32),
            pltpu.VMEM((3 * PAD, D), F32),
            pltpu.VMEM((3 * PAD, 4 * PAD), BF16),
            pltpu.VMEM((5 * PAD, D), BF16),
            pltpu.SemaphoreType.DMA((14,)),
        ],
        compiler_params=pltpu.CompilerParams(vmem_limit_bytes=60 * 2**20),
        cost_estimate=pl.CostEstimate(flops=14 * 10**9, bytes_accessed=20 * 10**6, transcendentals=800000),
    )(place, sharp, shift, coef, *operands)


def join_kernel(place_ref, one, two, three, four, image_out, caption_out, held, rows):
    for k, piece in enumerate((one, two, three, four)):
        held[k, :, 0:81] = piece[...]
    for place in range(NX):
        back = (place_ref[2] - place) & 3
        for head in range(2):
            for n in range(9):
                rows[head, place * 9 : place * 9 + 9, n * 128 : (n + 1) * 128] = held[
                    back, head, pl.ds(n, 9, stride=9)
                ]
    image_out[...] = rows[0, 0:36]
    caption_out[...] = rows[1, 0:36]


def join_rows(place, *pieces):
    vmem = pl.BlockSpec(memory_space=pltpu.VMEM)
    return pl.pallas_call(
        join_kernel,
        out_shape=[jax.ShapeDtypeStruct((36, D), F32)] * 2,
        in_specs=[pl.BlockSpec(memory_space=pltpu.SMEM)] + [vmem] * 4,
        out_specs=[vmem] * 2,
        scratch_shapes=[pltpu.VMEM((4, 2, 144, 128), F32), pltpu.VMEM((2, 48, D), F32)],
    )(place, *pieces)


def local(
    picture_encoder_features,
    text_encoder_features,
    picture_projector,
    text_projector,
    matching_target,
    sharpness_param,
    offset_shift,
    objective_multiplier,
):
    place = lax.axis_index("dp")
    core, y_lo = place % 2, (place // 2) % 2
    x, y_hi = lax.axis_index("replica") // 2, lax.axis_index("replica") % 2
    y = y_hi * 2 + y_lo
    role = jnp.stack([core, y_lo, x, y]).astype(jnp.int32)
    coefficient = objective_multiplier / (lax.axis_size("dp") * R)

    own_img = swap_cores(picture_encoder_features)
    own_cap = swap_cores(text_encoder_features)
    target_other = swap_cores(matching_target)
    cap, img, target_other = lax.optimization_barrier(
        (text_encoder_features, picture_encoder_features, target_other)
    )
    cap_sib = swap_chips(cap)
    img_far = image_to_neighbour(img)
    img_extra = image_down(img)

    blocks = (picture_encoder_features, own_img, text_encoder_features, own_cap)
    *kept, from_own = own_part(
        role, sharpness_param, offset_shift, coefficient, matching_target[None], target_other[None],
        *blocks, picture_projector, text_projector,
    )
    cap_sib, img_far, img_extra, kept, from_own, blocks = lax.optimization_barrier(
        (cap_sib, img_far, img_extra, kept, from_own, blocks)
    )
    cap_sib_other = swap_cores(cap_sib)
    img_far_other = swap_cores(img_far)
    img_extra_other = swap_cores(img_extra)
    order, turned = turn_own(role, *blocks)
    parts = arrived_part(
        role, sharpness_param, offset_shift, coefficient,
        cap_sib, cap_sib_other, img_far, img_far_other, img_extra, img_extra_other,
        picture_projector, text_projector, order, *kept, turned, from_own,
    )

    one = [parts[0]] + [first_axis(parts[by], by) for by in (1, 3, 2)]
    one = sum(v.astype(F32) for v in one).astype(BF16)
    pieces = [one[by * 72 : (by + 1) * 72] for by in range(4)]
    two = [pieces[0]] + [second_axis(pieces[by], by) for by in (1, 3, 2)]
    two = sum(v.astype(F32) for v in two).astype(BF16).reshape(NZ, 81, 128)
    three = lax.all_to_all(two, AXES, 0, 0, axis_index_groups=ALONG_Z)
    mine = jnp.sum(three.astype(F32), axis=0)

    first = core == 0
    ring, cross = pass_on(mine), pass_across(mine)
    home = core == y_hi
    image_piece = jnp.where(home & first, mine, jnp.where(home | first, ring, cross))
    caption_piece = jnp.where(home & first, ring, jnp.where(home, mine, jnp.where(first, cross, ring)))
    both = jnp.stack([image_piece, caption_piece])
    return join_rows(role, both, *[along_x(both, by) for by in (1, 2, 3)])


def solution(mesh):
    placed = (
        P(("dp", "replica"), None),
        P(("dp", "replica"), None),
        P(),
        P(),
        P(("dp", "replica")),
        P(),
        P(),
        P(),
    )
    return jax.shard_map(
        local, mesh=mesh, in_specs=placed, out_specs=(P("dp", None), P("dp", None)), check_vma=False
    )
```

```python
import jax
import jax.numpy as jnp
import numpy as np
from jax import lax
from jax.experimental import pallas as pl
from jax.experimental.pallas import tpu as pltpu
from jax.sharding import PartitionSpec as P

AXES = ("dp", "replica")
NX, NY, NZ = 4, 4, 8
R, D, PAD = 224, 1152, 256
F32, BF16 = jnp.float32, jnp.bfloat16


def device_at(x, y, z, core):
    x, y, z = x % NX, y % NY, z % NZ
    return (z * 4 + (y % 2) * 2 + core) * 8 + x * 2 + y // 2


PLACES = [(x, y, z, c) for x in range(NX) for y in range(NY) for z in range(NZ) for c in range(2)]


ALONG_Z = [[device_at(x, y, z, c) for z in range(NZ)] for x in range(NX) for y in range(NY) for c in range(2)]


def moved(value, to):
    pairs = []
    for place in PLACES:
        target = to(*place)
        if target is not None:
            pairs.append((device_at(*place), device_at(*target)))
    return lax.ppermute(value, AXES, pairs)


def swap_cores(value):
    return moved(value, lambda x, y, z, c: (x, y, z, 1 - c))


def swap_chips(value):
    return moved(value, lambda x, y, z, c: (x, y ^ 1, z, c))


def image_to_neighbour(value):
    return moved(value, lambda x, y, z, c: (x, y, z - 1, c) if y % 2 == 0 else (x, y, z + 1, c))


def first_axis(value, by):
    return moved(value, lambda x, y, z, c: (x + by, y, z, c) if c == 0 else (x, y + by, z, c))


def second_axis(value, by):
    return moved(value, lambda x, y, z, c: (x, y + by, z, c) if c == 0 else (x + by, y, z, c))


def along_x(value, by):
    return moved(value, lambda x, y, z, c: (x + by, y, z, c))


def pass_on(value):
    def to(x, y, z, c):
        if c == y // 2:
            return (x, y ^ 2, z, c)
        return (x, y, z, 1 - c)

    return moved(value, to)


def pass_across(value):
    return moved(value, lambda x, y, z, c: (x, y ^ 2, z, 1 - c) if c != y // 2 else None)


def image_down(value):
    return moved(value, lambda x, y, z, c: (x, y, z - 1, c) if y % 2 == 1 and c == 0 else None)


THIRDS = [(n, 384) for n in range(0, D, 384)]


IMAGE_AT = np.array([[0, 1, 4, 5, 100], [2, 3, -2, -1, 6]])
CAPTION_AT = np.array([[0, 1, 2, 3], [2, 3, 0, 1]])
APART = CAPTION_AT[:, None, :] - IMAGE_AT[:, :, None]
TAKEN = ((APART >= -3) & (APART <= 2)).astype(float).tolist()


def nt_dot(a, b):
    return lax.dot_general(a, b, (((1,), (1,)), ((), ())), preferred_element_type=F32)


def fetch(src, dst, sem):
    copy = pltpu.make_async_copy(src, dst, sem)
    copy.start()
    return copy


def by_role(place_ref, choices, sems):
    waits = []
    for k, (zero, one, dst) in enumerate(choices):

        @pl.when(place_ref[0] == 0)
        def _():
            fetch(zero, dst, sems.at[k])

        @pl.when(place_ref[0] == 1)
        def _():
            fetch(one, dst, sems.at[k])

        waits.append(pltpu.make_async_copy(zero, dst, sems.at[k]))
    return waits


def project(feats, head, tmp, rows):
    squares = jnp.zeros((rows, 1), F32)
    for n, w in THIRDS:
        p = jnp.dot(feats[0:rows], head[:, n : n + w], preferred_element_type=F32)
        tmp[0:rows, n : n + w] = p
        squares = squares + jnp.sum(p * p, axis=1, keepdims=True)
    return lax.rsqrt(squares + 1e-6)


def one_hot(place_ref, pv):
    core, x, y = place_ref[0], place_ref[2], place_ref[3]

    @pl.loop(0, 3)
    def _(k):
        base = pl.multiple_of(k * 384, 384)
        row = lax.broadcasted_iota(jnp.int32, (384, 1), 0) + base
        group = (row * 7282) >> 16
        one, two = (group >> 5) & 3, (group >> 3) & 3
        to_x = (x + jnp.where(core == 0, one, two)) & 3
        to_y = (y + jnp.where(core == 0, two, one)) & 3
        order = (group & 7) * 144 + row - group * 9 + (to_y & 1) * 72 + (to_y >> 1) * 36 + to_x * 9
        hit = lax.broadcasted_iota(jnp.int32, (384, D), 1) == order
        pv[pl.ds(base, 384)] = jnp.where(hit, 1.0, 0.0).astype(BF16)


def pair_weights(scalars, rows, cols, xs, height, ys, scale_of, gs, label=None):
    sharpness, shift = scalars
    logits = nt_dot(rows, cols) * sharpness + shift
    for i, x in enumerate(xs):
        for j, y in enumerate(ys):
            part = logits[i * height : (i + 1) * height, j * PAD : (j + 1) * PAD]
            scale = scale_of(x, y)
            if label is not None and x == y:
                match = label(x)
                g = jnp.where(match, -scale, scale) * jax.nn.sigmoid(jnp.where(match, -part, part))
            else:
                g = scale * jax.nn.sigmoid(part)
            gs[i * height : (i + 1) * height, j * PAD : (j + 1) * PAD] = g.astype(BF16)


def own_kernel(
    place_ref, sharp_ref, shift_ref, coef_ref, mine_ref, other_ref, im, io, cm, co, wi, wc,
    zx_out, zy_out, ux_out, ix_out, dz_out,
    f, w, tmp, zx, zy, ux, ix, gs, dz, targets, sems,
):
    core = place_ref[0]
    first = by_role(
        place_ref, [(im, co, f.at[0, pl.ds(0, R)]), (io, cm, f.at[0, pl.ds(R, R)]), (wi, wc, w.at[0])],
        sems.at[pl.ds(0, 3)],
    )
    second = by_role(
        place_ref, [(cm, io, f.at[1, pl.ds(0, R)]), (co, im, f.at[1, pl.ds(R, R)]), (wc, wi, w.at[1])],
        sems.at[pl.ds(3, 3)],
    )
    targets[...] = jnp.full((2, PAD), -1, jnp.int32)
    targets[0:1, 0:R] = jnp.where(core == 0, mine_ref[...], other_ref[...])
    targets[1:2, 0:R] = jnp.where(core == 0, other_ref[...], mine_ref[...])
    for wait in first:
        wait.wait()
    inv = project(f.at[0], w.at[0], tmp, 2 * R)
    ix[...] = jnp.broadcast_to(inv, (2 * R, 128))
    unit = tmp[...] * inv
    ux[...] = unit
    zx[...] = unit.astype(BF16)
    outs = [fetch(ux, ux_out, sems.at[6]), fetch(zx, zx_out, sems.at[7]), fetch(ix, ix_out, sems.at[8])]
    for wait in second:
        wait.wait()
    inv = project(f.at[1], w.at[1], tmp, 2 * R)
    for b in range(2):
        zy[b * PAD : b * PAD + R] = (tmp[b * R : (b + 1) * R] * inv[b * R : (b + 1) * R]).astype(BF16)
        zy[b * PAD + R : (b + 1) * PAD] = jnp.zeros((PAD - R, D), BF16)
    outs.append(fetch(zy, zy_out, sems.at[10]))

    def label(k):
        down, across = lax.broadcasted_iota(jnp.int32, (R, PAD), 0), lax.broadcasted_iota(jnp.int32, (R, PAD), 1)
        by_row = jnp.broadcast_to(targets[k : k + 1], (R, PAD))
        by_col = jnp.sum(jnp.where(down == across, by_row, 0), axis=1, keepdims=True)
        target = jnp.where(core == 0, jnp.broadcast_to(by_col, (R, PAD)), by_row)
        return jnp.where(core == 0, across, down) == target

    scalars = (sharp_ref[0], shift_ref[0])
    pair_weights(scalars, zx[...], zy[...], (0, 1), R, (0, 1), lambda x, y: coef_ref[0], gs, label)

    @pl.loop(0, 3, unroll=3)
    def _(k):
        cols = pl.ds(pl.multiple_of(k * 384, 384), 384)
        dz[:, cols] = sharp_ref[0] * jnp.dot(gs[...], zy[:, cols], preferred_element_type=F32)

    outs.append(fetch(dz, dz_out, sems.at[11]))

    for copy in outs:
        copy.wait()


def own_part(place, sharp, shift, coef, mine, other, *operands):
    smem = pl.BlockSpec(memory_space=pltpu.SMEM)
    vmem = pl.BlockSpec(memory_space=pltpu.VMEM)
    hbm = pl.BlockSpec(memory_space=pl.ANY)
    results = [
        ((2 * R, D), BF16), ((2 * PAD, D), BF16), ((2 * R, D), F32), ((2 * R, 128), F32),
        ((2 * R, D), F32),
    ]
    return pl.pallas_call(
        own_kernel,
        out_shape=[jax.ShapeDtypeStruct(*result) for result in results],
        in_specs=[smem] * 4 + [vmem] * 2 + [hbm] * 6,
        out_specs=[hbm] * 5,
        scratch_shapes=[
            pltpu.VMEM((2, 2 * R, D), BF16),
            pltpu.VMEM((2, D, D), BF16),
            pltpu.VMEM((2 * R, D), F32),
            pltpu.VMEM((2 * R, D), BF16),
            pltpu.VMEM((2 * PAD, D), BF16),
            pltpu.VMEM((2 * R, D), F32),
            pltpu.VMEM((2 * R, 128), F32),
            pltpu.VMEM((2 * R, 2 * PAD), BF16),
            pltpu.VMEM((2 * R, D), F32),
            pltpu.VMEM((2, PAD), jnp.int32),
            pltpu.SemaphoreType.DMA((13,)),
        ],
        compiler_params=pltpu.CompilerParams(vmem_limit_bytes=60 * 2**20),
        cost_estimate=pl.CostEstimate(flops=6 * 10**9, bytes_accessed=16 * 10**6, transcendentals=500000),
    )(place, sharp, shift, coef, mine, other, *operands)


def turn_kernel(place_ref, im, io, cm, co, pv_out, ft_out, f, pv, ft, sems):
    feats = by_role(
        place_ref, [(im, co, f.at[pl.ds(0, R)]), (io, cm, f.at[pl.ds(R, R)])], sems.at[pl.ds(0, 2)]
    )
    one_hot(place_ref, pv)
    outs = [fetch(pv, pv_out, sems.at[2])]
    for wait in feats:
        wait.wait()

    @pl.loop(0, 3, unroll=3)
    def _(k):
        rows = pl.ds(pl.multiple_of(k * 384, 384), 384)
        ft[rows, 0 : 2 * R] = nt_dot(pv[rows], f[...]).astype(BF16)

    ft[:, 2 * R :] = jnp.zeros((D, 2 * PAD - 2 * R), BF16)
    for copy in outs + [fetch(ft, ft_out, sems.at[3])]:
        copy.wait()


def turn_own(place, *operands):
    hbm = pl.BlockSpec(memory_space=pl.ANY)
    return pl.pallas_call(
        turn_kernel,
        out_shape=[jax.ShapeDtypeStruct((D, D), BF16), jax.ShapeDtypeStruct((D, 2 * PAD), BF16)],
        in_specs=[pl.BlockSpec(memory_space=pltpu.SMEM)] + [hbm] * 4,
        out_specs=[hbm] * 2,
        scratch_shapes=[
            pltpu.VMEM((2 * R, D), BF16),
            pltpu.VMEM((D, D), BF16),
            pltpu.VMEM((D, 2 * PAD), BF16),
            pltpu.SemaphoreType.DMA((4,)),
        ],
        compiler_params=pltpu.CompilerParams(vmem_limit_bytes=60 * 2**20),
        cost_estimate=pl.CostEstimate(flops=2 * 10**9, bytes_accessed=6 * 10**6, transcendentals=0),
    )(place, *operands)


def arrived_kernel(
    place_ref, sharp_ref, shift_ref, coef_ref,
    sm, so, fm, fo, em, eo, wi, wc, order, zx_in, zy_in, ux_in, ix_in, ft_in, dz_in,
    out0, out1, out2, out3,
    fi, fc, w, pv, zx, z, uo, ui, uc, io_, ii, ic, fto, fta, dz, da, gs, dp, sems,
):
    role, y_lo = place_ref[0], place_ref[1]
    scalars = (sharp_ref[0], shift_ref[0])

    def slot(blocks, k):
        return blocks.at[pl.ds(k * PAD, R)]

    images = by_role(place_ref, [(fm, fo, slot(fi, 0)), (fo, fm, slot(fi, 1)), (em, eo, slot(fi, 2))], sems.at[pl.ds(0, 3)])
    images.append(fetch(wi, w.at[0], sems.at[3]))
    for s in range(3):
        fi[s * PAD + R : (s + 1) * PAD] = jnp.zeros((PAD - R, D), BF16)
    for s in range(2):
        fc[s * PAD + R : (s + 1) * PAD] = jnp.zeros((PAD - R, D), BF16)
    dp[2 * R : 2 * PAD] = jnp.zeros((2 * (PAD - R), D), BF16)
    for wait in images:
        wait.wait()
    captions = by_role(place_ref, [(sm, so, slot(fc, 0)), (so, sm, slot(fc, 1))], sems.at[pl.ds(4, 2)])
    captions.append(fetch(wc, w.at[1], sems.at[6]))

    def unit_rows(feats, head, unit, inverse, m, base):
        inv = project(feats, head, unit, m)
        inverse[...] = jnp.broadcast_to(inv, (m, 128))
        unit[...] = unit[...] * inv
        z[pl.ds(pl.multiple_of(base, PAD), m)] = unit[...].astype(BF16)

    unit_rows(fi, w.at[0], ui, ii, 3 * PAD, role * 5 * PAD)
    for wait in captions:
        wait.wait()
    order_copy = fetch(order, pv, sems.at[7])
    late = [
        fetch(zx_in, zx, sems.at[8]),
        fetch(zy_in, z.at[pl.ds(3 * PAD, 2 * PAD)], sems.at[9]),
        fetch(ux_in, uo, sems.at[10]),
        fetch(ix_in, io_, sems.at[11]),
        fetch(dz_in, dz, sems.at[12]),
        fetch(ft_in, fto, sems.at[13]),
    ]
    unit_rows(fc, w.at[1], uc, ic, 2 * PAD, (1 - role) * 5 * PAD)
    order_copy.wait()

    def turn(feats, m):
        @pl.loop(0, 3)
        def _(k):
            rows = pl.ds(pl.multiple_of(k * 384, 384), 384)
            fta[rows, 0:m] = nt_dot(pv[rows], feats[...]).astype(BF16)

    @pl.when(role == 0)
    def _():
        turn(fi, 3 * PAD)

    @pl.when(role == 1)
    def _():
        turn(fc, 2 * PAD)
        fta[:, 2 * PAD : 3 * PAD] = jnp.zeros((D, PAD), BF16)

    for copy in late:
        copy.wait()

    def spread(m, cols, y0, y1, kept, unit, inverse, base):
        for n, wd in THIRDS:
            d = scalars[0] * jnp.dot(gs[0:m, 0:cols], z[y0 * PAD : y1 * PAD, n : n + wd], preferred_element_type=F32)
            if kept:
                d = d + dz[:, n : n + wd]
            da[0:m, n : n + wd] = d

        along = jnp.sum(da[0:m] * unit[0:m], axis=1, keepdims=True)
        dp[base : base + m] = ((da[0:m] - unit[0:m] * along) * inverse[0:m, 0:1]).astype(BF16)

    def scale(image, caption):
        return coef_ref[0] * jnp.where(y_lo == 0, TAKEN[0][image][caption], TAKEN[1][image][caption])

    def by_image(x, y):
        return scale(x, y)

    def by_caption(x, y):
        return scale(y, x)

    @pl.when(role == 0)
    def _():
        pair_weights(scalars, zx[...], z[5 * PAD : 7 * PAD], (0, 1), R, (2, 3), by_image, gs)
        spread(2 * R, 2 * PAD, 5, 7, True, uo, io_, 0)
        pair_weights(scalars, z[0 : 2 * PAD], z[4 * PAD : 7 * PAD], (2, 3), PAD, (1, 2, 3), by_image, gs)
        spread(2 * PAD, 3 * PAD, 4, 7, False, ui, ii, 2 * PAD)
        pair_weights(scalars, z[2 * PAD : 3 * PAD], z[4 * PAD : 5 * PAD], (4,), PAD, (1,), by_image, gs)
        spread(PAD, PAD, 4, 5, False, ui.at[2 * PAD : 3 * PAD], ii.at[2 * PAD : 3 * PAD], 4 * PAD)

    @pl.when(role == 1)
    def _():
        pair_weights(scalars, zx[...], z[5 * PAD : 8 * PAD], (0, 1), R, (2, 3, 4), by_caption, gs)
        spread(2 * R, 3 * PAD, 5, 8, True, uo, io_, 0)
        pair_weights(scalars, z[0 : 2 * PAD], z[3 * PAD : 7 * PAD], (2, 3), PAD, (0, 1, 2, 3), by_caption, gs)
        spread(2 * PAD, 4 * PAD, 3, 7, False, uc, ic, 2 * PAD)
        dp[4 * PAD : 5 * PAD] = jnp.zeros((PAD, D), BF16)

    @pl.loop(0, 3)
    def _(k):
        at = pl.ds(pl.multiple_of(k * 384, 384), 384)
        own = dp[0 : 2 * PAD, at]
        rest = dp[2 * PAD : 5 * PAD, at]
        for i, out in enumerate((out0, out1, out2, out3)):
            rows = slice(i * 288, (i + 1) * 288)
            out[:, at] = (
                jnp.dot(fto[rows], own, preferred_element_type=F32)
                + jnp.dot(fta[rows], rest, preferred_element_type=F32)
            ).astype(BF16)


def arrived_part(place, sharp, shift, coef, *operands):
    smem = pl.BlockSpec(memory_space=pltpu.SMEM)
    vmem = pl.BlockSpec(memory_space=pltpu.VMEM)
    return pl.pallas_call(
        arrived_kernel,
        out_shape=[jax.ShapeDtypeStruct((D // 4, D), BF16)] * 4,
        in_specs=[smem] * 4 + [pl.BlockSpec(memory_space=pl.ANY)] * 15,
        out_specs=[vmem] * 4,
        scratch_shapes=[
            pltpu.VMEM((3 * PAD, D), BF16),
            pltpu.VMEM((2 * PAD, D), BF16),
            pltpu.VMEM((2, D, D), BF16),
            pltpu.VMEM((D, D), BF16),
            pltpu.VMEM((2 * R, D), BF16),
            pltpu.VMEM((8 * PAD, D), BF16),
            pltpu.VMEM((2 * R, D), F32),
            pltpu.VMEM((3 * PAD, D), F32),
            pltpu.VMEM((2 * PAD, D), F32),
            pltpu.VMEM((2 * R, 128), F32),
            pltpu.VMEM((3 * PAD, 128), F32),
            pltpu.VMEM((2 * PAD, 128), F32),
            pltpu.VMEM((D, 2 * PAD), BF16),
            pltpu.VMEM((D, 3 * PAD), BF16),
            pltpu.VMEM((2 * R, D), F32),
            pltpu.VMEM((3 * PAD, D), F32),
            pltpu.VMEM((3 * PAD, 4 * PAD), BF16),
            pltpu.VMEM((5 * PAD, D), BF16),
            pltpu.SemaphoreType.DMA((14,)),
        ],
        compiler_params=pltpu.CompilerParams(vmem_limit_bytes=60 * 2**20),
        cost_estimate=pl.CostEstimate(flops=14 * 10**9, bytes_accessed=20 * 10**6, transcendentals=800000),
    )(place, sharp, shift, coef, *operands)


def join_kernel(place_ref, one, two, three, four, image_out, caption_out, held):
    for k, piece in enumerate((one, two, three, four)):
        held[k] = piece[...]
    for place in range(NX):
        back = (place_ref[2] - place) & 3
        for head, out in enumerate((image_out, caption_out)):
            for row in range(9):
                at = place * 9 + row
                for n in range(9):
                    out[at : at + 1, n * 128 : (n + 1) * 128] = held[back, head, row * 9 + n : row * 9 + n + 1]


def join_rows(place, *pieces):
    vmem = pl.BlockSpec(memory_space=pltpu.VMEM)
    return pl.pallas_call(
        join_kernel,
        out_shape=[jax.ShapeDtypeStruct((36, D), F32)] * 2,
        in_specs=[pl.BlockSpec(memory_space=pltpu.SMEM)] + [vmem] * 4,
        out_specs=[vmem] * 2,
        scratch_shapes=[pltpu.VMEM((4, 2, 81, 128), F32)],
    )(place, *pieces)


def local(
    picture_encoder_features,
    text_encoder_features,
    picture_projector,
    text_projector,
    matching_target,
    sharpness_param,
    offset_shift,
    objective_multiplier,
):
    place = lax.axis_index("dp")
    core, y_lo = place % 2, (place // 2) % 2
    x, y_hi = lax.axis_index("replica") // 2, lax.axis_index("replica") % 2
    y = y_hi * 2 + y_lo
    role = jnp.stack([core, y_lo, x, y]).astype(jnp.int32)
    coefficient = objective_multiplier / (lax.axis_size("dp") * R)

    own_img = swap_cores(picture_encoder_features)
    own_cap = swap_cores(text_encoder_features)
    target_other = swap_cores(matching_target)
    cap, img, target_other = lax.optimization_barrier(
        (text_encoder_features, picture_encoder_features, target_other)
    )
    cap_sib = swap_chips(cap)
    img_far = image_to_neighbour(img)
    img_extra = image_down(img)

    blocks = (picture_encoder_features, own_img, text_encoder_features, own_cap)
    *kept, from_own = own_part(
        role, sharpness_param, offset_shift, coefficient, matching_target[None], target_other[None],
        *blocks, picture_projector, text_projector,
    )
    cap_sib, img_far, img_extra, kept, from_own, blocks = lax.optimization_barrier(
        (cap_sib, img_far, img_extra, kept, from_own, blocks)
    )
    cap_sib_other = swap_cores(cap_sib)
    img_far_other = swap_cores(img_far)
    img_extra_other = swap_cores(img_extra)
    order, turned = turn_own(role, *blocks)
    parts = arrived_part(
        role, sharpness_param, offset_shift, coefficient,
        cap_sib, cap_sib_other, img_far, img_far_other, img_extra, img_extra_other,
        picture_projector, text_projector, order, *kept, turned, from_own,
    )

    one = [parts[0]] + [first_axis(parts[by], by) for by in (1, 3, 2)]
    one = sum(v.astype(F32) for v in one).astype(BF16)
    pieces = [one[by * 72 : (by + 1) * 72] for by in range(4)]
    two = [pieces[0]] + [second_axis(pieces[by], by) for by in (1, 3, 2)]
    two = sum(v.astype(F32) for v in two).astype(BF16).reshape(NZ, 81, 128)
    three = lax.all_to_all(two, AXES, 0, 0, axis_index_groups=ALONG_Z)
    mine = jnp.sum(three.astype(F32), axis=0)

    first = core == 0
    ring, cross = pass_on(mine), pass_across(mine)
    home = core == y_hi
    image_piece = jnp.where(home & first, mine, jnp.where(home | first, ring, cross))
    caption_piece = jnp.where(home & first, ring, jnp.where(home, mine, jnp.where(first, cross, ring)))
    both = jnp.stack([image_piece, caption_piece])
    return join_rows(role, both, *[along_x(both, by) for by in (1, 2, 3)])


def solution(mesh):
    placed = (
        P(("dp", "replica"), None),
        P(("dp", "replica"), None),
        P(),
        P(),
        P(("dp", "replica")),
        P(),
        P(),
        P(),
    )
    return jax.shard_map(
        local, mesh=mesh, in_specs=placed, out_specs=(P("dp", None), P("dp", None)), check_vma=False
    )
```
